32 devices in a mesh: dp: 16 (over z, y, x), mp: 2 (over core).
Axes of the slice: x: 2, y: 2, z: 4, core: 2. Of those that a mesh axis runs over, the one named last changes fastest.
Arguments:
- inputs: bfloat16 [21888, 512], P('dp'), may hold values from -6 to 6
- region_counts: int32 [96], P('dp'), may hold values from 10 to 100, as said below
- w_query: bfloat16 [512, 512], P(None, 'mp'), may hold values from -0.25 to 0.25
- b_query: float32 [512], P('mp'), may hold values from -3 to 3
- w_key: bfloat16 [512, 512], P(None, 'mp'), may hold values from -0.25 to 0.25
- w_value: bfloat16 [512, 512], P(None, 'mp'), may hold values from -0.25 to 0.25
- b_value: float32 [512], P('mp'), may hold values from -3 to 3
- w_out: bfloat16 [512, 512], P('mp'), may hold values from -3 to 3
- b_out: float32 [512], replicated, may hold values from -3 to 3
- gain_one: float32 [512], replicated, may hold values from 0.5 to 1.5
- shift_one: float32 [512], replicated, may hold values from -3 to 3
- w_up: bfloat16 [512, 2048], P(None, 'mp'), may hold values from -0.25 to 0.25
- b_up: float32 [2048], P('mp'), may hold values from -3 to 3
- w_down: bfloat16 [2048, 512], P('mp'), may hold values from -0.125 to 0.125
- b_down: float32 [512], replicated, may hold values from -3 to 3
- gain_two: float32 [512], replicated, may hold values from 0.5 to 1.5
- shift_two: float32 [512], replicated, may hold values from -3 to 3
- cotangent: float32 [21888, 512], P('dp'), may hold values from -6 to 6
Outputs:
- output: bfloat16 [21888, 512], P(('dp', 'mp'))
- input_grad: float32 [21888, 512], P(('dp', 'mp'))
- grad_w_query: float32 [512, 512], P('dp', 'mp')
- grad_b_query: float32 [512], P('mp')
- grad_w_key: float32 [512, 512], P('dp', 'mp')
- grad_w_value: float32 [512, 512], P('dp', 'mp')
- grad_b_value: float32 [512], P('mp')
- grad_w_out: float32 [512, 512], P('mp', 'dp')
- grad_b_out: float32 [512], replicated
- grad_gain_one: float32 [512], replicated
- grad_shift_one: float32 [512], replicated
- grad_w_up: float32 [512, 2048], P('dp', 'mp')
- grad_b_up: float32 [2048], P('mp')
- grad_w_down: float32 [2048, 512], P('mp', 'dp')
- grad_b_down: float32 [512], replicated
- grad_gain_two: float32 [512], replicated
- grad_shift_two: float32 [512], replicated
The draws below stay inside these ranges and needn't reach their ends.
Inputs may be any that keep to these rules, and one draw needn't show every extreme that they name: `region_counts`: valid region slots of each item; some item has all 100 slots valid and some item has the fewest.
All inputs are finite; a program needn't handle non-finite values.
Results may differ from the reference program's by a relative error of at most 0.02.
Values may be sent and summed in bfloat16 or wider, within the bound.
A program may use at most 128 MiB of HBM per device.

```python
import jax
import jax.numpy as jnp
from jax import lax

D = 512
HEAD_DIM = 64
FF = 2048
TEXT = 128
REGIONS = 100
ITEMS = 96
TOKENS = 21888


def draw_region_counts(key, part):
    key = jax.random.fold_in(key, 7)
    first_key, second_key, third_key = jax.random.split(key, 3)
    smallest = max(REGIONS // 10, 1)
    counted = jax.random.randint(first_key, (ITEMS,), smallest, REGIONS + 1)
    fullest = jax.random.randint(second_key, (), 0, ITEMS)
    emptiest = (fullest + 1 + jax.random.randint(third_key, (), 0, ITEMS - 1)) % ITEMS
    counted = counted.at[fullest].set(REGIONS)
    return counted.at[emptiest].set(smallest).astype(jnp.int32)


def steps_of(own_key, extent, cuts, low, top_value):
    gain = 1.0
    for dim, parts in cuts:
        draws = jax.random.uniform(jax.random.fold_in(jax.random.fold_in(own_key, 6), dim), (parts,), jnp.float32, low / len(cuts), top_value / len(cuts))
        gain = gain * jnp.repeat(jnp.exp(draws), extent[dim] // parts).reshape((-1,) + (1,) * (len(extent) - 1 - dim))
    return gain


def scatter_about(rng, dims, width, reach, shards=(), held_as=jnp.bfloat16):
    drawn = jax.random.normal(rng, dims, jnp.float32) * width
    if len(shards) > 0:
        drawn = steps_of(rng, dims, shards, -0.22, 0.18) * drawn
    return jnp.clip(drawn, min=-reach, max=reach).astype(held_as)


def setup_inputs(seed: int = 0) -> dict:
    key_list = jax.random.split(jax.random.key(seed), 19)
    inputs = scatter_about(key_list[0], (TOKENS, D), 1.0, 6.0, ((0, 16),))
    region_counts = draw_region_counts(jax.random.fold_in(key_list[18], 71), 0)
    w_query = scatter_about(key_list[2], (D, D), D ** -0.5, 0.25, ((1, 2),))
    b_query = scatter_about(key_list[3], (D,), 0.5, 3.0, ((0, 2),), jnp.float32)
    w_key = scatter_about(key_list[4], (D, D), D ** -0.5, 0.25, ((1, 2),))
    w_value = scatter_about(key_list[5], (D, D), D ** -0.5, 0.25, ((1, 2),))
    b_value = scatter_about(key_list[6], (D,), 0.5, 3.0, ((0, 2),), jnp.float32)
    w_out = scatter_about(key_list[7], (D, D), (max(D // 128, 1)) ** -0.5, 3.0, ((0, 2),))
    b_out = scatter_about(key_list[8], (D,), 0.5, 3.0, (), jnp.float32)
    gain_one = jnp.clip(1.0 + 0.1 * jax.random.normal(key_list[9], (D,), jnp.float32), 0.5, 1.5)
    shift_one = scatter_about(key_list[10], (D,), 0.5, 3.0, (), jnp.float32)
    w_up = scatter_about(key_list[11], (D, FF), D ** -0.5, 0.25, ((1, 2),))
    b_up = scatter_about(key_list[12], (FF,), 0.5, 3.0, ((0, 2),), jnp.float32)
    w_down = scatter_about(key_list[13], (FF, D), FF ** -0.5, 0.125, ((0, 2),))
    b_down = scatter_about(key_list[14], (D,), 0.5, 3.0, (), jnp.float32)
    gain_two = jnp.clip(1.0 + 0.1 * jax.random.normal(key_list[15], (D,), jnp.float32), 0.5, 1.5)
    shift_two = scatter_about(key_list[16], (D,), 0.5, 3.0, (), jnp.float32)
    cotangent = scatter_about(key_list[17], (TOKENS, D), 1.0, 6.0, ((0, 16),), jnp.float32)
    return dict(inputs=inputs, region_counts=region_counts, w_query=w_query, b_query=b_query, w_key=w_key, w_value=w_value, b_value=b_value, w_out=w_out, b_out=b_out, gain_one=gain_one, shift_one=shift_one, w_up=w_up, b_up=b_up, w_down=w_down, b_down=b_down, gain_two=gain_two, shift_two=shift_two, cotangent=cotangent)


@jax.custom_vjp
def low(v):
    return lax.optimization_barrier(v.astype(jnp.bfloat16)).astype(jnp.float32)

@jax.custom_vjp
def low_back(v):
    return v

def low_keep(v):
    return (low(v), None)

def low_pass(kept, grad):
    return (grad,)

def back_keep(v):
    return (v, None)

def back_low(kept, grad):
    return (low(grad),)
low.defvjp(low_keep, low_pass)
low_back.defvjp(back_keep, back_low)
precise = lax.Precision.HIGHEST

def product(first_op, second_op):
    return jnp.dot(first_op, second_op, precision=precise, preferred_element_type=jnp.float32)

def layer_norm(values, gain_vec, shift_vec):
    row_mean = lax.optimization_barrier(jnp.mean(values, axis=-1, keepdims=True))
    centred = values - row_mean
    inverse = lax.rsqrt(lax.optimization_barrier(jnp.mean(centred * centred, axis=-1, keepdims=True)) + 1e-12)
    return centred * inverse * gain_vec + shift_vec

def forward(inputs, region_counts, w_query, b_query, w_key, w_value, b_value, w_out, b_out, gain_one, shift_one, w_up, b_up, w_down, b_down, gain_two, shift_two):
    item_count = region_counts.shape[0]
    length = TEXT + REGIONS
    heads_all = w_query.shape[1] // HEAD_DIM
    score_scale = HEAD_DIM ** (-0.5)

    def split_heads(flat_rows):
        return flat_rows.reshape(item_count, length, heads_all, HEAD_DIM)
    queries = split_heads(low(low_back(product(inputs, w_query) + b_query)))
    key_rows = split_heads(low(low_back(product(inputs, w_key))))
    value_rows = split_heads(low(low_back(product(inputs, w_value) + b_value)))
    raw_scores = jnp.einsum('ishd,ithd->ihst', queries, key_rows, precision=precise) * score_scale
    position = jnp.arange(length)
    visible = (position[None, :] < TEXT) | (position[None, :] - TEXT < region_counts[:, None])
    scores = jnp.where(visible[:, None, None, :], low_back(raw_scores), -1000000000.0)
    probs = jax.nn.softmax(scores, axis=-1)
    context = jnp.einsum('ihst,ithd->ishd', low(probs), value_rows, precision=precise)
    context = low(low_back(context.reshape(item_count * length, heads_all * HEAD_DIM)))
    attended = low_back(product(context, w_out))
    hidden_one = layer_norm(attended + b_out + inputs, gain_one, shift_one)
    upper_part = low_back(product(low(hidden_one), w_up) + b_up)
    active = low(jax.nn.gelu(upper_part, approximate=False))
    lowered = low_back(product(active, w_down))
    return layer_norm(lowered + b_down + hidden_one, gain_two, shift_two)

def reference(inputs, region_counts, w_query, b_query, w_key, w_value, b_value, w_out, b_out, gain_one, shift_one, w_up, b_up, w_down, b_down, gain_two, shift_two, cotangent):
    parameters = tuple((weight.astype(jnp.float32) for weight in (w_query, b_query, w_key, w_value, b_value, w_out, b_out, gain_one, shift_one, w_up, b_up, w_down, b_down, gain_two, shift_two)))
    group_items = 16
    group_count = ITEMS // group_items
    group_rows = group_items * (TEXT + REGIONS)
    input_groups = inputs.astype(jnp.float32).reshape(group_count, group_rows, D)
    count_groups = region_counts.reshape(group_count, group_items)
    cotangent_groups = cotangent.astype(jnp.float32).reshape(group_count, group_rows, D)

    def step(totals, pieces):
        block_rows, block_counts, block_cotangent = pieces

        def apply(block_input, *weights):
            return forward(block_input, block_counts, *weights)
        result, pullback = jax.vjp(apply, block_rows, *parameters)
        gradients = pullback(block_cotangent)
        totals = jax.tree.map(jnp.add, totals, tuple(gradients[1:]))
        return (totals, (result.astype(jnp.bfloat16), gradients[0]))
    zeros = tuple((jnp.zeros_like(weight) for weight in parameters))
    totals, (outputs, input_grads) = lax.scan(step, zeros, (input_groups, count_groups, cotangent_groups))
    return (outputs.reshape(ITEMS * (TEXT + REGIONS), D), input_grads.reshape(ITEMS * (TEXT + REGIONS), D), totals[0], totals[1], totals[2], totals[3], totals[4], totals[5], totals[6], totals[7], totals[8], totals[9], totals[10], totals[11], totals[12], totals[13], totals[14])
```

```python
import functools
import types

import jax
import jax.numpy as jnp
from jax import lax
from jax.experimental import pallas as pl
from jax.experimental.pallas import tpu as pltpu
from jax.sharding import PartitionSpec as P

HEAD_DIM = 64
TEXT = 128


def layer_stats(pre_rows):
    row_mean = jnp.mean(pre_rows, axis=-1, keepdims=True)
    centred = pre_rows - row_mean
    inverse = lax.rsqrt(jnp.mean(centred * centred, axis=-1, keepdims=True) + 1e-12)
    return (centred * inverse, inverse)


def norm_back(grad_rows, normed, inverse, gain_vec):
    scaled = grad_rows * gain_vec
    return inverse * (
        scaled
        - jnp.mean(scaled, axis=-1, keepdims=True)
        - normed * jnp.mean(scaled * normed, axis=-1, keepdims=True)
    )


def gelu_slope(upper_part):
    return (
        0.5 * (1.0 + lax.erf(upper_part * 0.7071067811865476))
        + upper_part * jnp.exp(-0.5 * upper_part * upper_part) * 0.3989422804014327
    )


def contract_rows(first_op, second_op):
    return lax.dot_general(
        first_op, second_op, (((0,), (0,)), ((), ())), preferred_element_type=jnp.float32
    )


def times_transposed(first_op, second_op):
    return lax.dot_general(
        first_op, second_op, (((1,), (1,)), ((), ())), preferred_element_type=jnp.float32
    )


def per_device(
    inputs,
    region_counts,
    w_query,
    b_query,
    w_key,
    w_value,
    b_value,
    w_out,
    b_out,
    gain_one,
    shift_one,
    w_up,
    b_up,
    w_down,
    b_down,
    gain_two,
    shift_two,
    cotangent,
):
    total_rows = inputs.shape[0]
    item_count = region_counts.shape[0]
    length = total_rows // item_count
    heads_here = w_query.shape[1] // HEAD_DIM
    score_scale = HEAD_DIM ** (-0.5)
    share_rows = total_rows // lax.axis_size("mp")
    row_start = lax.axis_index("mp") * share_rows

    def own_rows(full_rows):
        return lax.dynamic_slice_in_dim(full_rows, row_start, share_rows, 0)

    def split_heads(flat_rows):
        return flat_rows.reshape(item_count, length, heads_here, HEAD_DIM)

    position = jnp.arange(length)
    visible = (position[None, :] < TEXT) | (position[None, :] - TEXT < region_counts[:, None])
    key_mask = visible[:, None, None, :]
    queries = (jnp.dot(inputs, w_query, preferred_element_type=jnp.float32) + b_query).astype(
        jnp.bfloat16
    )
    key_rows = jnp.dot(inputs, w_key, preferred_element_type=jnp.float32).astype(jnp.bfloat16)
    value_rows = (jnp.dot(inputs, w_value, preferred_element_type=jnp.float32) + b_value).astype(
        jnp.bfloat16
    )
    query_heads = split_heads(queries)
    key_heads = split_heads(key_rows)
    value_heads = split_heads(value_rows)

    def masked_scores():
        raw_scores = (
            jnp.einsum(
                "ishd,ithd->ihst", query_heads, key_heads, preferred_element_type=jnp.float32
            )
            * score_scale
        )
        return jnp.where(key_mask, raw_scores, -1000000000.0)

    scores = masked_scores()
    row_top = jnp.max(scores, axis=-1, keepdims=True)
    exponent = jnp.exp(scores - row_top)
    row_total = jnp.sum(exponent, axis=-1, keepdims=True)
    probs = exponent / row_total
    log_total = row_top + jnp.log(row_total)
    context = jnp.einsum(
        "ihst,ithd->ishd",
        probs.astype(jnp.bfloat16),
        value_heads,
        preferred_element_type=jnp.float32,
    )
    context = context.reshape(total_rows, heads_here * HEAD_DIM).astype(jnp.bfloat16)
    partial_attn = jnp.dot(context, w_out, preferred_element_type=jnp.float32)
    attended = lax.psum(partial_attn, "mp")
    normed_one, inverse_one = layer_stats(attended + b_out + inputs.astype(jnp.float32))
    hidden_one = normed_one * gain_one + shift_one
    hidden_low = hidden_one.astype(jnp.bfloat16)
    upper_part = jnp.dot(hidden_low, w_up, preferred_element_type=jnp.float32) + b_up
    active = jax.nn.gelu(upper_part, approximate=False).astype(jnp.bfloat16)
    partial_ffn = jnp.dot(active, w_down, preferred_element_type=jnp.float32)
    lowered = lax.psum(partial_ffn, "mp")
    normed_two, inverse_two = layer_stats(lowered + b_down + hidden_one)
    output = own_rows(normed_two * gain_two + shift_two).astype(jnp.bfloat16)
    grad_pre_two = norm_back(cotangent, normed_two, inverse_two, gain_two)
    down_low = grad_pre_two.astype(jnp.bfloat16)
    grad_output = own_rows(cotangent)
    normed_two_own = own_rows(normed_two)
    grad_two_own = own_rows(grad_pre_two)
    grad_gain_two = jnp.sum(grad_output * normed_two_own, axis=0)
    grad_shift_two = jnp.sum(grad_output, axis=0)
    grad_b_down = jnp.sum(grad_two_own, axis=0)
    grad_w_down = contract_rows(active, down_low)
    active_grad = times_transposed(down_low, w_down)
    upper_grad = (active_grad * gelu_slope(upper_part)).astype(jnp.bfloat16)
    grad_b_up = jnp.sum(upper_grad.astype(jnp.float32), axis=0)
    grad_w_up = contract_rows(hidden_low, upper_grad)
    partial_hidden = times_transposed(upper_grad, w_up)
    hidden_grad = lax.psum(partial_hidden, "mp") + grad_pre_two
    grad_pre_one = norm_back(hidden_grad, normed_one, inverse_one, gain_one)
    out_low = grad_pre_one.astype(jnp.bfloat16)
    hidden_grad_own = own_rows(hidden_grad)
    normed_one_own = own_rows(normed_one)
    grad_one_own = own_rows(grad_pre_one)
    grad_gain_one = jnp.sum(hidden_grad_own * normed_one_own, axis=0)
    grad_shift_one = jnp.sum(hidden_grad_own, axis=0)
    grad_b_out = jnp.sum(grad_one_own, axis=0)
    grad_w_out = contract_rows(context, out_low)
    context_grad = split_heads(times_transposed(out_low, w_out).astype(jnp.bfloat16))
    probs_again = jnp.exp(masked_scores() - log_total)
    prob_grad = jnp.einsum(
        "ishd,ithd->ihst", context_grad, value_heads, preferred_element_type=jnp.float32
    )
    row_inner = jnp.sum(probs_again * prob_grad, axis=-1, keepdims=True)
    score_grad = (probs_again * (prob_grad - row_inner)).astype(jnp.bfloat16)
    query_grad = (
        (
            jnp.einsum("ihst,ithd->ishd", score_grad, key_heads, preferred_element_type=jnp.float32)
            * score_scale
        )
        .astype(jnp.bfloat16)
        .reshape(total_rows, heads_here * HEAD_DIM)
    )
    key_grad = (
        (
            jnp.einsum(
                "ihst,ishd->ithd", score_grad, query_heads, preferred_element_type=jnp.float32
            )
            * score_scale
        )
        .astype(jnp.bfloat16)
        .reshape(total_rows, heads_here * HEAD_DIM)
    )
    value_grad = jnp.einsum(
        "ihst,ishd->ithd",
        probs_again.astype(jnp.bfloat16),
        context_grad,
        preferred_element_type=jnp.float32,
    ).astype(jnp.bfloat16)
    value_grad = value_grad.reshape(total_rows, heads_here * HEAD_DIM)
    grad_b_query = jnp.sum(query_grad.astype(jnp.float32), axis=0)
    grad_b_value = jnp.sum(value_grad.astype(jnp.float32), axis=0)
    grad_w_query = contract_rows(inputs, query_grad)
    grad_w_key = contract_rows(inputs, key_grad)
    grad_w_value = contract_rows(inputs, value_grad)
    partial_input = (
        times_transposed(query_grad, w_query)
        + times_transposed(key_grad, w_key)
        + times_transposed(value_grad, w_value)
    )
    input_grad = own_rows(
        lax.psum(partial_input.astype(jnp.bfloat16), "mp").astype(jnp.float32) + grad_pre_one
    )
    bias_sums = lax.psum((grad_b_query, grad_b_value, grad_b_up), "dp")
    norm_sums = lax.psum(
        (grad_b_out, grad_gain_one, grad_shift_one, grad_b_down, grad_gain_two, grad_shift_two),
        ("dp", "mp"),
    )
    weight_sums = (
        lax.psum_scatter(
            grad_w_query.astype(jnp.bfloat16), "dp", scatter_dimension=0, tiled=True
        ).astype(jnp.float32),
        lax.psum_scatter(
            grad_w_key.astype(jnp.bfloat16), "dp", scatter_dimension=0, tiled=True
        ).astype(jnp.float32),
        lax.psum_scatter(
            grad_w_value.astype(jnp.bfloat16), "dp", scatter_dimension=0, tiled=True
        ).astype(jnp.float32),
        lax.psum_scatter(
            grad_w_out.astype(jnp.bfloat16), "dp", scatter_dimension=1, tiled=True
        ).astype(jnp.float32),
        lax.psum_scatter(
            grad_w_up.astype(jnp.bfloat16), "dp", scatter_dimension=0, tiled=True
        ).astype(jnp.float32),
        lax.psum_scatter(
            grad_w_down.astype(jnp.bfloat16), "dp", scatter_dimension=1, tiled=True
        ).astype(jnp.float32),
    )
    return (
        output,
        input_grad,
        weight_sums[0],
        bias_sums[0],
        weight_sums[1],
        weight_sums[2],
        bias_sums[1],
        weight_sums[3],
        norm_sums[0],
        norm_sums[1],
        norm_sums[2],
        weight_sums[4],
        bias_sums[2],
        weight_sums[5],
        norm_sums[3],
        norm_sums[4],
        norm_sums[5],
    )


ITEM_PAD = 16
MESH = pl.DeviceIdType.MESH
BF = jnp.bfloat16
F32 = jnp.float32
BLOCK = 256
UNITS = 12
X_FIRST, Y_FIRST, LOW_FIRST, HIGH_FIRST = 0, 1, 2, 3
ORDER = (0, 1, 2, 3, 0, 1, 2, 3, 0, 1, 2, 3)


def dot_nn(a, b):
    return lax.dot_general(a, b, (((1,), (0,)), ((), ())), preferred_element_type=F32)


def dot_nt(a, b):
    return lax.dot_general(a, b, (((1,), (1,)), ((), ())), preferred_element_type=F32)


def layer_kernel(dims, names, *refs):
    r = types.SimpleNamespace(**dict(zip(names, refs, strict=True)))
    items, length, rows_pad, lanes, nz, shard = dims
    total = items * rows_pad
    chunks = r.wu_h.shape[1] // BLOCK
    width = r.x_h.shape[1]
    dp, mp = lax.axis_index("dp"), lax.axis_index("mp")
    z, y, x = dp // 4, (dp // 2) % 2, dp % 2

    def at(z_, y_, x_):
        return z_ * 4 + y_ * 2 + x_

    core = (dp, 1 - mp)
    x_side = (at(z, y, 1 - x), mp)
    y_side = (at(z, 1 - y, x), mp)
    z_side = [(at((z + step) % nz, y, x), mp) for step in range(1, nz)]
    low_side = (at(z + 1 - 2 * (z % 2), y, x), mp)
    high_side = (at(nz - 1 - z, y, x), mp)
    plane_side = [(at(z, (y + step // 2) % 2, (x + step) % 2), mp) for step in range(1, 4)]

    local = []

    def bring(src, dst):
        copy = pltpu.make_async_copy(src, dst, r.in_sem.at[len(local)])
        copy.start()
        local.append(copy)
        return copy

    c_x = bring(r.x_h, r.x_raw)
    c_w = [bring(src, r.wqkv.at[0, k]) for k, src in enumerate((r.wq_h, r.wk_h, r.wv_h))]
    c_p = [bring(r.b_query_h, r.bias_q.at[0]), bring(r.b_value_h, r.bias_v.at[0]), bring(r.b_up_h, r.bias_u.at[0])]
    vectors = (
        (r.b_out_h, r.b_out), (r.gain_one_h, r.gain_one), (r.shift_one_h, r.shift_one),
        (r.b_down_h, r.b_down), (r.gain_two_h, r.gain_two), (r.shift_two_h, r.shift_two))
    c_vec = [bring(src, dst) for src, dst in vectors]
    c_wo = bring(r.wo_h, r.wo.at[0])
    c_wu = [bring(r.wu_h.at[:, pl.ds(c * BLOCK, BLOCK)], r.wu.at[c]) for c in range(chunks)]
    c_wd = bring(r.wd_h, r.wd.at[pl.ds(0, chunks)])
    full_rows = r.cot_h.shape[0]
    c_cot = bring(r.cot_h, r.cot_raw.at[pl.ds(0, full_rows)])

    barrier = pltpu.get_barrier_semaphore()
    near = [core] + plane_side + z_side
    for device in near:
        pl.semaphore_signal(barrier, inc=1, device_id=device, device_id_type=MESH)
    pl.semaphore_wait(barrier, len(near))

    remote = []

    def send_weight(src, dst):
        k = len(remote)
        copy = pltpu.make_async_remote_copy(
            src_ref=src, dst_ref=dst, send_sem=r.w_send.at[k], recv_sem=r.w_recv.at[k],
            device_id=core, device_id_type=MESH)
        copy.start()
        remote.append(copy)
        return copy

    s_w = [send_weight(src, r.wqkv.at[1, k]) for k, src in enumerate((r.wq_h, r.wk_h, r.wv_h))]
    s_w += [send_weight(src, dst.at[1]) for src, dst in (
        (r.b_query_h, r.bias_q), (r.b_value_h, r.bias_v), (r.b_up_h, r.bias_u))]
    s_wo = send_weight(r.wo_h, r.wo.at[1])
    s_wu = [send_weight(r.wu_h.at[:, pl.ds(c * BLOCK, BLOCK)], r.wu.at[chunks + c]) for c in range(chunks)]
    s_wd = send_weight(r.wd_h, r.wd.at[pl.ds(chunks, chunks)])

    pad_rows = lanes - rows_pad

    def transposed(block):
        full = jnp.concatenate([block, jnp.zeros((pad_rows, block.shape[1]), F32)], axis=0)
        return full.T.astype(BF)

    def rows_of(i):
        return pl.ds(pl.multiple_of(i * rows_pad, 16), rows_pad)

    def lanes_of(i):
        return pl.ds(pl.multiple_of(i * lanes, lanes), lanes)

    def clear(n, carry):
        r.probs[n, pl.ds(rows_pad, pad_rows), :] = jnp.zeros((pad_rows, lanes), BF)
        return carry

    lax.fori_loop(0, r.probs.shape[0], clear, 0)
    zero_block = jnp.zeros((pad_rows, BLOCK), BF)
    for i in range(items):
        r.upg[i, pl.ds(rows_pad, pad_rows), :] = zero_block
        r.olow[i, pl.ds(rows_pad, pad_rows), :] = jnp.zeros((pad_rows, r.olow.shape[2]), BF)
        for j in range(2 * chunks):
            r.active[j, i, pl.ds(rows_pad, pad_rows), :] = zero_block
    for k in range(2):
        r.dscore[k, pl.ds(rows_pad, pad_rows), :] = jnp.zeros((pad_rows, lanes), BF)
    one_row = jnp.where(lax.broadcasted_iota(jnp.int32, (16, items * lanes), 0) == 0, 1.0, 0.0).astype(BF)
    r.xT[pl.ds(width, 16), :] = one_row
    r.hT[pl.ds(width, 16), :] = one_row

    cot_rows = r.cot_raw.shape[0]
    r.cot_raw[pl.ds(full_rows, cot_rows - full_rows), :] = jnp.zeros((cot_rows - full_rows, width), F32)

    c_x.wait()
    down_ = lax.broadcasted_iota(jnp.int32, (rows_pad, 256), 0)
    across = lax.broadcasted_iota(jnp.int32, (rows_pad, 256), 1)
    for i in range(items):
        block = None
        for m in range(2):
            start = (m * items + i) * length
            window = start // 16 * 16
            count = min(256, full_rows - window)
            shift = jnp.where(mp == m, start - window, 2 * 256)
            pick = jnp.where((across == down_ + shift) & (down_ < length), 1.0, 0.0).astype(BF)
            term = dot_nn(pick[:, :count], r.x_raw[pl.ds(window, count), :])
            block = term if block is None else block + term
        r.x_v[rows_of(i), :] = block.astype(BF)
        r.xT[pl.ds(0, width), lanes_of(i)] = transposed(block)

    def project(slot):
        def one(k, carry):
            shift = jnp.where(k == 0, r.bias_q[slot], jnp.where(k == 2, r.bias_v[slot], 0.0))
            acc = dot_nn(r.x_v[...], r.wqkv[slot, k]) + shift
            for i in range(items):
                block = acc[i * rows_pad:(i + 1) * rows_pad]
                r.nat[slot * items + i, k] = block.astype(BF)
                low = block.astype(BF).astype(F32)
                r.tra[slot * items + i, k] = transposed(low * jnp.where(k == 2, 1.0, 0.125))
            return carry

        lax.fori_loop(0, 3, one, 0)

    for c in c_w + c_p:
        c.wait()
    project(0)
    for s in s_w:
        s.wait_recv()
    project(1)

    lane = lax.broadcasted_iota(jnp.int32, (1, 128), 1)
    half = [jnp.where(lane < 64, 1.0, 0.0).astype(BF), jnp.where(lane >= 64, 1.0, 0.0).astype(BF)]

    position = lax.broadcasted_iota(jnp.int32, (rows_pad, lanes), 0)

    def attend(n, carry):
        i = lax.rem(n, items)
        mask = jnp.where(position < TEXT + r.counts[mp * items + i], 0.0, -1e9)
        parts = []
        for h in range(4):
            pair = slice((h // 2) * 128, (h // 2) * 128 + 128)
            keys = r.nat[n, 1, :, pair] * half[h % 2]
            score = dot_nn(keys, r.tra[n, 0, pair, :]) + mask
            top = jnp.max(score, axis=0, keepdims=True)
            e = jnp.exp(score - top)
            p = e * (1.0 / jnp.sum(e, axis=0, keepdims=True))
            r.probs[n * 4 + h, pl.ds(0, rows_pad), :] = p.astype(BF)
            parts.append(dot_nn(r.tra[n, 2, h * 64:(h + 1) * 64, :], r.probs[n * 4 + h]))
        context = jnp.concatenate(parts, axis=0)
        slot = n // items
        r.ctxT[slot, :, lanes_of(i)] = context.astype(BF)
        r.ctx[slot, rows_of(i), :] = context.T[:rows_pad].astype(BF)
        return carry

    lax.fori_loop(0, 2 * items, attend, 0)

    c_wo.wait()
    s_wo.wait_recv()
    for c in c_vec:
        c.wait()

    def first_norm(i, carry):
        att = dot_nn(r.ctx[0, rows_of(i), :], r.wo[0]) + dot_nn(r.ctx[1, rows_of(i), :], r.wo[1])
        pre = att + r.b_out[...] + r.x_v[rows_of(i), :].astype(F32)
        centred = pre - jnp.mean(pre, axis=1, keepdims=True)
        inverse = lax.rsqrt(jnp.mean(centred * centred, axis=1, keepdims=True) + 1e-12)
        normed = centred * inverse
        r.n1[rows_of(i), :] = normed
        r.inv1[rows_of(i), :] = jnp.broadcast_to(inverse, (rows_pad, 128))
        hidden = normed * r.gain_one[...] + r.shift_one[...]
        r.hlow[rows_of(i), :] = hidden.astype(BF)
        r.hT[pl.ds(0, width), lanes_of(i)] = transposed(hidden)
        return carry

    lax.fori_loop(0, items, first_norm, 0)

    for c in c_wu + [c_wd]:
        c.wait()
    for s in s_wu + [s_wd]:
        s.wait_recv()
    r.acc[...] = jnp.zeros(r.acc.shape, F32)

    def feed(j, carry):
        slot, c = j // chunks, lax.rem(j, chunks)
        up_bias = r.bias_u[slot, :, pl.ds(pl.multiple_of(c * BLOCK, BLOCK), BLOCK)]
        for i in range(items):
            u = dot_nn(r.hlow[rows_of(i), :], r.wu[j]) + up_bias
            phi = 0.5 + 0.5 * lax.erf(u * 0.7071067811865476)
            r.slope[j, rows_of(i), :] = (phi + u * (jnp.exp(-0.5 * u * u) * 0.3989422804014327)).astype(BF)
            act = (u * phi).astype(BF)
            r.active[j, i, pl.ds(0, rows_pad), :] = act
            r.acc[rows_of(i), :] += dot_nn(act, r.wd[j])
        return carry

    lax.fori_loop(0, 2 * chunks, feed, 0)

    c_cot.wait()
    sums = [None, None, None]

    valid = lax.broadcasted_iota(jnp.int32, (rows_pad, 1), 0) < length

    def second_norm(i, carry):
        gain2, shift2, bdown = carry
        hidden = r.n1[rows_of(i), :] * r.gain_one[...] + r.shift_one[...]
        pre = r.acc[rows_of(i), :] + r.b_down[...] + hidden
        centred = pre - jnp.mean(pre, axis=1, keepdims=True)
        inverse = lax.rsqrt(jnp.mean(centred * centred, axis=1, keepdims=True) + 1e-12)
        normed = centred * inverse
        r.out_f[pl.ds(i * length, rows_pad), :] = normed * r.gain_two[...] + r.shift_two[...]
        pieces = [r.cot_raw[pl.ds((m * items + i) * length, rows_pad), :] for m in range(2)]
        cot = jnp.where(valid, jnp.where(mp == 0, pieces[0], pieces[1]), 0.0)
        g = cot * r.gain_two[...]
        grad = inverse * (
            g - jnp.mean(g, axis=1, keepdims=True) - normed * jnp.mean(g * normed, axis=1, keepdims=True))
        r.gp[rows_of(i), :] = grad
        r.dlow[rows_of(i), :] = grad.astype(BF)
        r.dT[:, lanes_of(i)] = transposed(grad)
        return (gain2 + jnp.sum(cot * normed, axis=0, keepdims=True),
                shift2 + jnp.sum(cot, axis=0, keepdims=True),
                bdown + jnp.sum(grad, axis=0, keepdims=True))

    zero_vec = jnp.zeros((1, width), F32)
    carry = (zero_vec, zero_vec, zero_vec)
    for i in range(items):
        carry = second_norm(i, carry)
    gain2, shift2, bdown = carry
    r.out_v[...] = r.out_f[pl.ds(0, items * length), :].astype(BF)
    out_copy = pltpu.make_async_copy(r.out_v, r.out_h, r.out_sem.at[0])
    out_copy.start()

    def to_core(u):
        return pltpu.make_async_remote_copy(
            src_ref=r.g_out.at[u], dst_ref=r.g_core.at[u], send_sem=r.core_send.at[u],
            recv_sem=r.core_recv.at[u], device_id=core, device_id_type=MESH)

    place_z = jnp.where(z == 0, 0, jnp.where(z == nz - 1, 1, z + 1))
    route = (
        (x, y, z, x_side, y_side), (y, x, z, y_side, x_side),
        (place_z // 2, place_z % 2, y * 2 + x, low_side, high_side), (z // 2, z % 2, y * 2 + x, high_side, low_side))
    shards = 4 * nz

    def shard_order(order):
        if order == X_FIRST:
            return [at(c, b, a) for a in range(2) for b in range(2) for c in range(nz)]
        if order == Y_FIRST:
            return [at(c, a, b) for a in range(2) for b in range(2) for c in range(nz)]
        ring = (0, nz - 1, 1, 2) if order == LOW_FIRST else (0, 1, 2, 3)
        return [at(c, b, a) for c in ring for b in range(2) for a in range(2)]

    def stage_a(u, order):
        first, _, _, device, _ = route[order]
        return pltpu.make_async_remote_copy(
            src_ref=r.g.at[u, pl.ds((1 - first) * 8, 8)], dst_ref=r.g_a.at[u], send_sem=r.a_send.at[u],
            recv_sem=r.a_recv.at[u], device_id=device, device_id_type=MESH)

    def stage_b(u, order):
        first, second, _, _, device = route[order]
        return pltpu.make_async_remote_copy(
            src_ref=r.g.at[u, pl.ds(first * 8 + (1 - second) * 4, 4)], dst_ref=r.g_b.at[u], send_sem=r.b_send.at[u],
            recv_sem=r.b_recv.at[u], device_id=device, device_id_type=MESH)

    def stage_c(u, order, step):
        first, second, _, _, _ = route[order]
        if order in (X_FIRST, Y_FIRST):
            place, device = (z + step) % nz, z_side[step - 1]
        else:
            place, device = ((y + step // 2) % 2) * 2 + (x + step) % 2, plane_side[step - 1]
        return pltpu.make_async_remote_copy(
            src_ref=r.g.at[u, first * 8 + second * 4 + place], dst_ref=r.g_c.at[u, step - 1],
            send_sem=r.c_send.at[u, step - 1], recv_sem=r.c_recv.at[u, step - 1],
            device_id=device, device_id_type=MESH)

    def start_core(u, value):
        r.g_out[u] = value.astype(BF)
        to_core(u).start()

    def start_a(u, value, order):
        to_core(u).wait_recv()
        total_ = (value + r.g_core[u].astype(F32)).astype(BF)
        for place, block in enumerate(shard_order(order)):
            r.g[u, place] = total_[block * shard:(block + 1) * shard]
        stage_a(u, order).start()

    def start_b(u):
        order = ORDER[u]
        stage_a(u, order).wait()
        kept = pl.ds(route[order][0] * 8, 8)
        r.g[u, kept] = r.g[u, kept] + r.g_a[u]
        stage_b(u, order).start()

    def start_c(u):
        order = ORDER[u]
        stage_b(u, order).wait()
        kept = pl.ds(route[order][0] * 8 + route[order][1] * 4, 4)
        r.g[u, kept] = r.g[u, kept] + r.g_b[u]
        for step in range(1, 4):
            stage_c(u, order, step).start()

    def finish(u):
        order = ORDER[u]
        first, second, third, _, _ = route[order]
        acc = r.g[u, first * 8 + second * 4 + third].astype(F32)
        for step in range(1, 4):
            stage_c(u, order, step).wait()
            acc += r.g_c[u, step - 1].astype(F32)
        return acc

    def vec_copy(k, stage, src, device):
        return pltpu.make_async_remote_copy(
            src_ref=src, dst_ref=r.v_in.at[k, stage], send_sem=r.v_send.at[k, stage],
            recv_sem=r.v_recv.at[k, stage], device_id=device, device_id_type=MESH)

    def vec_core(k):
        return vec_copy(k, 0, r.v_out.at[k], core)

    def vec_side(k, stage):
        return vec_copy(k, stage, r.v_sum.at[k, stage - 1], (x_side, y_side)[stage - 1])

    def vec_z(k, step):
        return vec_copy(k, 2 + step, r.v_sum.at[k, 2], z_side[step - 1])

    def vec_next(k, stage):
        if stage == 0:
            vec_core(k).wait()
            r.v_sum[k, 0] = r.v_own[k] + r.v_in[k, 0]
            vec_side(k, 1).start()
        elif stage == 1:
            vec_side(k, 1).wait()
            r.v_sum[k, 1] = r.v_sum[k, 0] + r.v_in[k, 1]
            vec_side(k, 2).start()
        elif stage == 2:
            vec_side(k, 2).wait()
            r.v_sum[k, 2] = r.v_sum[k, 1] + r.v_in[k, 2]
            for step in range(1, nz):
                vec_z(k, step).start()
        else:
            for step in range(1, nz):
                vec_z(k, step).wait()
            terms = [r.v_sum[k, 2]] + [r.v_in[k, 2 + step] for step in range(1, nz)]
            acc = jnp.zeros(terms[0].shape, F32)
            for zz in range(nz):
                came = lax.rem(z - zz + nz, nz)
                term = terms[0]
                for step in range(1, nz):
                    term = jnp.where(came == step, terms[step], term)
                acc = acc + term
            if k == 0:
                for j, ref in enumerate((r.bout_o, r.gain1_o, r.shift1_o, r.bdown_o, r.gain2_o, r.shift2_o)):
                    for part in range(2):
                        ref[:, part * BLOCK:(part + 1) * BLOCK] = acc[2 * j + part:2 * j + part + 1]
                for c in range(chunks):
                    r.bup_o[:, c * BLOCK:(c + 1) * BLOCK] = acc[12 + c:13 + c]
            else:
                r.bq_o[...] = acc[0:1]
                r.bv_o[...] = acc[1:2]

    r.acc[...] = r.gp[...]

    def feed_back(j):
        da = dot_nt(r.dlow[...], r.wd[j])
        ug = (da * r.slope[j].astype(F32)).astype(BF)
        for i in range(items):
            r.upg[i, pl.ds(0, rows_pad), :] = ug[i * rows_pad:(i + 1) * rows_pad]
        r.acc[...] += dot_nt(ug, r.wu[j])
        down = dot_nn(r.dT[...], r.active[j].reshape(items * lanes, BLOCK))
        up = dot_nn(r.hT[...], r.upg[...].reshape(items * lanes, BLOCK))
        return down, up

    def back_far(c, carry):
        down, up = feed_back(chunks + c)
        start_core(2 * c, down)
        start_core(2 * c + 1, up[:width])
        r.v_out[0, pl.ds(12 + c, 1), :] = up[width:width + 1]
        return carry

    lax.fori_loop(0, chunks, back_far, 0)

    def back_own(half, carry):
        for k in range(2):
            c = 2 * half + k
            down, up = feed_back(c)
            start_a(2 * c, down, 2 * k)
            start_a(2 * c + 1, up[:width], 2 * k + 1)
            r.v_own[0, pl.ds(12 + c, 1), :] = up[width:width + 1]
        return carry

    lax.fori_loop(0, chunks // 2, back_own, 0)
    start_b(0)
    start_b(1)

    def first_back(i, carry):
        bout, gain1, shift1 = carry
        hidden_grad = r.acc[rows_of(i), :]
        normed = r.n1[rows_of(i), :]
        inverse = r.inv1[rows_of(i), :][:, :1]
        g = hidden_grad * r.gain_one[...]
        grad = inverse * (
            g - jnp.mean(g, axis=1, keepdims=True) - normed * jnp.mean(g * normed, axis=1, keepdims=True))
        r.gp[rows_of(i), :] = grad
        r.olow[i, pl.ds(0, rows_pad), :] = grad.astype(BF)
        r.dT[:, lanes_of(i)] = transposed(grad)
        return (bout + jnp.sum(grad, axis=0, keepdims=True),
                gain1 + jnp.sum(hidden_grad * normed, axis=0, keepdims=True),
                shift1 + jnp.sum(hidden_grad, axis=0, keepdims=True))

    bout, gain1, shift1 = lax.fori_loop(0, items, first_back, (zero_vec, zero_vec, zero_vec))
    for k, v in enumerate((bout, gain1, shift1, bdown, gain2, shift2)):
        for part in range(2):
            piece = v[:, part * BLOCK:(part + 1) * BLOCK]
            r.v_out[0, pl.ds(2 * k + part, 1), :] = piece
            r.v_own[0, pl.ds(2 * k + part, 1), :] = piece
    vec_core(0).start()
    start_b(2)
    start_b(3)

    start_core(8, dot_nt(r.dT[...], r.ctxT[1]))
    out_grad = dot_nt(r.dT[...], r.ctxT[0])
    for slot in range(2):
        for i in range(items):
            r.cgT[slot * items + i] = dot_nt(r.wo[slot], r.olow[i]).astype(BF)
    start_a(8, out_grad, ORDER[8])
    start_b(4)
    start_b(5)

    def attend_back(n):
        i = lax.rem(n, items)
        slot = n // items
        for h in range(4):
            pair = slice((h // 2) * 128, (h // 2) * 128 + 128)
            head = slice(h * 64, (h + 1) * 64)
            values = r.nat[n, 2, :, pair] * half[h % 2]
            pg = dot_nn(values, r.cgT[n, pair, :])
            p = r.probs[n * 4 + h, pl.ds(0, rows_pad), :].astype(F32)
            inner = jnp.sum(p * pg, axis=0, keepdims=True)
            r.dscore[h % 2, pl.ds(0, rows_pad), :] = (p * (pg - inner)).astype(BF)
            ds = r.dscore[h % 2]
            base = h * 64
            r.gT[slot, pl.ds(base, 64), lanes_of(i)] = dot_nn(r.tra[n, 1, head, :], ds).astype(BF)
            r.gT[slot, pl.ds(256 + base, 64), lanes_of(i)] = dot_nt(r.tra[n, 0, head, :], ds).astype(BF)
            r.gT[slot, pl.ds(512 + base, 64), lanes_of(i)] = dot_nt(
                r.cgT[n, head, :], r.probs[n * 4 + h]).astype(BF)

    def projection_grad(slot, k):
        return dot_nt(r.xT[...], r.gT[slot, pl.ds(k * 256, 256), :])

    after = (
        lambda: (start_b(6), start_b(7), start_c(0), start_c(1), vec_next(0, 0)),
        lambda: (start_c(2), start_c(3), start_b(8), vec_next(0, 1)),
        lambda: (start_c(4), start_c(5), vec_next(0, 2)),
        lambda: (start_c(6), start_c(7), vec_next(0, 3)),
        lambda: (start_c(8),),
        lambda: None)

    for n in range(2 * items):
        attend_back((n + items) % (2 * items))
        after[n]()
        if n == items - 1:
            for k in range(3):
                grad = projection_grad(1, k)
                start_core(9 + k, grad[:width])
                if k == 0:
                    r.v_out[1, pl.ds(0, 1), :] = grad[width:width + 1]
                if k == 2:
                    r.v_out[1, pl.ds(1, 1), :] = grad[width:width + 1]
            vec_core(1).start()
    for k in range(3):
        grad = projection_grad(0, k)
        start_a(9 + k, grad[:width], ORDER[9 + k])
        if k == 0:
            r.v_own[1, pl.ds(0, 1), :] = grad[width:width + 1]
        if k == 2:
            r.v_own[1, pl.ds(1, 1), :] = grad[width:width + 1]
    vec_next(1, 0)

    for i in range(items):
        acc = None
        for slot in range(2):
            for k in range(3):
                term = dot_nn(r.wqkv[slot, k], r.gT[slot, pl.ds(k * 256, 256), lanes_of(i)])
                acc = term if acc is None else acc + term
        r.ig_v[pl.ds(i * length, length), :] = acc.T[:length] + r.gp[pl.ds(i * rows_pad, length), :]
    grad_copy = pltpu.make_async_copy(r.ig_v, r.ig_h, r.out_sem.at[1])
    grad_copy.start()
    for k in range(3):
        start_b(9 + k)
    vec_next(1, 1)
    for c in range(chunks):
        r.gd_o[:, c * BLOCK:(c + 1) * BLOCK] = finish(2 * c)
        r.gu_o[:, c * BLOCK:(c + 1) * BLOCK] = finish(2 * c + 1)
    r.go_o[...] = finish(8)
    for k in range(3):
        start_c(9 + k)
    vec_next(1, 2)
    r.gq_o[...] = finish(9)
    r.gk_o[...] = finish(10)
    r.gv_o[...] = finish(11)
    vec_next(1, 3)

    for s in remote:
        s.wait_send()
    for u in range(UNITS):
        to_core(u).wait_send()
    out_copy.wait()
    grad_copy.wait()


def hand_over(count, *refs):
    held, sems = refs[2 * count:3 * count], refs[-1]
    into = [pltpu.make_async_copy(refs[k], held[k], sems.at[0, k]) for k in range(count)]
    out = [pltpu.make_async_copy(held[k], refs[count + k], sems.at[1, k]) for k in range(count)]
    for c in into:
        c.start()
    for c, d in zip(into, out, strict=True):
        c.wait()
        d.start()
    for d in out:
        d.wait()


def layer_by_items(
    inputs, region_counts, w_query, b_query, w_key, w_value, b_value, w_out, b_out, gain_one, shift_one,
    w_up, b_up, w_down, b_down, gain_two, shift_two, cotangent,
):
    total_rows, width = inputs.shape
    item_count = region_counts.shape[0]
    length = total_rows // item_count
    items = item_count // 2
    rows_pad = -(-length // ITEM_PAD) * ITEM_PAD
    lanes = -(-length // 128) * 128
    dp_size = lax.axis_size("dp")
    nz = dp_size // 4
    shard = width // dp_size
    total = items * rows_pad
    chunks = w_up.shape[1] // BLOCK
    own_rows = items * length

    two_chunks = 2 * chunks
    hd = w_query.shape[1]
    inner = [
        ("x_raw", (total_rows, width), BF), ("x_v", (total, width), BF), ("cot_raw", (total_rows + 16, width), F32),
        ("bias_q", (2, 1, BLOCK), F32), ("bias_v", (2, 1, BLOCK), F32), ("bias_u", (2, 1, chunks * BLOCK), F32),
        ("b_out", (1, width), F32), ("gain_one", (1, width), F32), ("shift_one", (1, width), F32),
        ("b_down", (1, width), F32), ("gain_two", (1, width), F32), ("shift_two", (1, width), F32),
        ("wqkv", (2, 3, width, hd), BF), ("wo", (2, hd, width), BF),
        ("wu", (two_chunks, width, BLOCK), BF), ("wd", (two_chunks, BLOCK, width), BF),
        ("xT", (width + 16, items * lanes), BF), ("hT", (width + 16, items * lanes), BF),
        ("dT", (width, items * lanes), BF),
        ("nat", (2 * items, 3, rows_pad, hd), BF), ("tra", (2 * items, 3, hd, lanes), BF),
        ("probs", (8 * items, lanes, lanes), BF), ("ctxT", (2, hd, items * lanes), BF),
        ("ctx", (2, total, hd), BF), ("n1", (total, width), F32), ("inv1", (total, 128), F32),
        ("hlow", (total, width), BF), ("slope", (two_chunks, total, BLOCK), BF),
        ("active", (two_chunks, items, lanes, BLOCK), BF), ("acc", (total, width), F32),
        ("out_f", (total, width), F32), ("out_v", (own_rows, width), BF), ("ig_v", (own_rows, width), F32), ("gp", (total, width), F32), ("dlow", (total, width), BF),
        ("upg", (items, lanes, BLOCK), BF), ("olow", (items, lanes, width), BF),
        ("cgT", (2 * items, hd, lanes), BF), ("dscore", (2, lanes, lanes), BF),
        ("gT", (2, 3 * hd, items * lanes), BF),
        ("g_out", (UNITS, width, BLOCK), BF), ("g_core", (UNITS, width, BLOCK), BF),
        ("g", (UNITS, 16, shard, BLOCK), BF), ("g_a", (UNITS, 8, shard, BLOCK), BF),
        ("g_b", (UNITS, 4, shard, BLOCK), BF), ("g_c", (UNITS, 3, shard, BLOCK), BF),
        ("v_out", (2, 16, BLOCK), F32), ("v_own", (2, 16, BLOCK), F32),
        ("v_in", (2, 2 + nz, 16, BLOCK), F32), ("v_sum", (2, 3, 16, BLOCK), F32),
    ]
    n_weights = 8 + chunks
    sems = [
        ("in_sem", (16 + chunks,)), ("w_send", (n_weights,)), ("w_recv", (n_weights,)), ("out_sem", (2,)),
        ("core_send", (UNITS,)), ("core_recv", (UNITS,)), ("a_send", (UNITS,)), ("a_recv", (UNITS,)),
        ("b_send", (UNITS,)), ("b_recv", (UNITS,)), ("c_send", (UNITS, 3)), ("c_recv", (UNITS, 3)),
        ("v_send", (2, 2 + nz)), ("v_recv", (2, 2 + nz)),
    ]
    operands = [
        ("counts", region_counts), ("x_h", inputs), ("cot_h", cotangent), ("wq_h", w_query), ("wk_h", w_key),
        ("wv_h", w_value), ("wo_h", w_out), ("wu_h", w_up), ("wd_h", w_down.reshape(chunks, BLOCK, width)),
        ("b_query_h", b_query[None]), ("b_value_h", b_value[None]), ("b_up_h", b_up[None]), ("b_out_h", b_out[None]),
        ("gain_one_h", gain_one[None]), ("shift_one_h", shift_one[None]), ("b_down_h", b_down[None]),
        ("gain_two_h", gain_two[None]), ("shift_two_h", shift_two[None]),
    ]
    hidden = chunks * BLOCK
    results = [
        ("out_h", (own_rows, width), BF, pl.ANY), ("ig_h", (own_rows, width), F32, pl.ANY),
        ("gq_o", (shard, hd), F32, pltpu.VMEM), ("bq_o", (1, hd), F32, pltpu.VMEM),
        ("gk_o", (shard, hd), F32, pltpu.VMEM), ("gv_o", (shard, hd), F32, pltpu.VMEM),
        ("bv_o", (1, hd), F32, pltpu.VMEM), ("go_o", (shard, hd), F32, pltpu.VMEM),
        ("bout_o", (1, width), F32, pltpu.VMEM), ("gain1_o", (1, width), F32, pltpu.VMEM),
        ("shift1_o", (1, width), F32, pltpu.VMEM), ("gu_o", (shard, hidden), F32, pltpu.VMEM),
        ("bup_o", (1, hidden), F32, pltpu.VMEM), ("gd_o", (shard, hidden), F32, pltpu.VMEM),
        ("bdown_o", (1, width), F32, pltpu.VMEM), ("gain2_o", (1, width), F32, pltpu.VMEM),
        ("shift2_o", (1, width), F32, pltpu.VMEM),
    ]
    names = [n for n, _ in operands] + [n for n, *_ in results] + [n for n, *_ in inner] + [n for n, _ in sems]
    smem = pl.BlockSpec(memory_space=pltpu.SMEM)
    shapes = [jax.ShapeDtypeStruct(s, d) for _, s, d, _ in results]
    made = pl.pallas_call(
        functools.partial(layer_kernel, (items, length, rows_pad, lanes, nz, shard), names),
        out_shape=shapes,
        in_specs=[smem] + [pl.BlockSpec(memory_space=pl.ANY)] * (len(operands) - 1),
        out_specs=[pl.BlockSpec(memory_space=m) for *_, m in results],
        scratch_shapes=[pltpu.VMEM(s, d) for _, s, d in inner] + [pltpu.SemaphoreType.DMA(s) for _, s in sems],
        compiler_params=pltpu.CompilerParams(
            collective_id=0, has_side_effects=True, vmem_limit_bytes=63 * 2**20),
        name="layer",
    )(*[v for _, v in operands])
    count = len(shapes)
    made = pl.pallas_call(
        functools.partial(hand_over, count),
        out_shape=shapes,
        in_specs=[pl.BlockSpec(memory_space=pl.ANY)] * count,
        out_specs=[pl.BlockSpec(memory_space=pl.ANY)] * count,
        scratch_shapes=[pltpu.VMEM(s.shape, s.dtype) for s in shapes] + [pltpu.SemaphoreType.DMA((2, count))],
        name="hand_over",
    )(*made)
    made = [v.reshape(-1) if v.shape[0] == 1 else v for v in made]
    made[7], made[13] = made[7].T, made[13].T
    return tuple(made)


def solution(mesh):
    placed = (
        P("dp", None),
        P("dp"),
        P(None, "mp"),
        P("mp"),
        P(None, "mp"),
        P(None, "mp"),
        P("mp"),
        P("mp", None),
        P(),
        P(),
        P(),
        P(None, "mp"),
        P("mp"),
        P("mp", None),
        P(),
        P(),
        P(),
        P("dp", None),
    )
    dp_size, mp_size = mesh.shape["dp"], mesh.shape["mp"]

    def body(*args):
        width, hidden = args[0].shape[1], args[11].shape[1]
        whole_items = mp_size == 2 and args[1].shape[0] % 2 == 0
        even_shards = dp_size == 16 and width % (16 * dp_size) == 0
        blocks = args[2].shape[1] == BLOCK and width == 2 * BLOCK and hidden == 4 * BLOCK
        fits = args[0].shape[0] // args[1].shape[0] <= 256
        if whole_items and even_shards and blocks and fits:
            return layer_by_items(*args)
        return per_device(*args)

    return jax.shard_map(
        body,
        mesh=mesh,
        in_specs=placed,
        out_specs=(
            P(("dp", "mp"), None),
            P(("dp", "mp"), None),
            P("dp", "mp"),
            P("mp"),
            P("dp", "mp"),
            P("dp", "mp"),
            P("mp"),
            P("mp", "dp"),
            P(),
            P(),
            P(),
            P("dp", "mp"),
            P("mp"),
            P("mp", "dp"),
            P(),
            P(),
            P(),
        ),
        check_vma=False,
    )
```

```python
import functools
import types

import jax
import jax.numpy as jnp
from jax import lax
from jax.experimental import pallas as pl
from jax.experimental.pallas import tpu as pltpu
from jax.sharding import PartitionSpec as P

HEAD_DIM = 64
TEXT = 128


def layer_stats(pre_rows):
    row_mean = jnp.mean(pre_rows, axis=-1, keepdims=True)
    centred = pre_rows - row_mean
    inverse = lax.rsqrt(jnp.mean(centred * centred, axis=-1, keepdims=True) + 1e-12)
    return (centred * inverse, inverse)


def norm_back(grad_rows, normed, inverse, gain_vec):
    scaled = grad_rows * gain_vec
    return inverse * (
        scaled
        - jnp.mean(scaled, axis=-1, keepdims=True)
        - normed * jnp.mean(scaled * normed, axis=-1, keepdims=True)
    )


def gelu_slope(upper_part):
    return (
        0.5 * (1.0 + lax.erf(upper_part * 0.7071067811865476))
        + upper_part * jnp.exp(-0.5 * upper_part * upper_part) * 0.3989422804014327
    )


def contract_rows(first_op, second_op):
    return lax.dot_general(
        first_op, second_op, (((0,), (0,)), ((), ())), preferred_element_type=jnp.float32
    )


def times_transposed(first_op, second_op):
    return lax.dot_general(
        first_op, second_op, (((1,), (1,)), ((), ())), preferred_element_type=jnp.float32
    )


def per_device(
    inputs,
    region_counts,
    w_query,
    b_query,
    w_key,
    w_value,
    b_value,
    w_out,
    b_out,
    gain_one,
    shift_one,
    w_up,
    b_up,
    w_down,
    b_down,
    gain_two,
    shift_two,
    cotangent,
):
    total_rows = inputs.shape[0]
    item_count = region_counts.shape[0]
    length = total_rows // item_count
    heads_here = w_query.shape[1] // HEAD_DIM
    score_scale = HEAD_DIM ** (-0.5)
    share_rows = total_rows // lax.axis_size("mp")
    row_start = lax.axis_index("mp") * share_rows

    def own_rows(full_rows):
        return lax.dynamic_slice_in_dim(full_rows, row_start, share_rows, 0)

    def split_heads(flat_rows):
        return flat_rows.reshape(item_count, length, heads_here, HEAD_DIM)

    position = jnp.arange(length)
    visible = (position[None, :] < TEXT) | (position[None, :] - TEXT < region_counts[:, None])
    key_mask = visible[:, None, None, :]
    queries = (jnp.dot(inputs, w_query, preferred_element_type=jnp.float32) + b_query).astype(
        jnp.bfloat16
    )
    key_rows = jnp.dot(inputs, w_key, preferred_element_type=jnp.float32).astype(jnp.bfloat16)
    value_rows = (jnp.dot(inputs, w_value, preferred_element_type=jnp.float32) + b_value).astype(
        jnp.bfloat16
    )
    query_heads = split_heads(queries)
    key_heads = split_heads(key_rows)
    value_heads = split_heads(value_rows)

    def masked_scores():
        raw_scores = (
            jnp.einsum(
                "ishd,ithd->ihst", query_heads, key_heads, preferred_element_type=jnp.float32
            )
            * score_scale
        )
        return jnp.where(key_mask, raw_scores, -1000000000.0)

    scores = masked_scores()
    row_top = jnp.max(scores, axis=-1, keepdims=True)
    exponent = jnp.exp(scores - row_top)
    row_total = jnp.sum(exponent, axis=-1, keepdims=True)
    probs = exponent / row_total
    log_total = row_top + jnp.log(row_total)
    context = jnp.einsum(
        "ihst,ithd->ishd",
        probs.astype(jnp.bfloat16),
        value_heads,
        preferred_element_type=jnp.float32,
    )
    context = context.reshape(total_rows, heads_here * HEAD_DIM).astype(jnp.bfloat16)
    partial_attn = jnp.dot(context, w_out, preferred_element_type=jnp.float32)
    attended = lax.psum(partial_attn, "mp")
    normed_one, inverse_one = layer_stats(attended + b_out + inputs.astype(jnp.float32))
    hidden_one = normed_one * gain_one + shift_one
    hidden_low = hidden_one.astype(jnp.bfloat16)
    upper_part = jnp.dot(hidden_low, w_up, preferred_element_type=jnp.float32) + b_up
    active = jax.nn.gelu(upper_part, approximate=False).astype(jnp.bfloat16)
    partial_ffn = jnp.dot(active, w_down, preferred_element_type=jnp.float32)
    lowered = lax.psum(partial_ffn, "mp")
    normed_two, inverse_two = layer_stats(lowered + b_down + hidden_one)
    output = own_rows(normed_two * gain_two + shift_two).astype(jnp.bfloat16)
    grad_pre_two = norm_back(cotangent, normed_two, inverse_two, gain_two)
    down_low = grad_pre_two.astype(jnp.bfloat16)
    grad_output = own_rows(cotangent)
    normed_two_own = own_rows(normed_two)
    grad_two_own = own_rows(grad_pre_two)
    grad_gain_two = jnp.sum(grad_output * normed_two_own, axis=0)
    grad_shift_two = jnp.sum(grad_output, axis=0)
    grad_b_down = jnp.sum(grad_two_own, axis=0)
    grad_w_down = contract_rows(active, down_low)
    active_grad = times_transposed(down_low, w_down)
    upper_grad = (active_grad * gelu_slope(upper_part)).astype(jnp.bfloat16)
    grad_b_up = jnp.sum(upper_grad.astype(jnp.float32), axis=0)
    grad_w_up = contract_rows(hidden_low, upper_grad)
    partial_hidden = times_transposed(upper_grad, w_up)
    hidden_grad = lax.psum(partial_hidden, "mp") + grad_pre_two
    grad_pre_one = norm_back(hidden_grad, normed_one, inverse_one, gain_one)
    out_low = grad_pre_one.astype(jnp.bfloat16)
    hidden_grad_own = own_rows(hidden_grad)
    normed_one_own = own_rows(normed_one)
    grad_one_own = own_rows(grad_pre_one)
    grad_gain_one = jnp.sum(hidden_grad_own * normed_one_own, axis=0)
    grad_shift_one = jnp.sum(hidden_grad_own, axis=0)
    grad_b_out = jnp.sum(grad_one_own, axis=0)
    grad_w_out = contract_rows(context, out_low)
    context_grad = split_heads(times_transposed(out_low, w_out).astype(jnp.bfloat16))
    probs_again = jnp.exp(masked_scores() - log_total)
    prob_grad = jnp.einsum(
        "ishd,ithd->ihst", context_grad, value_heads, preferred_element_type=jnp.float32
    )
    row_inner = jnp.sum(probs_again * prob_grad, axis=-1, keepdims=True)
    score_grad = (probs_again * (prob_grad - row_inner)).astype(jnp.bfloat16)
    query_grad = (
        (
            jnp.einsum("ihst,ithd->ishd", score_grad, key_heads, preferred_element_type=jnp.float32)
            * score_scale
        )
        .astype(jnp.bfloat16)
        .reshape(total_rows, heads_here * HEAD_DIM)
    )
    key_grad = (
        (
            jnp.einsum(
                "ihst,ishd->ithd", score_grad, query_heads, preferred_element_type=jnp.float32
            )
            * score_scale
        )
        .astype(jnp.bfloat16)
        .reshape(total_rows, heads_here * HEAD_DIM)
    )
    value_grad = jnp.einsum(
        "ihst,ishd->ithd",
        probs_again.astype(jnp.bfloat16),
        context_grad,
        preferred_element_type=jnp.float32,
    ).astype(jnp.bfloat16)
    value_grad = value_grad.reshape(total_rows, heads_here * HEAD_DIM)
    grad_b_query = jnp.sum(query_grad.astype(jnp.float32), axis=0)
    grad_b_value = jnp.sum(value_grad.astype(jnp.float32), axis=0)
    grad_w_query = contract_rows(inputs, query_grad)
    grad_w_key = contract_rows(inputs, key_grad)
    grad_w_value = contract_rows(inputs, value_grad)
    partial_input = (
        times_transposed(query_grad, w_query)
        + times_transposed(key_grad, w_key)
        + times_transposed(value_grad, w_value)
    )
    input_grad = own_rows(
        lax.psum(partial_input.astype(jnp.bfloat16), "mp").astype(jnp.float32) + grad_pre_one
    )
    bias_sums = lax.psum((grad_b_query, grad_b_value, grad_b_up), "dp")
    norm_sums = lax.psum(
        (grad_b_out, grad_gain_one, grad_shift_one, grad_b_down, grad_gain_two, grad_shift_two),
        ("dp", "mp"),
    )
    weight_sums = (
        lax.psum_scatter(
            grad_w_query.astype(jnp.bfloat16), "dp", scatter_dimension=0, tiled=True
        ).astype(jnp.float32),
        lax.psum_scatter(
            grad_w_key.astype(jnp.bfloat16), "dp", scatter_dimension=0, tiled=True
        ).astype(jnp.float32),
        lax.psum_scatter(
            grad_w_value.astype(jnp.bfloat16), "dp", scatter_dimension=0, tiled=True
        ).astype(jnp.float32),
        lax.psum_scatter(
            grad_w_out.astype(jnp.bfloat16), "dp", scatter_dimension=1, tiled=True
        ).astype(jnp.float32),
        lax.psum_scatter(
            grad_w_up.astype(jnp.bfloat16), "dp", scatter_dimension=0, tiled=True
        ).astype(jnp.float32),
        lax.psum_scatter(
            grad_w_down.astype(jnp.bfloat16), "dp", scatter_dimension=1, tiled=True
        ).astype(jnp.float32),
    )
    return (
        output,
        input_grad,
        weight_sums[0],
        bias_sums[0],
        weight_sums[1],
        weight_sums[2],
        bias_sums[1],
        weight_sums[3],
        norm_sums[0],
        norm_sums[1],
        norm_sums[2],
        weight_sums[4],
        bias_sums[2],
        weight_sums[5],
        norm_sums[3],
        norm_sums[4],
        norm_sums[5],
    )


ITEM_PAD = 16
MESH = pl.DeviceIdType.MESH
BF = jnp.bfloat16
F32 = jnp.float32
BLOCK = 256
UNITS = 12
X_FIRST, Y_FIRST, Z_FIRST = 0, 1, 2
ORDER = (0, 1, 2, 0, 1, 2, 0, 1, 1, 1, 2, 0)


def dot_nn(a, b):
    return lax.dot_general(a, b, (((1,), (0,)), ((), ())), preferred_element_type=F32)


def dot_nt(a, b):
    return lax.dot_general(a, b, (((1,), (1,)), ((), ())), preferred_element_type=F32)


def layer_kernel(dims, names, *refs):
    r = types.SimpleNamespace(**dict(zip(names, refs, strict=True)))
    items, length, rows_pad, lanes, nz, shard = dims
    total = items * rows_pad
    chunks = r.wu_h.shape[1] // BLOCK
    width = r.x_h.shape[1]
    dp, mp = lax.axis_index("dp"), lax.axis_index("mp")
    z, y, x = dp // 4, (dp // 2) % 2, dp % 2

    def at(z_, y_, x_):
        return z_ * 4 + y_ * 2 + x_

    core = (dp, 1 - mp)
    x_side = (at(z, y, 1 - x), mp)
    y_side = (at(z, 1 - y, x), mp)
    z_side = [(at((z + step) % nz, y, x), mp) for step in range(1, nz)]
    low_side = (at(z + 1 - 2 * (z % 2), y, x), mp)
    high_side = z_side[1]
    plane_side = [(at(z, (y + step // 2) % 2, (x + step) % 2), mp) for step in range(1, 4)]

    local = []

    def bring(src, dst):
        copy = pltpu.make_async_copy(src, dst, r.in_sem.at[len(local)])
        copy.start()
        local.append(copy)
        return copy

    c_x = bring(r.x_h, r.x_raw)
    c_w = [bring(src, r.wqkv.at[0, k]) for k, src in enumerate((r.wq_h, r.wk_h, r.wv_h))]
    c_p = [bring(r.b_query_h, r.bias_q.at[0]), bring(r.b_value_h, r.bias_v.at[0]), bring(r.b_up_h, r.bias_u.at[0])]
    vectors = (
        (r.b_out_h, r.b_out), (r.gain_one_h, r.gain_one), (r.shift_one_h, r.shift_one),
        (r.b_down_h, r.b_down), (r.gain_two_h, r.gain_two), (r.shift_two_h, r.shift_two))
    c_vec = [bring(src, dst) for src, dst in vectors]
    c_wo = bring(r.wo_h, r.wo.at[0])
    c_wu = [bring(r.wu_h.at[:, pl.ds(c * BLOCK, BLOCK)], r.wu.at[c]) for c in range(chunks)]
    c_wd = bring(r.wd_h, r.wd.at[pl.ds(0, chunks)])
    full_rows = r.x_h.shape[0]
    base = items * length // 8 * 8
    cot_count = full_rows - base
    c_cot = bring(r.cot_h.at[pl.ds(pl.multiple_of(mp * base, 8), cot_count)], r.cot_raw.at[pl.ds(0, cot_count)])

    barrier = pltpu.get_barrier_semaphore()
    near = [core] + plane_side + z_side
    for device in near:
        pl.semaphore_signal(barrier, inc=1, device_id=device, device_id_type=MESH)
    pl.semaphore_wait(barrier, len(near))

    remote = []

    def send_weight(src, dst):
        k = len(remote)
        copy = pltpu.make_async_remote_copy(
            src_ref=src, dst_ref=dst, send_sem=r.w_send.at[k], recv_sem=r.w_recv.at[k],
            device_id=core, device_id_type=MESH)
        copy.start()
        remote.append(copy)
        return copy

    s_w = [send_weight(src, r.wqkv.at[1, k]) for k, src in enumerate((r.wq_h, r.wk_h, r.wv_h))]
    s_w += [send_weight(src, dst.at[1]) for src, dst in (
        (r.b_query_h, r.bias_q), (r.b_value_h, r.bias_v), (r.b_up_h, r.bias_u))]
    s_wo = send_weight(r.wo_h, r.wo.at[1])
    s_wu = [send_weight(r.wu_h.at[:, pl.ds(c * BLOCK, BLOCK)], r.wu.at[chunks + c]) for c in range(chunks)]
    s_wd = send_weight(r.wd_h, r.wd.at[pl.ds(chunks, chunks)])

    pad_rows = lanes - rows_pad

    def transposed(block):
        full = jnp.concatenate([block, jnp.zeros((pad_rows, block.shape[1]), F32)], axis=0)
        return full.T.astype(BF)

    def rows_of(i):
        return pl.ds(pl.multiple_of(i * rows_pad, 16), rows_pad)

    def lanes_of(i):
        return pl.ds(pl.multiple_of(i * lanes, lanes), lanes)

    def clear(n, carry):
        r.probs[n, pl.ds(rows_pad, pad_rows), :] = jnp.zeros((pad_rows, lanes), BF)
        return carry

    lax.fori_loop(0, r.probs.shape[0], clear, 0)
    zero_block = jnp.zeros((pad_rows, BLOCK), BF)
    for i in range(items):
        r.olow[i, pl.ds(rows_pad, pad_rows), :] = jnp.zeros((pad_rows, width), BF)
        for j in range(r.upg.shape[0]):
            r.upg[j, i, pl.ds(rows_pad, pad_rows), :] = zero_block
        for j in range(2 * chunks):
            r.active[j, i, pl.ds(rows_pad, pad_rows), :] = zero_block
    for k in range(r.dscore.shape[0]):
        r.dscore[k, pl.ds(rows_pad, pad_rows), :] = jnp.zeros((pad_rows, lanes), BF)
    one_row = jnp.where(lax.broadcasted_iota(jnp.int32, (16, items * lanes), 0) == 0, 1.0, 0.0).astype(BF)
    r.xT[pl.ds(width, 16), :] = one_row
    r.hT[pl.ds(width, 16), :] = one_row
    cot_rows = r.cot_raw.shape[0]
    r.cot_raw[pl.ds(cot_count, cot_rows - cot_count), :] = jnp.zeros((cot_rows - cot_count, width), F32)

    c_x.wait()
    down_ = lax.broadcasted_iota(jnp.int32, (rows_pad, 256), 0)
    across = lax.broadcasted_iota(jnp.int32, (rows_pad, 256), 1)
    for i in range(items):
        block = None
        for m in range(2):
            start = (m * items + i) * length
            window = start // 16 * 16
            count = min(256, full_rows - window)
            shift = jnp.where(mp == m, start - window, 2 * 256)
            pick = jnp.where((across == down_ + shift) & (down_ < length), 1.0, 0.0).astype(BF)
            term = dot_nn(pick[:, :count], r.x_raw[pl.ds(window, count), :])
            block = term if block is None else block + term
        r.x_v[rows_of(i), :] = block.astype(BF)

    def project(slot, k):
        r.work[k] = dot_nn(r.x_v[...], r.wqkv[slot, k])

    def keep(slot, k):
        for i in range(items):
            block = r.work[k, pl.ds(i * rows_pad, rows_pad), :]
            n = slot * items + i
            if k == 0:
                r.tra[n, 0] = transposed((block + r.bias_q[slot]) * 0.125)
            elif k == 1:
                r.keys[n] = block.astype(BF)
            else:
                block = block + r.bias_v[slot]
                r.values[n] = block.astype(BF)
                r.tra[n, 2] = transposed(block)

    for c in c_w + c_p:
        c.wait()
    for k in range(3):
        project(0, k)
    for k in range(3):
        keep(0, k)
    for c in s_w:
        c.wait_recv()
    for k in range(3):
        project(1, k)

    lane = lax.broadcasted_iota(jnp.int32, (1, 128), 1)
    half = [jnp.where(lane < 64, 1.0, 0.0).astype(BF), jnp.where(lane >= 64, 1.0, 0.0).astype(BF)]
    position = lax.broadcasted_iota(jnp.int32, (rows_pad, lanes), 0)

    def pair_of(h):
        return slice((h // 2) * 128, (h // 2) * 128 + 128)

    def head_of(h):
        return slice(h * 64, (h + 1) * 64)

    def scores_of(n):
        for h in range(4):
            r.score[(n % 2) * 4 + h] = dot_nn(r.keys[n, :, pair_of(h)] * half[h % 2], r.tra[n, 0, pair_of(h), :])

    def soften(n):
        mask = jnp.where(position < TEXT + r.counts[mp * items + n % items], 0.0, -1e9)
        for h in range(4):
            score = r.score[(n % 2) * 4 + h] + mask
            top = jnp.max(score, axis=0, keepdims=True)
            e = jnp.exp(score - top)
            p = e * (1.0 / jnp.sum(e, axis=0, keepdims=True))
            r.probs[n * 4 + h, pl.ds(0, rows_pad), :] = p.astype(BF)

    def contexts_of(n):
        parts = [dot_nn(r.tra[n, 2, head_of(h), :], r.probs[n * 4 + h]) for h in range(4)]
        context = jnp.concatenate(parts, axis=0)
        slot, i = n // items, n % items
        r.ctxT[slot, :, pl.ds(i * lanes, lanes)] = context.astype(BF)
        r.ctx[slot, pl.ds(i * rows_pad, rows_pad), :] = context.T[:rows_pad].astype(BF)

    scores_of(0)
    for n in range(2 * items):
        if n + 1 < 2 * items:
            if n + 1 == items:
                for k in range(3):
                    keep(1, k)
            scores_of(n + 1)
        soften(n)
        contexts_of(n)

    c_wo.wait()
    s_wo.wait_recv()
    for c in c_vec:
        c.wait()

    def attended(i):
        rows = pl.ds(i * rows_pad, rows_pad)
        r.acc[rows, :] = dot_nn(r.ctx[0, rows, :], r.wo[0]) + dot_nn(r.ctx[1, rows, :], r.wo[1])

    def first_norm(i):
        rows = pl.ds(i * rows_pad, rows_pad)
        pre = r.acc[rows, :] + r.b_out[...] + r.x_v[rows, :].astype(F32)
        centred = pre - jnp.mean(pre, axis=1, keepdims=True)
        inverse = lax.rsqrt(jnp.mean(centred * centred, axis=1, keepdims=True) + 1e-12)
        normed = centred * inverse
        r.n1[rows, :] = normed
        r.inv1[rows, :] = jnp.broadcast_to(inverse, (rows_pad, 128))
        r.hlow[rows, :] = (normed * r.gain_one[...] + r.shift_one[...]).astype(BF)

    for i in range(items):
        attended(i)
    for i in range(items):
        first_norm(i)

    for c in c_wu + [c_wd]:
        c.wait()
    for c in s_wu + [s_wd]:
        c.wait_recv()
    c_cot.wait()
    valid = lax.broadcasted_iota(jnp.int32, (rows_pad, 1), 0) < length

    def own_cotangent(i):
        at_ = [r.cot_raw[pl.ds(m * (items * length - base) + i * length, rows_pad), :] for m in range(2)]
        r.cot[pl.ds(i * rows_pad, rows_pad), :] = jnp.where(valid, jnp.where(mp == 0, at_[0], at_[1]), 0.0)

    def lift(j):
        slot, c = j // chunks, j % chunks
        r.work[j % 2] = dot_nn(r.hlow[...], r.wu[j]) + r.bias_u[slot, :, c * BLOCK:(c + 1) * BLOCK]

    def activate(j):
        for i in range(items):
            rows = pl.ds(i * rows_pad, rows_pad)
            u = r.work[j % 2, rows, :]
            phi = 0.5 + 0.5 * lax.erf(u * 0.7071067811865476)
            r.slope[j, rows, :] = (phi + u * (jnp.exp(-0.5 * u * u) * 0.3989422804014327)).astype(BF)
            r.active[j, i, pl.ds(0, rows_pad), :] = (u * phi).astype(BF)

    def lower(j):
        part = dot_nn(r.active[j][:, :rows_pad].reshape(total, BLOCK), r.wd[j])
        if j == 0:
            r.acc[...] = part
        else:
            r.acc[...] += part

    lift(0)
    for j in range(2 * chunks):
        if j > 0:
            lower(j - 1)
        if j + 1 < 2 * chunks:
            lift(j + 1)
        activate(j)
        if 2 <= j < 2 + items:
            own_cotangent(j - 2)
    lower(2 * chunks - 1)

    def mean(v):
        return jnp.mean(v, axis=1, keepdims=True)

    def column_sum(v):
        return jnp.sum(v, axis=0, keepdims=True)

    gain2, shift2, bdown = [], [], []

    def second_norm(i):
        rows = pl.ds(i * rows_pad, rows_pad)
        hidden = r.n1[rows, :] * r.gain_one[...] + r.shift_one[...]
        pre = r.acc[rows, :] + r.b_down[...] + hidden
        centred = pre - mean(pre)
        inverse = lax.rsqrt(mean(centred * centred) + 1e-12)
        normed = centred * inverse
        cot = r.cot[rows, :]
        g = cot * r.gain_two[...]
        grad = inverse * (g - mean(g) - normed * mean(g * normed))
        r.gp[rows, :] = grad
        r.dlow[rows, :] = grad.astype(BF)
        r.dT[:, pl.ds(i * lanes, lanes)] = transposed(grad)
        r.acc[pl.ds(i * length, rows_pad), :] = normed * r.gain_two[...] + r.shift_two[...]
        gain2.append(column_sum(cot * normed))
        shift2.append(column_sum(cot))
        bdown.append(column_sum(grad))

    for i in range(items):
        second_norm(i)

    def to_core(u):
        return pltpu.make_async_remote_copy(
            src_ref=r.g_out.at[u], dst_ref=r.g.at[u], send_sem=r.core_send.at[u],
            recv_sem=r.core_recv.at[u], device_id=core, device_id_type=MESH)

    route = (
        (x, y, z, x_side, y_side), (y, x, z, y_side, x_side), (z % 2, z // 2, y * 2 + x, low_side, high_side))

    def shard_order(order):
        if order == X_FIRST:
            return [at(c, b, a) for a in range(2) for b in range(2) for c in range(nz)]
        if order == Y_FIRST:
            return [at(c, a, b) for a in range(2) for b in range(2) for c in range(nz)]
        return [at(2 * b + a, c, d) for a in range(2) for b in range(2) for c in range(2) for d in range(2)]

    def stage_a(u, order):
        first, _, _, device, _ = route[order]
        return pltpu.make_async_remote_copy(
            src_ref=r.g.at[u, pl.ds((1 - first) * 8, 8)], dst_ref=r.g_a.at[u], send_sem=r.a_send.at[u],
            recv_sem=r.a_recv.at[u], device_id=device, device_id_type=MESH)

    def stage_b(u, order):
        first, second, _, _, device = route[order]
        return pltpu.make_async_remote_copy(
            src_ref=r.g.at[u, pl.ds(first * 8 + (1 - second) * 4, 4)], dst_ref=r.g_b.at[u], send_sem=r.b_send.at[u],
            recv_sem=r.b_recv.at[u], device_id=device, device_id_type=MESH)

    def stage_c(u, order, step):
        first, second, _, _, _ = route[order]
        if order in (X_FIRST, Y_FIRST):
            place, device = (z + step) % nz, z_side[step - 1]
        else:
            place, device = ((y + step // 2) % 2) * 2 + (x + step) % 2, plane_side[step - 1]
        return pltpu.make_async_remote_copy(
            src_ref=r.g.at[u, first * 8 + second * 4 + place], dst_ref=r.g_c.at[u, step - 1],
            send_sem=r.c_send.at[u, step - 1], recv_sem=r.c_recv.at[u, step - 1],
            device_id=device, device_id_type=MESH)

    def start_core(u, value):
        for place, block in enumerate(shard_order(ORDER[u])):
            r.g_out[u, place] = value[block * shard:(block + 1) * shard].astype(BF)
        to_core(u).start()

    def hold(u, value):
        r.own[u % r.own.shape[0]] = value

    def start_a(u):
        to_core(u).wait_recv()
        for place, block in enumerate(shard_order(ORDER[u])):
            mine = r.own[u % r.own.shape[0], pl.ds(block * shard, shard), :]
            r.g[u, place] = (mine + r.g[u, place].astype(F32)).astype(BF)
        stage_a(u, ORDER[u]).start()

    def start_b(u):
        order = ORDER[u]
        stage_a(u, order).wait()
        kept = pl.ds(route[order][0] * 8, 8)
        r.g[u, kept] = r.g[u, kept] + r.g_a[u]
        stage_b(u, order).start()

    def start_c(u):
        order = ORDER[u]
        stage_b(u, order).wait()
        kept = pl.ds(route[order][0] * 8 + route[order][1] * 4, 4)
        r.g[u, kept] = r.g[u, kept] + r.g_b[u]
        for step in range(1, 4):
            stage_c(u, order, step).start()

    def finish(u):
        order = ORDER[u]
        first, second, third, _, _ = route[order]
        acc = r.g[u, first * 8 + second * 4 + third].astype(F32)
        for step in range(1, 4):
            stage_c(u, order, step).wait()
            acc += r.g_c[u, step - 1].astype(F32)
        return acc

    def vec_copy(k, stage, src, device):
        return pltpu.make_async_remote_copy(
            src_ref=src, dst_ref=r.v_in.at[k, stage], send_sem=r.v_send.at[k, stage],
            recv_sem=r.v_recv.at[k, stage], device_id=device, device_id_type=MESH)

    def vec_core(k):
        return vec_copy(k, 0, r.v_out.at[k], core)

    def vec_side(k, stage):
        return vec_copy(k, stage, r.v_sum.at[k, stage - 1], (x_side, y_side)[stage - 1])

    def vec_z(k, step):
        return vec_copy(k, 2 + step, r.v_sum.at[k, 2], z_side[step - 1])

    def vec_next(k, stage):
        if stage == 0:
            vec_core(k).wait()
            r.v_sum[k, 0] = r.v_own[k] + r.v_in[k, 0]
            vec_side(k, 1).start()
        elif stage == 1:
            vec_side(k, 1).wait()
            r.v_sum[k, 1] = r.v_sum[k, 0] + r.v_in[k, 1]
            vec_side(k, 2).start()
        elif stage == 2:
            vec_side(k, 2).wait()
            r.v_sum[k, 2] = r.v_sum[k, 1] + r.v_in[k, 2]
            for step in range(1, nz):
                vec_z(k, step).start()
        else:
            for step in range(1, nz):
                vec_z(k, step).wait()
            terms = [r.v_sum[k, 2]] + [r.v_in[k, 2 + step] for step in range(1, nz)]
            acc = jnp.zeros(terms[0].shape, F32)
            for zz in range(nz):
                came = lax.rem(z - zz + nz, nz)
                term = terms[0]
                for step in range(1, nz):
                    term = jnp.where(came == step, terms[step], term)
                acc = acc + term
            if k == 0:
                for j, ref in enumerate((r.bout_o, r.gain1_o, r.shift1_o, r.bdown_o, r.gain2_o, r.shift2_o)):
                    for part in range(2):
                        ref[:, part * BLOCK:(part + 1) * BLOCK] = acc[2 * j + part:2 * j + part + 1]
                for c in range(chunks):
                    r.bup_o[:, c * BLOCK:(c + 1) * BLOCK] = acc[12 + c:13 + c]
            else:
                r.bq_o[...] = acc[0:1]
                r.bv_o[...] = acc[1:2]

    def down_grad(j):
        return dot_nn(r.dT[...], r.active[j].reshape(items * lanes, BLOCK))

    def active_grad(j):
        r.work[j % 2] = dot_nt(r.dlow[...], r.wd[j])

    def upper_grad(j):
        for i in range(items):
            rows = pl.ds(i * rows_pad, rows_pad)
            r.upg[j % 3, i, pl.ds(0, rows_pad), :] = (r.work[j % 2, rows, :] * r.slope[j, rows, :].astype(F32)).astype(BF)

    def up_grad(j):
        return dot_nn(r.hT[...], r.upg[j % 3].reshape(items * lanes, BLOCK))

    def hidden_grad(j):
        r.gp[...] += dot_nt(r.upg[j % 3][:, :rows_pad].reshape(total, BLOCK), r.wu[j])

    def turn(i):
        rows = pl.ds(i * rows_pad, rows_pad)
        r.hT[pl.ds(0, width), pl.ds(i * lanes, lanes)] = transposed(r.hlow[rows, :].astype(F32))

    def turn_input(i):
        rows = pl.ds(i * rows_pad, rows_pad)
        r.xT[pl.ds(0, width), pl.ds(i * lanes, lanes)] = transposed(r.x_v[rows, :].astype(F32))

    def turn_keys(n):
        r.tra[n, 1] = transposed(r.keys[n].astype(F32) * 0.125)

    for c in range(chunks):
        start_core(c, down_grad(chunks + c))
    for c in range(chunks):
        hold(c, down_grad(c))
        if c < items:
            turn(c)
    r.out_v[...] = r.acc[pl.ds(0, items * length), :].astype(BF)
    out_copy = pltpu.make_async_copy(r.out_v, r.out_h, r.out_sem.at[0])
    out_copy.start()
    order = list(range(chunks, 2 * chunks)) + list(range(chunks))
    active_grad(order[0])
    for c in range(chunks):
        start_a(c)
    for k, j in enumerate(order):
        if k + 1 < 2 * chunks:
            active_grad(order[k + 1])
        upper_grad(j)
        up = up_grad(j)
        c = j % chunks
        if j >= chunks:
            start_core(chunks + c, up)
            r.v_out[0, pl.ds(12 + c, 1), :] = up[width:width + 1]
        else:
            hold(chunks + c, up[:width])
            r.v_own[0, pl.ds(12 + c, 1), :] = up[width:width + 1]
        hidden_grad(j)
        if k < 2 * items:
            turn_keys(k)
        else:
            turn_input(k - 2 * items)
        if j < chunks:
            start_a(chunks + c)
    turn_input(2)
    for u in range(3):
        start_b(u)

    bout, gain1, shift1 = [], [], []

    def first_back(i):
        rows = pl.ds(i * rows_pad, rows_pad)
        hidden = r.gp[rows, :]
        normed = r.n1[rows, :]
        inverse = r.inv1[rows, :][:, :1]
        g = hidden * r.gain_one[...]
        grad = inverse * (g - mean(g) - normed * mean(g * normed))
        r.gp[rows, :] = grad
        r.olow[i, pl.ds(0, rows_pad), :] = grad.astype(BF)
        r.oT[:, pl.ds(i * lanes, lanes)] = transposed(grad)
        bout.append(column_sum(grad))
        gain1.append(column_sum(hidden * normed))
        shift1.append(column_sum(hidden))

    for i in range(items):
        first_back(i)
    for k, v in enumerate((bout, gain1, shift1, bdown, gain2, shift2)):
        v = sum(v[1:], v[0])
        for part in range(2):
            piece = v[:, part * BLOCK:(part + 1) * BLOCK]
            r.v_out[0, pl.ds(2 * k + part, 1), :] = piece
            r.v_own[0, pl.ds(2 * k + part, 1), :] = piece
    vec_core(0).start()

    start_core(8, dot_nt(r.oT[...], r.ctxT[1]))
    for n in [*range(items, 2 * items), *range(items)]:
        r.cgT[n] = dot_nt(r.wo[n // items], r.olow[n % items]).astype(BF)
    hold(8, dot_nt(r.oT[...], r.ctxT[0]))

    def probs_grad(n):
        for h in range(4):
            r.score[(n % 2) * 4 + h] = dot_nn(r.values[n, :, pair_of(h)] * half[h % 2], r.cgT[n, pair_of(h), :])

    def store_grad(n, k, h, value):
        r.gT[n // items, pl.ds(k * 256 + h * 64, 64), pl.ds((n % items) * lanes, lanes)] = value.astype(BF)

    def value_grad(n):
        for h in range(4):
            store_grad(n, 2, h, dot_nt(r.cgT[n, head_of(h), :], r.probs[n * 4 + h]))

    def score_grad(n):
        for h in range(4):
            pg = r.score[(n % 2) * 4 + h]
            p = r.probs[n * 4 + h, pl.ds(0, rows_pad), :].astype(F32)
            inner = jnp.sum(p * pg, axis=0, keepdims=True)
            r.dscore[(n % 2) * 4 + h, pl.ds(0, rows_pad), :] = (p * (pg - inner)).astype(BF)

    def query_key_grad(n):
        for h in range(4):
            ds = r.dscore[(n % 2) * 4 + h]
            store_grad(n, 0, h, dot_nn(r.tra[n, 1, head_of(h), :], ds))
            store_grad(n, 1, h, dot_nt(r.tra[n, 0, head_of(h), :], ds))

    def projection_grad(slot, k):
        return dot_nt(r.xT[...], r.gT[slot, pl.ds(k * 256, 256), :])

    after = (
        lambda: (start_a(8), vec_next(0, 0)),
        lambda: start_b(3),
        lambda: (start_c(0), start_c(1), start_c(2), vec_next(0, 1)),
        lambda: (start_b(4), start_b(5)),
        lambda: (start_b(6), start_c(3)),
        lambda: (start_b(7), start_c(4), vec_next(0, 2)))
    for k in range(2 * items):
        n = (k + items) % (2 * items)
        probs_grad(n)
        value_grad(n)
        score_grad(n)
        query_key_grad(n)
        if k == items - 1:
            for part in range(3):
                grad = projection_grad(1, part)
                start_core(9 + part, grad)
                if part != 1:
                    r.v_out[1, pl.ds(part // 2, 1), :] = grad[width:width + 1]
            vec_core(1).start()
        after[k]()
    for part in range(3):
        grad = projection_grad(0, part)
        hold(9 + part, grad[:width])
        if part != 1:
            r.v_own[1, pl.ds(part // 2, 1), :] = grad[width:width + 1]
        start_a(9 + part)
    vec_next(1, 0)

    for i in range(items):
        acc = None
        for slot in range(2):
            for k in range(3):
                term = dot_nn(r.wqkv[slot, k], r.gT[slot, pl.ds(k * 256, 256), pl.ds(i * lanes, lanes)])
                acc = term if acc is None else acc + term
        r.ig_v[pl.ds(i * length, length), :] = acc.T[:length] + r.gp[pl.ds(i * rows_pad, length), :]
    grad_copy = pltpu.make_async_copy(r.ig_v, r.ig_h, r.out_sem.at[1])
    grad_copy.start()
    start_b(8)
    start_c(5)
    start_c(6)
    start_c(7)
    for k in range(3):
        start_b(9 + k)
    vec_next(1, 1)
    start_c(8)
    vec_next(0, 3)
    for c in range(chunks):
        r.gd_o[:, c * BLOCK:(c + 1) * BLOCK] = finish(c)
        r.gu_o[:, c * BLOCK:(c + 1) * BLOCK] = finish(chunks + c)
    for k in range(3):
        start_c(9 + k)
    vec_next(1, 2)
    r.go_o[...] = finish(8)
    r.gq_o[...] = finish(9)
    r.gk_o[...] = finish(10)
    r.gv_o[...] = finish(11)
    vec_next(1, 3)

    for s in remote:
        s.wait_send()
    for u in range(UNITS):
        to_core(u).wait_send()
    out_copy.wait()
    grad_copy.wait()


def hand_over(count, *refs):
    held, sems = refs[2 * count:3 * count], refs[-1]
    into = [pltpu.make_async_copy(refs[k], held[k], sems.at[0, k]) for k in range(count)]
    out = [pltpu.make_async_copy(held[k], refs[count + k], sems.at[1, k]) for k in range(count)]
    for c in into:
        c.start()
    for c, d in zip(into, out, strict=True):
        c.wait()
        d.start()
    for d in out:
        d.wait()


def layer_by_items(
    inputs, region_counts, w_query, b_query, w_key, w_value, b_value, w_out, b_out, gain_one, shift_one,
    w_up, b_up, w_down, b_down, gain_two, shift_two, cotangent,
):
    total_rows, width = inputs.shape
    item_count = region_counts.shape[0]
    length = total_rows // item_count
    items = item_count // 2
    rows_pad = -(-length // ITEM_PAD) * ITEM_PAD
    lanes = -(-length // 128) * 128
    dp_size = lax.axis_size("dp")
    nz = dp_size // 4
    shard = width // dp_size
    total = items * rows_pad
    chunks = w_up.shape[1] // BLOCK
    own_rows = items * length

    two_chunks = 2 * chunks
    hd = w_query.shape[1]
    inner = [
        ("x_raw", (total_rows, width), BF), ("x_v", (total, width), BF),
        ("cot_raw", (total_rows - own_rows // 8 * 8 + 16, width), F32), ("cot", (total, width), F32),
        ("bias_q", (2, 1, BLOCK), F32), ("bias_v", (2, 1, BLOCK), F32), ("bias_u", (2, 1, chunks * BLOCK), F32),
        ("b_out", (1, width), F32), ("gain_one", (1, width), F32), ("shift_one", (1, width), F32),
        ("b_down", (1, width), F32), ("gain_two", (1, width), F32), ("shift_two", (1, width), F32),
        ("wqkv", (2, 3, width, hd), BF), ("wo", (2, hd, width), BF),
        ("wu", (two_chunks, width, BLOCK), BF), ("wd", (two_chunks, BLOCK, width), BF),
        ("xT", (width + 16, items * lanes), BF), ("hT", (width + 16, items * lanes), BF),
        ("dT", (width, items * lanes), BF), ("oT", (width, items * lanes), BF),
        ("keys", (2 * items, rows_pad, hd), BF), ("values", (2 * items, rows_pad, hd), BF),
        ("tra", (2 * items, 3, hd, lanes), BF), ("score", (8, rows_pad, lanes), F32),
        ("probs", (8 * items, lanes, lanes), BF), ("ctxT", (2, hd, items * lanes), BF),
        ("ctx", (2, total, hd), BF), ("n1", (total, width), F32), ("inv1", (total, 128), F32),
        ("hlow", (total, width), BF), ("slope", (two_chunks, total, BLOCK), BF),
        ("active", (two_chunks, items, lanes, BLOCK), BF), ("acc", (total, width), F32),
        ("work", (3, total, BLOCK), F32), ("own", (4, width, BLOCK), F32),
        ("out_v", (own_rows, width), BF), ("ig_v", (own_rows, width), F32), ("gp", (total, width), F32),
        ("dlow", (total, width), BF), ("upg", (3, items, lanes, BLOCK), BF), ("olow", (items, lanes, width), BF),
        ("cgT", (2 * items, hd, lanes), BF), ("dscore", (8, lanes, lanes), BF), ("gT", (2, 3 * hd, items * lanes), BF),
        ("g_out", (UNITS, 16, shard, BLOCK), BF), ("g", (UNITS, 16, shard, BLOCK), BF),
        ("g_a", (UNITS, 8, shard, BLOCK), BF), ("g_b", (UNITS, 4, shard, BLOCK), BF), ("g_c", (UNITS, 3, shard, BLOCK), BF),
        ("v_out", (2, 16, BLOCK), F32), ("v_own", (2, 16, BLOCK), F32),
        ("v_in", (2, 2 + nz, 16, BLOCK), F32), ("v_sum", (2, 3, 16, BLOCK), F32),
    ]
    n_weights = 8 + chunks
    sems = [
        ("in_sem", (16 + chunks,)), ("w_send", (n_weights,)), ("w_recv", (n_weights,)), ("out_sem", (2,)),
        ("core_send", (UNITS,)), ("core_recv", (UNITS,)), ("a_send", (UNITS,)), ("a_recv", (UNITS,)),
        ("b_send", (UNITS,)), ("b_recv", (UNITS,)), ("c_send", (UNITS, 3)), ("c_recv", (UNITS, 3)),
        ("v_send", (2, 2 + nz)), ("v_recv", (2, 2 + nz)),
    ]
    operands = [
        ("counts", region_counts), ("x_h", inputs), ("cot_h", cotangent), ("wq_h", w_query), ("wk_h", w_key),
        ("wv_h", w_value), ("wo_h", w_out), ("wu_h", w_up), ("wd_h", w_down.reshape(chunks, BLOCK, width)),
        ("b_query_h", b_query[None]), ("b_value_h", b_value[None]), ("b_up_h", b_up[None]), ("b_out_h", b_out[None]),
        ("gain_one_h", gain_one[None]), ("shift_one_h", shift_one[None]), ("b_down_h", b_down[None]),
        ("gain_two_h", gain_two[None]), ("shift_two_h", shift_two[None]),
    ]
    hidden = chunks * BLOCK
    results = [
        ("out_h", (own_rows, width), BF, pl.ANY), ("ig_h", (own_rows, width), F32, pl.ANY),
        ("gq_o", (shard, hd), F32, pltpu.VMEM), ("bq_o", (1, hd), F32, pltpu.VMEM),
        ("gk_o", (shard, hd), F32, pltpu.VMEM), ("gv_o", (shard, hd), F32, pltpu.VMEM),
        ("bv_o", (1, hd), F32, pltpu.VMEM), ("go_o", (shard, hd), F32, pltpu.VMEM),
        ("bout_o", (1, width), F32, pltpu.VMEM), ("gain1_o", (1, width), F32, pltpu.VMEM),
        ("shift1_o", (1, width), F32, pltpu.VMEM), ("gu_o", (shard, hidden), F32, pltpu.VMEM),
        ("bup_o", (1, hidden), F32, pltpu.VMEM), ("gd_o", (shard, hidden), F32, pltpu.VMEM),
        ("bdown_o", (1, width), F32, pltpu.VMEM), ("gain2_o", (1, width), F32, pltpu.VMEM),
        ("shift2_o", (1, width), F32, pltpu.VMEM),
    ]
    names = [n for n, _ in operands] + [n for n, *_ in results] + [n for n, *_ in inner] + [n for n, _ in sems]
    smem = pl.BlockSpec(memory_space=pltpu.SMEM)
    shapes = [jax.ShapeDtypeStruct(s, d) for _, s, d, _ in results]
    made = pl.pallas_call(
        functools.partial(layer_kernel, (items, length, rows_pad, lanes, nz, shard), names),
        out_shape=shapes,
        in_specs=[smem] + [pl.BlockSpec(memory_space=pl.ANY)] * (len(operands) - 1),
        out_specs=[pl.BlockSpec(memory_space=m) for *_, m in results],
        scratch_shapes=[pltpu.VMEM(s, d) for _, s, d in inner] + [pltpu.SemaphoreType.DMA(s) for _, s in sems],
        compiler_params=pltpu.CompilerParams(
            collective_id=0, has_side_effects=True, vmem_limit_bytes=63 * 2**20),
        name="layer",
    )(*[v for _, v in operands])
    count = len(shapes)
    made = pl.pallas_call(
        functools.partial(hand_over, count),
        out_shape=shapes,
        in_specs=[pl.BlockSpec(memory_space=pl.ANY)] * count,
        out_specs=[pl.BlockSpec(memory_space=pl.ANY)] * count,
        scratch_shapes=[pltpu.VMEM(s.shape, s.dtype) for s in shapes] + [pltpu.SemaphoreType.DMA((2, count))],
        name="hand_over",
    )(*made)
    made = [v.reshape(-1) if v.shape[0] == 1 else v for v in made]
    made[7], made[13] = made[7].T, made[13].T
    return tuple(made)


def solution(mesh):
    placed = (
        P("dp", None),
        P("dp"),
        P(None, "mp"),
        P("mp"),
        P(None, "mp"),
        P(None, "mp"),
        P("mp"),
        P("mp", None),
        P(),
        P(),
        P(),
        P(None, "mp"),
        P("mp"),
        P("mp", None),
        P(),
        P(),
        P(),
        P("dp", None),
    )
    dp_size, mp_size = mesh.shape["dp"], mesh.shape["mp"]

    def body(*args):
        width, hidden = args[0].shape[1], args[11].shape[1]
        whole_items = mp_size == 2 and args[1].shape[0] % 2 == 0
        even_shards = dp_size == 16 and width % (16 * dp_size) == 0
        blocks = args[2].shape[1] == BLOCK and width == 2 * BLOCK and hidden == 4 * BLOCK
        fits = args[0].shape[0] // args[1].shape[0] <= 256
        if whole_items and even_shards and blocks and fits:
            return layer_by_items(*args)
        return per_device(*args)

    return jax.shard_map(
        body,
        mesh=mesh,
        in_specs=placed,
        out_specs=(
            P(("dp", "mp"), None),
            P(("dp", "mp"), None),
            P("dp", "mp"),
            P("mp"),
            P("dp", "mp"),
            P("dp", "mp"),
            P("mp"),
            P("mp", "dp"),
            P(),
            P(),
            P(),
            P("dp", "mp"),
            P("mp"),
            P("mp", "dp"),
            P(),
            P(),
            P(),
        ),
        check_vma=False,
    )
```

```python
import functools
import types

import jax
import jax.numpy as jnp
from jax import lax
from jax.experimental import pallas as pl
from jax.experimental.pallas import tpu as pltpu
from jax.sharding import PartitionSpec as P

HEAD_DIM = 64
TEXT = 128


def layer_stats(pre_rows):
    row_mean = jnp.mean(pre_rows, axis=-1, keepdims=True)
    centred = pre_rows - row_mean
    inverse = lax.rsqrt(jnp.mean(centred * centred, axis=-1, keepdims=True) + 1e-12)
    return (centred * inverse, inverse)


def norm_back(grad_rows, normed, inverse, gain_vec):
    scaled = grad_rows * gain_vec
    return inverse * (
        scaled
        - jnp.mean(scaled, axis=-1, keepdims=True)
        - normed * jnp.mean(scaled * normed, axis=-1, keepdims=True)
    )


def gelu_slope(upper_part):
    return (
        0.5 * (1.0 + lax.erf(upper_part * 0.7071067811865476))
        + upper_part * jnp.exp(-0.5 * upper_part * upper_part) * 0.3989422804014327
    )


def contract_rows(first_op, second_op):
    return lax.dot_general(
        first_op, second_op, (((0,), (0,)), ((), ())), preferred_element_type=jnp.float32
    )


def times_transposed(first_op, second_op):
    return lax.dot_general(
        first_op, second_op, (((1,), (1,)), ((), ())), preferred_element_type=jnp.float32
    )


def per_device(
    inputs,
    region_counts,
    w_query,
    b_query,
    w_key,
    w_value,
    b_value,
    w_out,
    b_out,
    gain_one,
    shift_one,
    w_up,
    b_up,
    w_down,
    b_down,
    gain_two,
    shift_two,
    cotangent,
):
    total_rows = inputs.shape[0]
    item_count = region_counts.shape[0]
    length = total_rows // item_count
    heads_here = w_query.shape[1] // HEAD_DIM
    score_scale = HEAD_DIM ** (-0.5)
    share_rows = total_rows // lax.axis_size("mp")
    row_start = lax.axis_index("mp") * share_rows

    def own_rows(full_rows):
        return lax.dynamic_slice_in_dim(full_rows, row_start, share_rows, 0)

    def split_heads(flat_rows):
        return flat_rows.reshape(item_count, length, heads_here, HEAD_DIM)

    position = jnp.arange(length)
    visible = (position[None, :] < TEXT) | (position[None, :] - TEXT < region_counts[:, None])
    key_mask = visible[:, None, None, :]
    queries = (jnp.dot(inputs, w_query, preferred_element_type=jnp.float32) + b_query).astype(
        jnp.bfloat16
    )
    key_rows = jnp.dot(inputs, w_key, preferred_element_type=jnp.float32).astype(jnp.bfloat16)
    value_rows = (jnp.dot(inputs, w_value, preferred_element_type=jnp.float32) + b_value).astype(
        jnp.bfloat16
    )
    query_heads = split_heads(queries)
    key_heads = split_heads(key_rows)
    value_heads = split_heads(value_rows)

    def masked_scores():
        raw_scores = (
            jnp.einsum(
                "ishd,ithd->ihst", query_heads, key_heads, preferred_element_type=jnp.float32
            )
            * score_scale
        )
        return jnp.where(key_mask, raw_scores, -1000000000.0)

    scores = masked_scores()
    row_top = jnp.max(scores, axis=-1, keepdims=True)
    exponent = jnp.exp(scores - row_top)
    row_total = jnp.sum(exponent, axis=-1, keepdims=True)
    probs = exponent / row_total
    log_total = row_top + jnp.log(row_total)
    context = jnp.einsum(
        "ihst,ithd->ishd",
        probs.astype(jnp.bfloat16),
        value_heads,
        preferred_element_type=jnp.float32,
    )
    context = context.reshape(total_rows, heads_here * HEAD_DIM).astype(jnp.bfloat16)
    partial_attn = jnp.dot(context, w_out, preferred_element_type=jnp.float32)
    attended = lax.psum(partial_attn, "mp")
    normed_one, inverse_one = layer_stats(attended + b_out + inputs.astype(jnp.float32))
    hidden_one = normed_one * gain_one + shift_one
    hidden_low = hidden_one.astype(jnp.bfloat16)
    upper_part = jnp.dot(hidden_low, w_up, preferred_element_type=jnp.float32) + b_up
    active = jax.nn.gelu(upper_part, approximate=False).astype(jnp.bfloat16)
    partial_ffn = jnp.dot(active, w_down, preferred_element_type=jnp.float32)
    lowered = lax.psum(partial_ffn, "mp")
    normed_two, inverse_two = layer_stats(lowered + b_down + hidden_one)
    output = own_rows(normed_two * gain_two + shift_two).astype(jnp.bfloat16)
    grad_pre_two = norm_back(cotangent, normed_two, inverse_two, gain_two)
    down_low = grad_pre_two.astype(jnp.bfloat16)
    grad_output = own_rows(cotangent)
    normed_two_own = own_rows(normed_two)
    grad_two_own = own_rows(grad_pre_two)
    grad_gain_two = jnp.sum(grad_output * normed_two_own, axis=0)
    grad_shift_two = jnp.sum(grad_output, axis=0)
    grad_b_down = jnp.sum(grad_two_own, axis=0)
    grad_w_down = contract_rows(active, down_low)
    active_grad = times_transposed(down_low, w_down)
    upper_grad = (active_grad * gelu_slope(upper_part)).astype(jnp.bfloat16)
    grad_b_up = jnp.sum(upper_grad.astype(jnp.float32), axis=0)
    grad_w_up = contract_rows(hidden_low, upper_grad)
    partial_hidden = times_transposed(upper_grad, w_up)
    hidden_grad = lax.psum(partial_hidden, "mp") + grad_pre_two
    grad_pre_one = norm_back(hidden_grad, normed_one, inverse_one, gain_one)
    out_low = grad_pre_one.astype(jnp.bfloat16)
    hidden_grad_own = own_rows(hidden_grad)
    normed_one_own = own_rows(normed_one)
    grad_one_own = own_rows(grad_pre_one)
    grad_gain_one = jnp.sum(hidden_grad_own * normed_one_own, axis=0)
    grad_shift_one = jnp.sum(hidden_grad_own, axis=0)
    grad_b_out = jnp.sum(grad_one_own, axis=0)
    grad_w_out = contract_rows(context, out_low)
    context_grad = split_heads(times_transposed(out_low, w_out).astype(jnp.bfloat16))
    probs_again = jnp.exp(masked_scores() - log_total)
    prob_grad = jnp.einsum(
        "ishd,ithd->ihst", context_grad, value_heads, preferred_element_type=jnp.float32
    )
    row_inner = jnp.sum(probs_again * prob_grad, axis=-1, keepdims=True)
    score_grad = (probs_again * (prob_grad - row_inner)).astype(jnp.bfloat16)
    query_grad = (
        (
            jnp.einsum("ihst,ithd->ishd", score_grad, key_heads, preferred_element_type=jnp.float32)
            * score_scale
        )
        .astype(jnp.bfloat16)
        .reshape(total_rows, heads_here * HEAD_DIM)
    )
    key_grad = (
        (
            jnp.einsum(
                "ihst,ishd->ithd", score_grad, query_heads, preferred_element_type=jnp.float32
            )
            * score_scale
        )
        .astype(jnp.bfloat16)
        .reshape(total_rows, heads_here * HEAD_DIM)
    )
    value_grad = jnp.einsum(
        "ihst,ishd->ithd",
        probs_again.astype(jnp.bfloat16),
        context_grad,
        preferred_element_type=jnp.float32,
    ).astype(jnp.bfloat16)
    value_grad = value_grad.reshape(total_rows, heads_here * HEAD_DIM)
    grad_b_query = jnp.sum(query_grad.astype(jnp.float32), axis=0)
    grad_b_value = jnp.sum(value_grad.astype(jnp.float32), axis=0)
    grad_w_query = contract_rows(inputs, query_grad)
    grad_w_key = contract_rows(inputs, key_grad)
    grad_w_value = contract_rows(inputs, value_grad)
    partial_input = (
        times_transposed(query_grad, w_query)
        + times_transposed(key_grad, w_key)
        + times_transposed(value_grad, w_value)
    )
    input_grad = own_rows(
        lax.psum(partial_input.astype(jnp.bfloat16), "mp").astype(jnp.float32) + grad_pre_one
    )
    bias_sums = lax.psum((grad_b_query, grad_b_value, grad_b_up), "dp")
    norm_sums = lax.psum(
        (grad_b_out, grad_gain_one, grad_shift_one, grad_b_down, grad_gain_two, grad_shift_two),
        ("dp", "mp"),
    )
    weight_sums = (
        lax.psum_scatter(
            grad_w_query.astype(jnp.bfloat16), "dp", scatter_dimension=0, tiled=True
        ).astype(jnp.float32),
        lax.psum_scatter(
            grad_w_key.astype(jnp.bfloat16), "dp", scatter_dimension=0, tiled=True
        ).astype(jnp.float32),
        lax.psum_scatter(
            grad_w_value.astype(jnp.bfloat16), "dp", scatter_dimension=0, tiled=True
        ).astype(jnp.float32),
        lax.psum_scatter(
            grad_w_out.astype(jnp.bfloat16), "dp", scatter_dimension=1, tiled=True
        ).astype(jnp.float32),
        lax.psum_scatter(
            grad_w_up.astype(jnp.bfloat16), "dp", scatter_dimension=0, tiled=True
        ).astype(jnp.float32),
        lax.psum_scatter(
            grad_w_down.astype(jnp.bfloat16), "dp", scatter_dimension=1, tiled=True
        ).astype(jnp.float32),
    )
    return (
        output,
        input_grad,
        weight_sums[0],
        bias_sums[0],
        weight_sums[1],
        weight_sums[2],
        bias_sums[1],
        weight_sums[3],
        norm_sums[0],
        norm_sums[1],
        norm_sums[2],
        weight_sums[4],
        bias_sums[2],
        weight_sums[5],
        norm_sums[3],
        norm_sums[4],
        norm_sums[5],
    )


ITEM_PAD = 16
MESH = pl.DeviceIdType.MESH
BF = jnp.bfloat16
F32 = jnp.float32
BLOCK = 256
UNITS = 12
X_FIRST, Y_FIRST, Z_FIRST = 0, 1, 2
ORDER = (2, 0, 1, 2, 0, 1, 0, 1, 0, 1, 0, 1)


def dot_nn(a, b):
    return lax.dot_general(a, b, (((1,), (0,)), ((), ())), preferred_element_type=F32)


def dot_nt(a, b):
    return lax.dot_general(a, b, (((1,), (1,)), ((), ())), preferred_element_type=F32)


def layer_kernel(dims, names, *refs):
    r = types.SimpleNamespace(**dict(zip(names, refs, strict=True)))
    items, length, rows_pad, lanes, nz, shard = dims
    total = items * rows_pad
    chunks = r.wu_h.shape[1] // BLOCK
    width = r.x_h.shape[1]
    dp, mp = lax.axis_index("dp"), lax.axis_index("mp")
    z, y, x = dp // 4, (dp // 2) % 2, dp % 2

    def at(z_, y_, x_):
        return z_ * 4 + y_ * 2 + x_

    core = (dp, 1 - mp)
    x_side = (at(z, y, 1 - x), mp)
    y_side = (at(z, 1 - y, x), mp)
    z_side = [(at((z + step) % nz, y, x), mp) for step in range(1, nz)]
    low_side = (at(z + 1 - 2 * (z % 2), y, x), mp)
    high_side = z_side[1]
    plane_side = [(at(z, (y + step // 2) % 2, (x + step) % 2), mp) for step in range(1, 4)]

    local = []

    def bring(src, dst):
        copy = pltpu.make_async_copy(src, dst, r.in_sem.at[len(local)])
        copy.start()
        local.append(copy)
        return copy

    c_x = bring(r.x_h, r.x_raw)
    c_w = [bring(src, r.wqkv.at[0, k]) for k, src in enumerate((r.wq_h, r.wk_h, r.wv_h))]
    c_p = [bring(r.b_query_h, r.bias_q.at[0]), bring(r.b_value_h, r.bias_v.at[0]), bring(r.b_up_h, r.bias_u.at[0])]

    barrier = pltpu.get_barrier_semaphore()
    near = [core] + plane_side + z_side
    for device in near:
        pl.semaphore_signal(barrier, inc=1, device_id=device, device_id_type=MESH)
    vectors = (
        (r.b_out_h, r.b_out), (r.gain_one_h, r.gain_one), (r.shift_one_h, r.shift_one),
        (r.b_down_h, r.b_down), (r.gain_two_h, r.gain_two), (r.shift_two_h, r.shift_two))
    c_vec = [bring(src, dst) for src, dst in vectors]
    c_wo = bring(r.wo_h, r.wo.at[0])
    c_wu = [bring(r.wu_h.at[:, pl.ds(c * BLOCK, BLOCK)], r.wu.at[c]) for c in range(chunks)]
    c_wd = bring(r.wd_h, r.wd.at[pl.ds(0, chunks)])
    full_rows = r.x_h.shape[0]
    base = items * length // 8 * 8
    cot_count = full_rows - base
    c_cot = bring(r.cot_h.at[pl.ds(pl.multiple_of(mp * base, 8), cot_count)], r.cot_raw.at[pl.ds(0, cot_count)])

    pad_rows = lanes - rows_pad

    def transposed(block):
        full = jnp.concatenate([block, jnp.zeros((pad_rows, block.shape[1]), F32)], axis=0)
        return full.T.astype(BF)

    def rows_of(i):
        return pl.ds(pl.multiple_of(i * rows_pad, 16), rows_pad)

    def lanes_of(i):
        return pl.ds(pl.multiple_of(i * lanes, lanes), lanes)

    def greet():
        pl.semaphore_wait(barrier, len(near))

    def clear(n, carry):
        r.probs[n, pl.ds(rows_pad, pad_rows), :] = jnp.zeros((pad_rows, lanes), BF)
        return carry

    lax.fori_loop(0, r.probs.shape[0], clear, 0)
    zero_block = jnp.zeros((pad_rows, BLOCK), BF)
    for i in range(items):
        r.olow[i, pl.ds(rows_pad, pad_rows), :] = jnp.zeros((pad_rows, width), BF)
        for j in range(r.upg.shape[0]):
            r.upg[j, i, pl.ds(rows_pad, pad_rows), :] = zero_block
        for j in range(2 * chunks):
            r.active[j, i, pl.ds(rows_pad, pad_rows), :] = zero_block
    for k in range(r.dscore.shape[0]):
        r.dscore[k, pl.ds(rows_pad, pad_rows), :] = jnp.zeros((pad_rows, lanes), BF)
    one_row = jnp.where(lax.broadcasted_iota(jnp.int32, (16, items * lanes), 0) == 0, 1.0, 0.0).astype(BF)
    r.xT[pl.ds(width, 16), :] = one_row
    r.hT[pl.ds(width, 16), :] = one_row
    cot_rows = r.cot_raw.shape[0]
    r.cot_raw[pl.ds(cot_count, cot_rows - cot_count), :] = jnp.zeros((cot_rows - cot_count, width), F32)

    c_x.wait()
    down_ = lax.broadcasted_iota(jnp.int32, (rows_pad, 256), 0)
    across = lax.broadcasted_iota(jnp.int32, (rows_pad, 256), 1)
    for i in range(items):
        block = None
        for m in range(2):
            start = (m * items + i) * length
            window = start // 16 * 16
            count = min(256, full_rows - window)
            shift = jnp.where(mp == m, start - window, 2 * 256)
            pick = jnp.where((across == down_ + shift) & (down_ < length), 1.0, 0.0).astype(BF)
            term = dot_nn(pick[:, :count], r.x_raw[pl.ds(window, count), :])
            block = term if block is None else block + term
        r.x_v[rows_of(i), :] = block.astype(BF)

    greet()

    remote = []

    def send_weight(src, dst):
        k = len(remote)
        copy = pltpu.make_async_remote_copy(
            src_ref=src, dst_ref=dst, send_sem=r.w_send.at[k], recv_sem=r.w_recv.at[k],
            device_id=core, device_id_type=MESH)
        copy.start()
        remote.append(copy)
        return copy

    s_w = [send_weight(src, r.wqkv.at[1, k]) for k, src in enumerate((r.wq_h, r.wk_h, r.wv_h))]
    s_w += [send_weight(src, dst.at[1]) for src, dst in (
        (r.b_query_h, r.bias_q), (r.b_value_h, r.bias_v), (r.b_up_h, r.bias_u))]
    s_wo = send_weight(r.wo_h, r.wo.at[1])
    s_wu = [send_weight(r.wu_h.at[:, pl.ds(c * BLOCK, BLOCK)], r.wu.at[chunks + c]) for c in range(chunks)]
    s_wd = send_weight(r.wd_h, r.wd.at[pl.ds(chunks, chunks)])

    def project(slot, k):
        r.work[k] = dot_nn(r.x_v[...], r.wqkv[slot, k])

    def keep(slot, k):
        for i in range(items):
            block = r.work[k, pl.ds(i * rows_pad, rows_pad), :]
            n = slot * items + i
            if k == 0:
                r.tra[n, 0] = transposed((block + r.bias_q[slot]) * 0.125)
            elif k == 1:
                r.keys[n] = block.astype(BF)
            else:
                block = block + r.bias_v[slot]
                r.values[n] = block.astype(BF)
                r.tra[n, 2] = transposed(block)

    for c in c_w + c_p:
        c.wait()
    for k in range(3):
        project(0, k)
    for k in range(3):
        keep(0, k)
    for c in s_w:
        c.wait_recv()
    for k in range(3):
        project(1, k)

    lane = lax.broadcasted_iota(jnp.int32, (1, 128), 1)
    half = [jnp.where(lane < 64, 1.0, 0.0).astype(BF), jnp.where(lane >= 64, 1.0, 0.0).astype(BF)]
    position = lax.broadcasted_iota(jnp.int32, (rows_pad, lanes), 0)

    def pair_of(h):
        return slice((h // 2) * 128, (h // 2) * 128 + 128)

    def head_of(h):
        return slice(h * 64, (h + 1) * 64)

    def scores_of(n):
        for h in range(4):
            r.score[(n % 2) * 4 + h] = dot_nn(r.keys[n, :, pair_of(h)] * half[h % 2], r.tra[n, 0, pair_of(h), :])

    def soften(n):
        mask = jnp.where(position < TEXT + r.counts[mp * items + n % items], 0.0, -1e9)
        for h in range(4):
            score = r.score[(n % 2) * 4 + h] + mask
            top = jnp.max(score, axis=0, keepdims=True)
            e = jnp.exp(score - top)
            p = e * (1.0 / jnp.sum(e, axis=0, keepdims=True))
            r.probs[n * 4 + h, pl.ds(0, rows_pad), :] = p.astype(BF)

    def contexts_of(n):
        parts = [dot_nn(r.tra[n, 2, head_of(h), :], r.probs[n * 4 + h]) for h in range(4)]
        context = jnp.concatenate(parts, axis=0)
        slot, i = n // items, n % items
        r.ctxT[slot, :, pl.ds(i * lanes, lanes)] = context.astype(BF)
        r.ctx[slot, pl.ds(i * rows_pad, rows_pad), :] = context.T[:rows_pad].astype(BF)

    scores_of(0)
    for n in range(2 * items):
        if n + 1 < 2 * items:
            if n + 1 == items:
                for k in range(3):
                    keep(1, k)
            scores_of(n + 1)
        soften(n)
        contexts_of(n)

    c_wo.wait()
    s_wo.wait_recv()
    for c in c_vec:
        c.wait()

    def attended(i):
        rows = pl.ds(i * rows_pad, rows_pad)
        r.acc[rows, :] = dot_nn(r.ctx[0, rows, :], r.wo[0]) + dot_nn(r.ctx[1, rows, :], r.wo[1])

    def first_norm(i):
        rows = pl.ds(i * rows_pad, rows_pad)
        pre = r.acc[rows, :] + r.b_out[...] + r.x_v[rows, :].astype(F32)
        centred = pre - jnp.mean(pre, axis=1, keepdims=True)
        inverse = lax.rsqrt(jnp.mean(centred * centred, axis=1, keepdims=True) + 1e-12)
        normed = centred * inverse
        r.n1[rows, :] = normed
        r.inv1[rows, :] = jnp.broadcast_to(inverse, (rows_pad, 128))
        r.hlow[rows, :] = (normed * r.gain_one[...] + r.shift_one[...]).astype(BF)

    for i in range(items):
        attended(i)
    for i in range(items):
        first_norm(i)

    for c in c_wu + [c_wd]:
        c.wait()
    for c in s_wu + [s_wd]:
        c.wait_recv()
    c_cot.wait()
    valid = lax.broadcasted_iota(jnp.int32, (rows_pad, 1), 0) < length

    def own_cotangent(i):
        at_ = [r.cot_raw[pl.ds(m * (items * length - base) + i * length, rows_pad), :] for m in range(2)]
        r.cot[pl.ds(i * rows_pad, rows_pad), :] = jnp.where(valid, jnp.where(mp == 0, at_[0], at_[1]), 0.0)

    def lift(j):
        slot, c = j // chunks, j % chunks
        r.work[j % 2] = dot_nn(r.hlow[...], r.wu[j]) + r.bias_u[slot, :, c * BLOCK:(c + 1) * BLOCK]

    def activate(j):
        for i in range(items):
            rows = pl.ds(i * rows_pad, rows_pad)
            u = r.work[j % 2, rows, :]
            phi = 0.5 + 0.5 * lax.erf(u * 0.7071067811865476)
            r.slope[j, rows, :] = (phi + u * (jnp.exp(-0.5 * u * u) * 0.3989422804014327)).astype(BF)
            r.active[j, i, pl.ds(0, rows_pad), :] = (u * phi).astype(BF)

    def lower(j):
        part = dot_nn(r.active[j][:, :rows_pad].reshape(total, BLOCK), r.wd[j])
        if j == 0:
            r.acc[...] = part
        else:
            r.acc[...] += part

    lift(0)
    for j in range(2 * chunks):
        if j > 0:
            lower(j - 1)
        if j + 1 < 2 * chunks:
            lift(j + 1)
        activate(j)
        if 2 <= j < 2 + items:
            own_cotangent(j - 2)
    lower(2 * chunks - 1)

    def mean(v):
        return jnp.mean(v, axis=1, keepdims=True)

    def column_sum(v):
        return jnp.sum(v, axis=0, keepdims=True)

    gain2, shift2, bdown = [], [], []

    def second_norm(i):
        rows = pl.ds(i * rows_pad, rows_pad)
        hidden = r.n1[rows, :] * r.gain_one[...] + r.shift_one[...]
        pre = r.acc[rows, :] + r.b_down[...] + hidden
        centred = pre - mean(pre)
        inverse = lax.rsqrt(mean(centred * centred) + 1e-12)
        normed = centred * inverse
        cot = r.cot[rows, :]
        g = cot * r.gain_two[...]
        grad = inverse * (g - mean(g) - normed * mean(g * normed))
        r.gp[rows, :] = grad
        r.dlow[rows, :] = grad.astype(BF)
        r.dT[:, pl.ds(i * lanes, lanes)] = transposed(grad)
        r.acc[pl.ds(i * length, rows_pad), :] = normed * r.gain_two[...] + r.shift_two[...]
        gain2.append(column_sum(cot * normed))
        shift2.append(column_sum(cot))
        bdown.append(column_sum(grad))

    for i in range(items):
        second_norm(i)

    def to_core(u):
        return pltpu.make_async_remote_copy(
            src_ref=r.g_out.at[u], dst_ref=r.g.at[u], send_sem=r.core_send.at[u],
            recv_sem=r.core_recv.at[u], device_id=core, device_id_type=MESH)

    route = (
        (x, y, z, x_side, y_side), (y, x, z, y_side, x_side), (z % 2, z // 2, y * 2 + x, low_side, high_side))

    def shard_order(order):
        if order == X_FIRST:
            return [at(c, b, a) for a in range(2) for b in range(2) for c in range(nz)]
        if order == Y_FIRST:
            return [at(c, a, b) for a in range(2) for b in range(2) for c in range(nz)]
        return [at(2 * b + a, c, d) for a in range(2) for b in range(2) for c in range(2) for d in range(2)]

    def stage_a(u, order):
        first, _, _, device, _ = route[order]
        return pltpu.make_async_remote_copy(
            src_ref=r.g.at[u, pl.ds((1 - first) * 8, 8)], dst_ref=r.g_a.at[u], send_sem=r.a_send.at[u],
            recv_sem=r.a_recv.at[u], device_id=device, device_id_type=MESH)

    def stage_b(u, order):
        first, second, _, _, device = route[order]
        return pltpu.make_async_remote_copy(
            src_ref=r.g.at[u, pl.ds(first * 8 + (1 - second) * 4, 4)], dst_ref=r.g_b.at[u], send_sem=r.b_send.at[u],
            recv_sem=r.b_recv.at[u], device_id=device, device_id_type=MESH)

    def stage_c(u, order, step):
        first, second, _, _, _ = route[order]
        if order in (X_FIRST, Y_FIRST):
            place, device = (z + step) % nz, z_side[step - 1]
        else:
            place, device = ((y + step // 2) % 2) * 2 + (x + step) % 2, plane_side[step - 1]
        return pltpu.make_async_remote_copy(
            src_ref=r.g.at[u, first * 8 + second * 4 + place], dst_ref=r.g_c.at[u, step - 1],
            send_sem=r.c_send.at[u, step - 1], recv_sem=r.c_recv.at[u, step - 1],
            device_id=device, device_id_type=MESH)

    def start_core(u, value):
        for place, block in enumerate(shard_order(ORDER[u])):
            r.g_out[u, place] = value[block * shard:(block + 1) * shard].astype(BF)
        to_core(u).start()

    def hold(u, value):
        r.own[u % r.own.shape[0]] = value

    def start_a(u):
        to_core(u).wait_recv()
        for place, block in enumerate(shard_order(ORDER[u])):
            mine = r.own[u % r.own.shape[0], pl.ds(block * shard, shard), :]
            r.g[u, place] = (mine + r.g[u, place].astype(F32)).astype(BF)
        stage_a(u, ORDER[u]).start()

    def start_b(u):
        order = ORDER[u]
        stage_a(u, order).wait_recv()
        kept = pl.ds(route[order][0] * 8, 8)
        r.g[u, kept] = r.g[u, kept] + r.g_a[u]
        stage_b(u, order).start()

    def start_c(u):
        order = ORDER[u]
        stage_b(u, order).wait_recv()
        kept = pl.ds(route[order][0] * 8 + route[order][1] * 4, 4)
        r.g[u, kept] = r.g[u, kept] + r.g_b[u]
        for step in range(1, 4):
            stage_c(u, order, step).start()

    def finish(u):
        order = ORDER[u]
        first, second, third, _, _ = route[order]
        acc = r.g[u, first * 8 + second * 4 + third].astype(F32)
        for step in range(1, 4):
            stage_c(u, order, step).wait_recv()
            acc += r.g_c[u, step - 1].astype(F32)
        return acc

    def vec_copy(k, stage, src, device):
        return pltpu.make_async_remote_copy(
            src_ref=src, dst_ref=r.v_in.at[k, stage], send_sem=r.v_send.at[k, stage],
            recv_sem=r.v_recv.at[k, stage], device_id=device, device_id_type=MESH)

    def vec_core(k):
        return vec_copy(k, 0, r.v_out.at[k], core)

    def vec_side(k, stage):
        return vec_copy(k, stage, r.v_sum.at[k, stage - 1], (x_side, y_side)[stage - 1])

    def vec_z(k, step):
        return vec_copy(k, 2 + step, r.v_sum.at[k, 2], z_side[step - 1])

    def vec_next(k, stage):
        if stage == 0:
            vec_core(k).wait_recv()
            r.v_sum[k, 0] = r.v_own[k] + r.v_in[k, 0]
            vec_side(k, 1).start()
        elif stage == 1:
            vec_side(k, 1).wait_recv()
            r.v_sum[k, 1] = r.v_sum[k, 0] + r.v_in[k, 1]
            vec_side(k, 2).start()
        elif stage == 2:
            vec_side(k, 2).wait_recv()
            r.v_sum[k, 2] = r.v_sum[k, 1] + r.v_in[k, 2]
            for step in range(1, nz):
                vec_z(k, step).start()
        else:
            for step in range(1, nz):
                vec_z(k, step).wait_recv()
            terms = [r.v_sum[k, 2]] + [r.v_in[k, 2 + step] for step in range(1, nz)]
            acc = jnp.zeros(terms[0].shape, F32)
            for zz in range(nz):
                came = lax.rem(z - zz + nz, nz)
                term = terms[0]
                for step in range(1, nz):
                    term = jnp.where(came == step, terms[step], term)
                acc = acc + term
            if k == 0:
                for j, ref in enumerate((r.bout_o, r.gain1_o, r.shift1_o, r.bdown_o, r.gain2_o, r.shift2_o)):
                    for part in range(2):
                        ref[:, part * BLOCK:(part + 1) * BLOCK] = acc[2 * j + part:2 * j + part + 1]
                for c in range(chunks):
                    r.bup_o[:, c * BLOCK:(c + 1) * BLOCK] = acc[12 + c:13 + c]
            else:
                r.bq_o[...] = acc[0:1]
                r.bv_o[...] = acc[1:2]

    def down_grad(j):
        return dot_nn(r.dT[...], r.active[j].reshape(items * lanes, BLOCK))

    def active_grad(j):
        r.work[j % 2] = dot_nt(r.dlow[...], r.wd[j])

    def upper_grad(j):
        for i in range(items):
            rows = pl.ds(i * rows_pad, rows_pad)
            r.upg[j % 3, i, pl.ds(0, rows_pad), :] = (r.work[j % 2, rows, :] * r.slope[j, rows, :].astype(F32)).astype(BF)

    def up_grad(j):
        return dot_nn(r.hT[...], r.upg[j % 3].reshape(items * lanes, BLOCK))

    def hidden_grad(j):
        r.gp[...] += dot_nt(r.upg[j % 3][:, :rows_pad].reshape(total, BLOCK), r.wu[j])

    def turn(i):
        rows = pl.ds(i * rows_pad, rows_pad)
        r.hT[pl.ds(0, width), pl.ds(i * lanes, lanes)] = transposed(r.hlow[rows, :].astype(F32))

    def turn_input(i):
        rows = pl.ds(i * rows_pad, rows_pad)
        r.xT[pl.ds(0, width), pl.ds(i * lanes, lanes)] = transposed(r.x_v[rows, :].astype(F32))

    def turn_keys(n):
        r.tra[n, 1] = transposed(r.keys[n].astype(F32) * 0.125)

    for c in range(chunks):
        start_core(c, down_grad(chunks + c))
    for c in range(chunks):
        hold(c, down_grad(c))
        if c < items:
            turn(c)
    r.out_o[...] = r.acc[pl.ds(0, items * length), :].astype(BF)
    order = list(range(chunks, 2 * chunks)) + list(range(chunks))
    active_grad(order[0])
    for c in range(chunks):
        start_a(c)
    for k, j in enumerate(order):
        if k + 1 < 2 * chunks:
            active_grad(order[k + 1])
        upper_grad(j)
        up = up_grad(j)
        c = j % chunks
        if j >= chunks:
            start_core(chunks + c, up)
            r.v_out[0, pl.ds(12 + c, 1), :] = up[width:width + 1]
        else:
            hold(chunks + c, up[:width])
            r.v_own[0, pl.ds(12 + c, 1), :] = up[width:width + 1]
        hidden_grad(j)
        if k < 2 * items:
            turn_keys(k)
        else:
            turn_input(k - 2 * items)
        if j < chunks:
            start_a(chunks + c)
    turn_input(2)
    for u in range(3):
        start_b(u)

    bout, gain1, shift1 = [], [], []

    def first_back(i):
        rows = pl.ds(i * rows_pad, rows_pad)
        hidden = r.gp[rows, :]
        normed = r.n1[rows, :]
        inverse = r.inv1[rows, :][:, :1]
        g = hidden * r.gain_one[...]
        grad = inverse * (g - mean(g) - normed * mean(g * normed))
        r.gp[rows, :] = grad
        r.olow[i, pl.ds(0, rows_pad), :] = grad.astype(BF)
        r.oT[:, pl.ds(i * lanes, lanes)] = transposed(grad)
        bout.append(column_sum(grad))
        gain1.append(column_sum(hidden * normed))
        shift1.append(column_sum(hidden))

    for i in range(items):
        first_back(i)
    for k, v in enumerate((bout, gain1, shift1, bdown, gain2, shift2)):
        v = sum(v[1:], v[0])
        for part in range(2):
            piece = v[:, part * BLOCK:(part + 1) * BLOCK]
            r.v_out[0, pl.ds(2 * k + part, 1), :] = piece
            r.v_own[0, pl.ds(2 * k + part, 1), :] = piece
    vec_core(0).start()

    start_core(8, dot_nt(r.oT[...], r.ctxT[1]))
    for n in [*range(items, 2 * items), *range(items)]:
        r.cgT[n] = dot_nt(r.wo[n // items], r.olow[n % items]).astype(BF)
    hold(8, dot_nt(r.oT[...], r.ctxT[0]))

    def probs_grad(n):
        for h in range(4):
            r.score[(n % 2) * 4 + h] = dot_nn(r.values[n, :, pair_of(h)] * half[h % 2], r.cgT[n, pair_of(h), :])

    def store_grad(n, k, h, value):
        r.gT[n // items, pl.ds(k * 256 + h * 64, 64), pl.ds((n % items) * lanes, lanes)] = value.astype(BF)

    def value_grad(n):
        for h in range(4):
            store_grad(n, 2, h, dot_nt(r.cgT[n, head_of(h), :], r.probs[n * 4 + h]))

    def score_grad(n):
        for h in range(4):
            pg = r.score[(n % 2) * 4 + h]
            p = r.probs[n * 4 + h, pl.ds(0, rows_pad), :].astype(F32)
            inner = jnp.sum(p * pg, axis=0, keepdims=True)
            r.dscore[(n % 2) * 4 + h, pl.ds(0, rows_pad), :] = (p * (pg - inner)).astype(BF)

    def query_key_grad(n):
        for h in range(4):
            ds = r.dscore[(n % 2) * 4 + h]
            store_grad(n, 0, h, dot_nn(r.tra[n, 1, head_of(h), :], ds))
            store_grad(n, 1, h, dot_nt(r.tra[n, 0, head_of(h), :], ds))

    def projection_grad(slot, k):
        return dot_nt(r.xT[...], r.gT[slot, pl.ds(k * 256, 256), :])

    after = (
        lambda: (start_a(8), vec_next(0, 0)),
        lambda: start_b(3),
        lambda: (start_c(0), start_c(1), start_c(2), vec_next(0, 1)),
        lambda: (start_b(4), start_b(5)),
        lambda: (start_b(6), start_c(3)),
        lambda: (start_b(7), start_c(4), vec_next(0, 2)))
    for k in range(2 * items):
        n = (k + items) % (2 * items)
        probs_grad(n)
        value_grad(n)
        score_grad(n)
        query_key_grad(n)
        if k == items - 1:
            for part in range(3):
                grad = projection_grad(1, part)
                start_core(9 + part, grad)
                if part != 1:
                    r.v_out[1, pl.ds(part // 2, 1), :] = grad[width:width + 1]
            vec_core(1).start()
        after[k]()
    for part in range(3):
        grad = projection_grad(0, part)
        hold(9 + part, grad[:width])
        if part != 1:
            r.v_own[1, pl.ds(part // 2, 1), :] = grad[width:width + 1]
        start_a(9 + part)
    vec_next(1, 0)

    for i in range(items):
        acc = None
        for slot in range(2):
            for k in range(3):
                term = dot_nn(r.wqkv[slot, k], r.gT[slot, pl.ds(k * 256, 256), pl.ds(i * lanes, lanes)])
                acc = term if acc is None else acc + term
        r.ig_o[pl.ds(i * length, length), :] = acc.T[:length] + r.gp[pl.ds(i * rows_pad, length), :]
    start_b(8)
    start_c(5)
    start_c(6)
    start_c(7)
    for k in range(3):
        start_b(9 + k)
    vec_next(1, 1)
    start_c(8)
    vec_next(0, 3)
    for c in range(chunks):
        r.gd_o[:, c * BLOCK:(c + 1) * BLOCK] = finish(c)
        r.gu_o[:, c * BLOCK:(c + 1) * BLOCK] = finish(chunks + c)
    for k in range(3):
        start_c(9 + k)
    vec_next(1, 2)
    r.go_o[...] = finish(8)
    r.gq_o[...] = finish(9)
    r.gk_o[...] = finish(10)
    r.gv_o[...] = finish(11)
    vec_next(1, 3)

    for s in remote:
        s.wait_send()
    for u in range(UNITS):
        to_core(u).wait_send()
        stage_a(u, ORDER[u]).wait_send()
        stage_b(u, ORDER[u]).wait_send()
        for step in range(1, 4):
            stage_c(u, ORDER[u], step).wait_send()
    for k in range(2):
        vec_core(k).wait_send()
        vec_side(k, 1).wait_send()
        vec_side(k, 2).wait_send()
        for step in range(1, nz):
            vec_z(k, step).wait_send()


def hand_over(count, *refs):
    sems = refs[-1]
    copies = [pltpu.make_async_copy(refs[k], refs[count + k], sems.at[k]) for k in range(count)]
    for c in copies:
        c.start()
    for c in copies:
        c.wait()


def layer_by_items(
    inputs, region_counts, w_query, b_query, w_key, w_value, b_value, w_out, b_out, gain_one, shift_one,
    w_up, b_up, w_down, b_down, gain_two, shift_two, cotangent,
):
    total_rows, width = inputs.shape
    item_count = region_counts.shape[0]
    length = total_rows // item_count
    items = item_count // 2
    rows_pad = -(-length // ITEM_PAD) * ITEM_PAD
    lanes = -(-length // 128) * 128
    dp_size = lax.axis_size("dp")
    nz = dp_size // 4
    shard = width // dp_size
    total = items * rows_pad
    chunks = w_up.shape[1] // BLOCK
    own_rows = items * length

    two_chunks = 2 * chunks
    hd = w_query.shape[1]
    inner = [
        ("x_raw", (total_rows, width), BF), ("x_v", (total, width), BF),
        ("cot_raw", (total_rows - own_rows // 8 * 8 + 16, width), F32), ("cot", (total, width), F32),
        ("bias_q", (2, 1, BLOCK), F32), ("bias_v", (2, 1, BLOCK), F32), ("bias_u", (2, 1, chunks * BLOCK), F32),
        ("b_out", (1, width), F32), ("gain_one", (1, width), F32), ("shift_one", (1, width), F32),
        ("b_down", (1, width), F32), ("gain_two", (1, width), F32), ("shift_two", (1, width), F32),
        ("wqkv", (2, 3, width, hd), BF), ("wo", (2, hd, width), BF),
        ("wu", (two_chunks, width, BLOCK), BF), ("wd", (two_chunks, BLOCK, width), BF),
        ("xT", (width + 16, items * lanes), BF), ("hT", (width + 16, items * lanes), BF),
        ("dT", (width, items * lanes), BF), ("oT", (width, items * lanes), BF),
        ("keys", (2 * items, rows_pad, hd), BF), ("values", (2 * items, rows_pad, hd), BF),
        ("tra", (2 * items, 3, hd, lanes), BF), ("score", (8, rows_pad, lanes), F32),
        ("probs", (8 * items, lanes, lanes), BF), ("ctxT", (2, hd, items * lanes), BF),
        ("ctx", (2, total, hd), BF), ("n1", (total, width), F32), ("inv1", (total, 128), F32),
        ("hlow", (total, width), BF), ("slope", (two_chunks, total, BLOCK), BF),
        ("active", (two_chunks, items, lanes, BLOCK), BF), ("acc", (total, width), F32),
        ("work", (3, total, BLOCK), F32), ("own", (4, width, BLOCK), F32),
        ("gp", (total, width), F32),
        ("dlow", (total, width), BF), ("upg", (3, items, lanes, BLOCK), BF), ("olow", (items, lanes, width), BF),
        ("cgT", (2 * items, hd, lanes), BF), ("dscore", (8, lanes, lanes), BF), ("gT", (2, 3 * hd, items * lanes), BF),
        ("g_out", (UNITS, 16, shard, BLOCK), BF), ("g", (UNITS, 16, shard, BLOCK), BF),
        ("g_a", (UNITS, 8, shard, BLOCK), BF), ("g_b", (UNITS, 4, shard, BLOCK), BF), ("g_c", (UNITS, 3, shard, BLOCK), BF),
        ("v_out", (2, 16, BLOCK), F32), ("v_own", (2, 16, BLOCK), F32),
        ("v_in", (2, 2 + nz, 16, BLOCK), F32), ("v_sum", (2, 3, 16, BLOCK), F32),
    ]
    n_weights = 8 + chunks
    sems = [
        ("in_sem", (16 + chunks,)), ("w_send", (n_weights,)), ("w_recv", (n_weights,)),
        ("core_send", (UNITS,)), ("core_recv", (UNITS,)), ("a_send", (UNITS,)), ("a_recv", (UNITS,)),
        ("b_send", (UNITS,)), ("b_recv", (UNITS,)), ("c_send", (UNITS, 3)), ("c_recv", (UNITS, 3)),
        ("v_send", (2, 2 + nz)), ("v_recv", (2, 2 + nz)),
    ]
    operands = [
        ("counts", region_counts), ("x_h", inputs), ("cot_h", cotangent), ("wq_h", w_query), ("wk_h", w_key),
        ("wv_h", w_value), ("wo_h", w_out), ("wu_h", w_up), ("wd_h", w_down.reshape(chunks, BLOCK, width)),
        ("b_query_h", b_query[None]), ("b_value_h", b_value[None]), ("b_up_h", b_up[None]), ("b_out_h", b_out[None]),
        ("gain_one_h", gain_one[None]), ("shift_one_h", shift_one[None]), ("b_down_h", b_down[None]),
        ("gain_two_h", gain_two[None]), ("shift_two_h", shift_two[None]),
    ]
    hidden = chunks * BLOCK
    results = [
        ("out_o", (own_rows, width), BF), ("ig_o", (own_rows, width), F32),
        ("gq_o", (shard, hd), F32), ("bq_o", (1, hd), F32),
        ("gk_o", (shard, hd), F32), ("gv_o", (shard, hd), F32),
        ("bv_o", (1, hd), F32), ("go_o", (shard, hd), F32),
        ("bout_o", (1, width), F32), ("gain1_o", (1, width), F32),
        ("shift1_o", (1, width), F32), ("gu_o", (shard, hidden), F32),
        ("bup_o", (1, hidden), F32), ("gd_o", (shard, hidden), F32),
        ("bdown_o", (1, width), F32), ("gain2_o", (1, width), F32),
        ("shift2_o", (1, width), F32),
    ]
    names = [n for n, _ in operands] + [n for n, *_ in results] + [n for n, *_ in inner] + [n for n, _ in sems]
    smem = pl.BlockSpec(memory_space=pltpu.SMEM)
    shapes = [jax.ShapeDtypeStruct(s, d) for _, s, d in results]
    made = pl.pallas_call(
        functools.partial(layer_kernel, (items, length, rows_pad, lanes, nz, shard), names),
        out_shape=[pltpu.VMEM(s, d) for _, s, d in results],
        in_specs=[smem] + [pl.BlockSpec(memory_space=pl.ANY)] * (len(operands) - 1),
        out_specs=[pl.BlockSpec(memory_space=pltpu.VMEM)] * len(results),
        scratch_shapes=[pltpu.VMEM(s, d) for _, s, d in inner] + [pltpu.SemaphoreType.DMA(s) for _, s in sems],
        compiler_params=pltpu.CompilerParams(
            collective_id=0, has_side_effects=True, vmem_limit_bytes=59 * 2**20),
        name="layer",
    )(*[v for _, v in operands])
    count = len(shapes)
    made = pl.pallas_call(
        functools.partial(hand_over, count),
        out_shape=shapes,
        in_specs=[pl.BlockSpec(memory_space=pltpu.VMEM)] * count,
        out_specs=[pl.BlockSpec(memory_space=pl.ANY)] * count,
        scratch_shapes=[pltpu.SemaphoreType.DMA((count,))],
        compiler_params=pltpu.CompilerParams(vmem_limit_bytes=2**20),
        name="hand_over",
    )(*[pltpu.with_memory_space_constraint(v, pltpu.VMEM) for v in made])
    made = [v.reshape(-1) if v.shape[0] == 1 else v for v in made]
    made[7], made[13] = made[7].T, made[13].T
    return tuple(made)


def solution(mesh):
    placed = (
        P("dp", None),
        P("dp"),
        P(None, "mp"),
        P("mp"),
        P(None, "mp"),
        P(None, "mp"),
        P("mp"),
        P("mp", None),
        P(),
        P(),
        P(),
        P(None, "mp"),
        P("mp"),
        P("mp", None),
        P(),
        P(),
        P(),
        P("dp", None),
    )
    dp_size, mp_size = mesh.shape["dp"], mesh.shape["mp"]

    def body(*args):
        width, hidden = args[0].shape[1], args[11].shape[1]
        whole_items = mp_size == 2 and args[1].shape[0] % 2 == 0
        even_shards = dp_size == 16 and width % (16 * dp_size) == 0
        blocks = args[2].shape[1] == BLOCK and width == 2 * BLOCK and hidden == 4 * BLOCK
        fits = args[0].shape[0] // args[1].shape[0] <= 256
        if whole_items and even_shards and blocks and fits:
            return layer_by_items(*args)
        return per_device(*args)

    return jax.shard_map(
        body,
        mesh=mesh,
        in_specs=placed,
        out_specs=(
            P(("dp", "mp"), None),
            P(("dp", "mp"), None),
            P("dp", "mp"),
            P("mp"),
            P("dp", "mp"),
            P("dp", "mp"),
            P("mp"),
            P("mp", "dp"),
            P(),
            P(),
            P(),
            P("dp", "mp"),
            P("mp"),
            P("mp", "dp"),
            P(),
            P(),
            P(),
        ),
        check_vma=False,
    )
```

```python
import functools
import types

import jax
import jax.numpy as jnp
from jax import lax
from jax.experimental import pallas as pl
from jax.experimental.pallas import tpu as pltpu
from jax.sharding import PartitionSpec as P

HEAD_DIM = 64
TEXT = 128


def layer_stats(pre_rows):
    row_mean = jnp.mean(pre_rows, axis=-1, keepdims=True)
    centred = pre_rows - row_mean
    inverse = lax.rsqrt(jnp.mean(centred * centred, axis=-1, keepdims=True) + 1e-12)
    return (centred * inverse, inverse)


def norm_back(grad_rows, normed, inverse, gain_vec):
    scaled = grad_rows * gain_vec
    return inverse * (
        scaled
        - jnp.mean(scaled, axis=-1, keepdims=True)
        - normed * jnp.mean(scaled * normed, axis=-1, keepdims=True)
    )


def gelu_slope(upper_part):
    return (
        0.5 * (1.0 + lax.erf(upper_part * 0.7071067811865476))
        + upper_part * jnp.exp(-0.5 * upper_part * upper_part) * 0.3989422804014327
    )


def contract_rows(first_op, second_op):
    return lax.dot_general(
        first_op, second_op, (((0,), (0,)), ((), ())), preferred_element_type=jnp.float32
    )


def times_transposed(first_op, second_op):
    return lax.dot_general(
        first_op, second_op, (((1,), (1,)), ((), ())), preferred_element_type=jnp.float32
    )


def per_device(
    inputs,
    region_counts,
    w_query,
    b_query,
    w_key,
    w_value,
    b_value,
    w_out,
    b_out,
    gain_one,
    shift_one,
    w_up,
    b_up,
    w_down,
    b_down,
    gain_two,
    shift_two,
    cotangent,
):
    total_rows = inputs.shape[0]
    item_count = region_counts.shape[0]
    length = total_rows // item_count
    heads_here = w_query.shape[1] // HEAD_DIM
    score_scale = HEAD_DIM ** (-0.5)
    share_rows = total_rows // lax.axis_size("mp")
    row_start = lax.axis_index("mp") * share_rows

    def own_rows(full_rows):
        return lax.dynamic_slice_in_dim(full_rows, row_start, share_rows, 0)

    def split_heads(flat_rows):
        return flat_rows.reshape(item_count, length, heads_here, HEAD_DIM)

    position = jnp.arange(length)
    visible = (position[None, :] < TEXT) | (position[None, :] - TEXT < region_counts[:, None])
    key_mask = visible[:, None, None, :]
    queries = (jnp.dot(inputs, w_query, preferred_element_type=jnp.float32) + b_query).astype(
        jnp.bfloat16
    )
    key_rows = jnp.dot(inputs, w_key, preferred_element_type=jnp.float32).astype(jnp.bfloat16)
    value_rows = (jnp.dot(inputs, w_value, preferred_element_type=jnp.float32) + b_value).astype(
        jnp.bfloat16
    )
    query_heads = split_heads(queries)
    key_heads = split_heads(key_rows)
    value_heads = split_heads(value_rows)

    def masked_scores():
        raw_scores = (
            jnp.einsum(
                "ishd,ithd->ihst", query_heads, key_heads, preferred_element_type=jnp.float32
            )
            * score_scale
        )
        return jnp.where(key_mask, raw_scores, -1000000000.0)

    scores = masked_scores()
    row_top = jnp.max(scores, axis=-1, keepdims=True)
    exponent = jnp.exp(scores - row_top)
    row_total = jnp.sum(exponent, axis=-1, keepdims=True)
    probs = exponent / row_total
    log_total = row_top + jnp.log(row_total)
    context = jnp.einsum(
        "ihst,ithd->ishd",
        probs.astype(jnp.bfloat16),
        value_heads,
        preferred_element_type=jnp.float32,
    )
    context = context.reshape(total_rows, heads_here * HEAD_DIM).astype(jnp.bfloat16)
    partial_attn = jnp.dot(context, w_out, preferred_element_type=jnp.float32)
    attended = lax.psum(partial_attn, "mp")
    normed_one, inverse_one = layer_stats(attended + b_out + inputs.astype(jnp.float32))
    hidden_one = normed_one * gain_one + shift_one
    hidden_low = hidden_one.astype(jnp.bfloat16)
    upper_part = jnp.dot(hidden_low, w_up, preferred_element_type=jnp.float32) + b_up
    active = jax.nn.gelu(upper_part, approximate=False).astype(jnp.bfloat16)
    partial_ffn = jnp.dot(active, w_down, preferred_element_type=jnp.float32)
    lowered = lax.psum(partial_ffn, "mp")
    normed_two, inverse_two = layer_stats(lowered + b_down + hidden_one)
    output = own_rows(normed_two * gain_two + shift_two).astype(jnp.bfloat16)
    grad_pre_two = norm_back(cotangent, normed_two, inverse_two, gain_two)
    down_low = grad_pre_two.astype(jnp.bfloat16)
    grad_output = own_rows(cotangent)
    normed_two_own = own_rows(normed_two)
    grad_two_own = own_rows(grad_pre_two)
    grad_gain_two = jnp.sum(grad_output * normed_two_own, axis=0)
    grad_shift_two = jnp.sum(grad_output, axis=0)
    grad_b_down = jnp.sum(grad_two_own, axis=0)
    grad_w_down = contract_rows(active, down_low)
    active_grad = times_transposed(down_low, w_down)
    upper_grad = (active_grad * gelu_slope(upper_part)).astype(jnp.bfloat16)
    grad_b_up = jnp.sum(upper_grad.astype(jnp.float32), axis=0)
    grad_w_up = contract_rows(hidden_low, upper_grad)
    partial_hidden = times_transposed(upper_grad, w_up)
    hidden_grad = lax.psum(partial_hidden, "mp") + grad_pre_two
    grad_pre_one = norm_back(hidden_grad, normed_one, inverse_one, gain_one)
    out_low = grad_pre_one.astype(jnp.bfloat16)
    hidden_grad_own = own_rows(hidden_grad)
    normed_one_own = own_rows(normed_one)
    grad_one_own = own_rows(grad_pre_one)
    grad_gain_one = jnp.sum(hidden_grad_own * normed_one_own, axis=0)
    grad_shift_one = jnp.sum(hidden_grad_own, axis=0)
    grad_b_out = jnp.sum(grad_one_own, axis=0)
    grad_w_out = contract_rows(context, out_low)
    context_grad = split_heads(times_transposed(out_low, w_out).astype(jnp.bfloat16))
    probs_again = jnp.exp(masked_scores() - log_total)
    prob_grad = jnp.einsum(
        "ishd,ithd->ihst", context_grad, value_heads, preferred_element_type=jnp.float32
    )
    row_inner = jnp.sum(probs_again * prob_grad, axis=-1, keepdims=True)
    score_grad = (probs_again * (prob_grad - row_inner)).astype(jnp.bfloat16)
    query_grad = (
        (
            jnp.einsum("ihst,ithd->ishd", score_grad, key_heads, preferred_element_type=jnp.float32)
            * score_scale
        )
        .astype(jnp.bfloat16)
        .reshape(total_rows, heads_here * HEAD_DIM)
    )
    key_grad = (
        (
            jnp.einsum(
                "ihst,ishd->ithd", score_grad, query_heads, preferred_element_type=jnp.float32
            )
            * score_scale
        )
        .astype(jnp.bfloat16)
        .reshape(total_rows, heads_here * HEAD_DIM)
    )
    value_grad = jnp.einsum(
        "ihst,ishd->ithd",
        probs_again.astype(jnp.bfloat16),
        context_grad,
        preferred_element_type=jnp.float32,
    ).astype(jnp.bfloat16)
    value_grad = value_grad.reshape(total_rows, heads_here * HEAD_DIM)
    grad_b_query = jnp.sum(query_grad.astype(jnp.float32), axis=0)
    grad_b_value = jnp.sum(value_grad.astype(jnp.float32), axis=0)
    grad_w_query = contract_rows(inputs, query_grad)
    grad_w_key = contract_rows(inputs, key_grad)
    grad_w_value = contract_rows(inputs, value_grad)
    partial_input = (
        times_transposed(query_grad, w_query)
        + times_transposed(key_grad, w_key)
        + times_transposed(value_grad, w_value)
    )
    input_grad = own_rows(
        lax.psum(partial_input.astype(jnp.bfloat16), "mp").astype(jnp.float32) + grad_pre_one
    )
    bias_sums = lax.psum((grad_b_query, grad_b_value, grad_b_up), "dp")
    norm_sums = lax.psum(
        (grad_b_out, grad_gain_one, grad_shift_one, grad_b_down, grad_gain_two, grad_shift_two),
        ("dp", "mp"),
    )
    weight_sums = (
        lax.psum_scatter(
            grad_w_query.astype(jnp.bfloat16), "dp", scatter_dimension=0, tiled=True
        ).astype(jnp.float32),
        lax.psum_scatter(
            grad_w_key.astype(jnp.bfloat16), "dp", scatter_dimension=0, tiled=True
        ).astype(jnp.float32),
        lax.psum_scatter(
            grad_w_value.astype(jnp.bfloat16), "dp", scatter_dimension=0, tiled=True
        ).astype(jnp.float32),
        lax.psum_scatter(
            grad_w_out.astype(jnp.bfloat16), "dp", scatter_dimension=1, tiled=True
        ).astype(jnp.float32),
        lax.psum_scatter(
            grad_w_up.astype(jnp.bfloat16), "dp", scatter_dimension=0, tiled=True
        ).astype(jnp.float32),
        lax.psum_scatter(
            grad_w_down.astype(jnp.bfloat16), "dp", scatter_dimension=1, tiled=True
        ).astype(jnp.float32),
    )
    return (
        output,
        input_grad,
        weight_sums[0],
        bias_sums[0],
        weight_sums[1],
        weight_sums[2],
        bias_sums[1],
        weight_sums[3],
        norm_sums[0],
        norm_sums[1],
        norm_sums[2],
        weight_sums[4],
        bias_sums[2],
        weight_sums[5],
        norm_sums[3],
        norm_sums[4],
        norm_sums[5],
    )


ITEM_PAD = 16
MESH = pl.DeviceIdType.MESH
BF = jnp.bfloat16
F32 = jnp.float32
BLOCK = 256
HALF = 128
WHOLE_UNITS, HALF_UNITS = 9, 6
UNITS = WHOLE_UNITS + HALF_UNITS
X_FIRST, Y_FIRST, Z_FIRST = 0, 1, 2
ORDER = (0, 1, 2, 0, 1, 2, 1, 1, 2, 0, 1, 0, 1, 0, 1)
PLAN = {
    13: (('M', 0, 1, 2, 3),),
    14: (('A', 0, 1),),
    21: (('M', 4, 5),),
    23: (('M', 6, 7),),
    24: (('A', 4),),
    25: (('A', 5),),
    26: (('B', 0, 1), ('A', 6),),
    27: (('B', 2), ('A', 7),),
    31: (('M', 8), ('D', -1), ('C', 1), ('B', 3, 4),),
    41: (('D', 0), ('A', 8), ('C', 0), ('B', 5),),
    43: (('M', 9, 10, 11, 12, 13, 14), ('E', -1), ('C', 2),),
    51: (('C', 4), ('B', 6),),
    53: (('D', 1), ('A', 9, 10, 11),),
    61: (('B', 7),),
    63: (('D', 2), ('E', 0), ('A', 12, 13, 14), ('C', 3), ('B', 8),),
    71: (('C', 5, 6), ('B', 9, 10, 11),),
    72: (('C', 7),),
    73: (('E', 1), ('B', 12, 13, 14), ('F', 0, 1, 2), ('C', 9, 10, 11), ('D', 3), ('E', 2), ('F', 3, 4), ('C', 12, 13, 14), ('C', 8), ('F', 5, 6, 7), ('F', 8, 9, 10, 11, 12, 13, 14), ('E', 3), ('D', 4), ('E', 4),),
    20: (('A', 2, 3),),
}


def dot_nn(a, b):
    return lax.dot_general(a, b, (((1,), (0,)), ((), ())), preferred_element_type=F32)


def dot_nt(a, b):
    return lax.dot_general(a, b, (((1,), (1,)), ((), ())), preferred_element_type=F32)


def layer_kernel(dims, names, *refs):
    r = types.SimpleNamespace(**dict(zip(names, refs, strict=True)))
    items, length, rows_pad, lanes, nz, shard = dims
    total = items * rows_pad
    chunks = r.wu_h.shape[1] // BLOCK
    width = r.x_h.shape[1]
    dp, mp = lax.axis_index("dp"), lax.axis_index("mp")
    z, y, x = dp // 4, (dp // 2) % 2, dp % 2

    def at(z_, y_, x_):
        return z_ * 4 + y_ * 2 + x_

    core = (dp, 1 - mp)
    x_side = (at(z, y, 1 - x), mp)
    y_side = (at(z, 1 - y, x), mp)
    z_side = [(at((z + step) % nz, y, x), mp) for step in range(1, nz)]
    low_side = (at(z + 1 - 2 * (z % 2), y, x), mp)
    high_side = z_side[1]
    plane_side = [(at(z, (y + step // 2) % 2, (x + step) % 2), mp) for step in range(1, 4)]

    local = []

    def bring(src, dst):
        copy = pltpu.make_async_copy(src, dst, r.in_sem.at[len(local)])
        copy.start()
        local.append(copy)
        return copy

    c_x = bring(r.x_h, r.x_raw)
    c_w = [bring(src, r.wqkv.at[0, k]) for k, src in enumerate((r.wq_h, r.wk_h, r.wv_h))]
    c_p = [bring(r.b_query_h, r.bias_q.at[0]), bring(r.b_value_h, r.bias_v.at[0]), bring(r.b_up_h, r.bias_u.at[0])]

    barrier = pltpu.get_barrier_semaphore()
    near = [core] + plane_side + z_side
    for device in near:
        pl.semaphore_signal(barrier, inc=1, device_id=device, device_id_type=MESH)
    vectors = (
        (r.b_out_h, r.b_out), (r.gain_one_h, r.gain_one), (r.shift_one_h, r.shift_one),
        (r.b_down_h, r.b_down), (r.gain_two_h, r.gain_two), (r.shift_two_h, r.shift_two))
    c_vec = [bring(src, dst) for src, dst in vectors]
    c_wo = bring(r.wo_h, r.wo.at[0])
    c_wu = [bring(r.wu_h.at[:, pl.ds(c * BLOCK, BLOCK)], r.wu.at[c]) for c in range(chunks)]
    c_wd = bring(r.wd_h, r.wd.at[pl.ds(0, chunks)])
    full_rows = r.x_h.shape[0]
    base = items * length // 8 * 8
    cot_count = full_rows - base
    c_cot = bring(r.cot_h.at[pl.ds(pl.multiple_of(mp * base, 8), cot_count)], r.cot_raw.at[pl.ds(0, cot_count)])

    pad_rows = lanes - rows_pad

    def transposed(block):
        full = jnp.concatenate([block, jnp.zeros((pad_rows, block.shape[1]), F32)], axis=0)
        return full.T.astype(BF)

    def rows_of(i):
        return pl.ds(pl.multiple_of(i * rows_pad, 16), rows_pad)

    def lanes_of(i):
        return pl.ds(pl.multiple_of(i * lanes, lanes), lanes)

    def greet():
        pl.semaphore_wait(barrier, len(near))

    def clear(n, carry):
        r.probs[n, pl.ds(rows_pad, pad_rows), :] = jnp.zeros((pad_rows, lanes), BF)
        return carry

    lax.fori_loop(0, r.probs.shape[0], clear, 0)
    zero_block = jnp.zeros((pad_rows, BLOCK), BF)
    for i in range(items):
        r.olow[i, pl.ds(rows_pad, pad_rows), :] = jnp.zeros((pad_rows, width), BF)
        for j in range(r.upg.shape[0]):
            r.upg[j, i, pl.ds(rows_pad, pad_rows), :] = zero_block
        for j in range(2 * chunks):
            r.active[j, i, pl.ds(rows_pad, pad_rows), :] = zero_block
    for k in range(r.dscore.shape[0]):
        r.dscore[k, pl.ds(rows_pad, pad_rows), :] = jnp.zeros((pad_rows, lanes), BF)
    one_row = jnp.where(lax.broadcasted_iota(jnp.int32, (16, items * lanes), 0) == 0, 1.0, 0.0).astype(BF)
    r.xT[pl.ds(width, 16), :] = one_row
    r.hT[pl.ds(width, 16), :] = one_row
    cot_rows = r.cot_raw.shape[0]
    r.cot_raw[pl.ds(cot_count, cot_rows - cot_count), :] = jnp.zeros((cot_rows - cot_count, width), F32)

    c_x.wait()
    down_ = lax.broadcasted_iota(jnp.int32, (rows_pad, 256), 0)
    across = lax.broadcasted_iota(jnp.int32, (rows_pad, 256), 1)
    for i in range(items):
        block = None
        for m in range(2):
            start = (m * items + i) * length
            window = start // 16 * 16
            count = min(256, full_rows - window)
            shift = jnp.where(mp == m, start - window, 2 * 256)
            pick = jnp.where((across == down_ + shift) & (down_ < length), 1.0, 0.0).astype(BF)
            term = dot_nn(pick[:, :count], r.x_raw[pl.ds(window, count), :])
            block = term if block is None else block + term
        r.x_v[rows_of(i), :] = block.astype(BF)

    greet()

    remote = []

    def send_weight(src, dst):
        k = len(remote)
        copy = pltpu.make_async_remote_copy(
            src_ref=src, dst_ref=dst, send_sem=r.w_send.at[k], recv_sem=r.w_recv.at[k],
            device_id=core, device_id_type=MESH)
        copy.start()
        remote.append(copy)
        return copy

    s_w = [send_weight(src, r.wqkv.at[1, k]) for k, src in enumerate((r.wq_h, r.wk_h, r.wv_h))]
    s_w += [send_weight(src, dst.at[1]) for src, dst in (
        (r.b_query_h, r.bias_q), (r.b_value_h, r.bias_v), (r.b_up_h, r.bias_u))]
    s_wo = send_weight(r.wo_h, r.wo.at[1])
    s_wu = [send_weight(r.wu_h.at[:, pl.ds(c * BLOCK, BLOCK)], r.wu.at[chunks + c]) for c in range(chunks)]
    s_wd = send_weight(r.wd_h, r.wd.at[pl.ds(chunks, chunks)])

    def project(slot, k):
        r.work[k] = dot_nn(r.x_v[...], r.wqkv[slot, k])

    def keep(slot, k):
        for i in range(items):
            block = r.work[k, pl.ds(i * rows_pad, rows_pad), :]
            n = slot * items + i
            if k == 0:
                r.tra[n, 0] = transposed((block + r.bias_q[slot]) * 0.125)
            elif k == 1:
                r.keys[n] = block.astype(BF)
            else:
                block = block + r.bias_v[slot]
                r.values[n] = block.astype(BF)
                r.tra[n, 2] = transposed(block)

    for c in c_w + c_p:
        c.wait()
    for k in range(3):
        project(0, k)
    for k in range(3):
        keep(0, k)
    lane = lax.broadcasted_iota(jnp.int32, (1, 128), 1)
    half = [jnp.where(lane < 64, 1.0, 0.0).astype(BF), jnp.where(lane >= 64, 1.0, 0.0).astype(BF)]
    position = lax.broadcasted_iota(jnp.int32, (rows_pad, lanes), 0)

    def pair_of(h):
        return slice((h // 2) * 128, (h // 2) * 128 + 128)

    def head_of(h):
        return slice(h * 64, (h + 1) * 64)

    def scores_of(n):
        for h in range(4):
            r.score[(n % 2) * 4 + h] = dot_nn(r.keys[n, :, pair_of(h)] * half[h % 2], r.tra[n, 0, pair_of(h), :])

    def soften(n):
        mask = jnp.where(position < TEXT + r.counts[mp * items + n % items], 0.0, -1e9)
        for h in range(4):
            score = r.score[(n % 2) * 4 + h] + mask
            top = jnp.max(score, axis=0, keepdims=True)
            e = jnp.exp(score - top)
            p = e * (1.0 / jnp.sum(e, axis=0, keepdims=True))
            r.probs[n * 4 + h, pl.ds(0, rows_pad), :] = p.astype(BF)

    def contexts_of(n):
        parts = [dot_nn(r.tra[n, 2, head_of(h), :], r.probs[n * 4 + h]) for h in range(4)]
        context = jnp.concatenate(parts, axis=0)
        slot, i = n // items, n % items
        r.ctxT[slot, :, pl.ds(i * lanes, lanes)] = context.astype(BF)
        r.ctx[slot, pl.ds(i * rows_pad, rows_pad), :] = context.T[:rows_pad].astype(BF)

    scores_of(0)
    for n in range(2 * items):
        if n + 1 == items:
            soften(n)
            for c in s_w:
                c.wait_recv()
            for k in range(3):
                project(1, k)
            contexts_of(n)
            for k in range(3):
                keep(1, k)
            scores_of(n + 1)
            continue
        if n + 1 < 2 * items:
            scores_of(n + 1)
        soften(n)
        contexts_of(n)

    c_wo.wait()
    s_wo.wait_recv()
    for c in c_vec:
        c.wait()

    def attended(i):
        rows = pl.ds(i * rows_pad, rows_pad)
        r.acc[rows, :] = dot_nn(r.ctx[0, rows, :], r.wo[0]) + dot_nn(r.ctx[1, rows, :], r.wo[1])

    def first_norm(i):
        rows = pl.ds(i * rows_pad, rows_pad)
        pre = r.acc[rows, :] + r.b_out[...] + r.x_v[rows, :].astype(F32)
        centred = pre - jnp.mean(pre, axis=1, keepdims=True)
        inverse = lax.rsqrt(jnp.mean(centred * centred, axis=1, keepdims=True) + 1e-12)
        normed = centred * inverse
        r.n1[rows, :] = normed
        r.inv1[rows, :] = jnp.broadcast_to(inverse, (rows_pad, 128))
        r.hlow[rows, :] = (normed * r.gain_one[...] + r.shift_one[...]).astype(BF)

    for i in range(items):
        attended(i)
    for i in range(items):
        first_norm(i)

    for c in c_wu + [c_wd]:
        c.wait()
    for c in s_wu + [s_wd]:
        c.wait_recv()
    c_cot.wait()
    valid = lax.broadcasted_iota(jnp.int32, (rows_pad, 1), 0) < length

    def own_cotangent(i):
        at_ = [r.cot_raw[pl.ds(m * (items * length - base) + i * length, rows_pad), :] for m in range(2)]
        r.cot[pl.ds(i * rows_pad, rows_pad), :] = jnp.where(valid, jnp.where(mp == 0, at_[0], at_[1]), 0.0)

    def lift(j):
        slot, c = j // chunks, j % chunks
        r.work[j % 2] = dot_nn(r.hlow[...], r.wu[j]) + r.bias_u[slot, :, c * BLOCK:(c + 1) * BLOCK]

    def activate(j):
        for i in range(items):
            rows = pl.ds(i * rows_pad, rows_pad)
            u = r.work[j % 2, rows, :]
            phi = 0.5 + 0.5 * lax.erf(u * 0.7071067811865476)
            r.slope[j, rows, :] = (phi + u * (jnp.exp(-0.5 * u * u) * 0.3989422804014327)).astype(BF)
            r.active[j, i, pl.ds(0, rows_pad), :] = (u * phi).astype(BF)

    def lower(j):
        part = dot_nn(r.active[j][:, :rows_pad].reshape(total, BLOCK), r.wd[j])
        if j == 0:
            r.acc[...] = part
        else:
            r.acc[...] += part

    lift(0)
    for j in range(2 * chunks):
        if j > 0:
            lower(j - 1)
        if j + 1 < 2 * chunks:
            lift(j + 1)
        activate(j)
        if 2 <= j < 2 + items:
            own_cotangent(j - 2)
    lower(2 * chunks - 1)

    def mean(v):
        return jnp.mean(v, axis=1, keepdims=True)

    def column_sum(v):
        return jnp.sum(v, axis=0, keepdims=True)

    gain2, shift2, bdown = [], [], []

    def second_norm(i):
        rows = pl.ds(i * rows_pad, rows_pad)
        hidden = r.n1[rows, :] * r.gain_one[...] + r.shift_one[...]
        pre = r.acc[rows, :] + r.b_down[...] + hidden
        centred = pre - mean(pre)
        inverse = lax.rsqrt(mean(centred * centred) + 1e-12)
        normed = centred * inverse
        cot = r.cot[rows, :]
        g = cot * r.gain_two[...]
        grad = inverse * (g - mean(g) - normed * mean(g * normed))
        r.gp[rows, :] = grad
        r.dlow[rows, :] = grad.astype(BF)
        r.dT[:, pl.ds(i * lanes, lanes)] = transposed(grad)
        r.acc[pl.ds(i * length, rows_pad), :] = normed * r.gain_two[...] + r.shift_two[...]
        gain2.append(column_sum(cot * normed))
        shift2.append(column_sum(cot))
        bdown.append(column_sum(grad))

    for i in range(items):
        second_norm(i)

    def held(u):
        if u < WHOLE_UNITS:
            return [ref.at[u] for ref in (r.g_out, r.g, r.g_a, r.g_b, r.g_c)]
        return [ref.at[u - WHOLE_UNITS] for ref in (r.h_out, r.h, r.h_a, r.h_b, r.h_c)]

    def size_of(u):
        return 0 if u < WHOLE_UNITS else 1

    def to_core(u):
        return pltpu.make_async_remote_copy(
            src_ref=held(u)[0], dst_ref=held(u)[1], send_sem=r.sent.at[0, size_of(u)],
            recv_sem=r.core_recv.at[u], device_id=core, device_id_type=MESH)

    route = (
        (x, y, z, x_side, y_side), (y, x, z, y_side, x_side), (z % 2, z // 2, y * 2 + x, low_side, high_side))

    def shard_order(order):
        if order == X_FIRST:
            return [at(c, b, a) for a in range(2) for b in range(2) for c in range(nz)]
        if order == Y_FIRST:
            return [at(c, a, b) for a in range(2) for b in range(2) for c in range(nz)]
        return [at(2 * b + a, c, d) for a in range(2) for b in range(2) for c in range(2) for d in range(2)]

    def stage_a(u, order):
        first, _, _, device, _ = route[order]
        return pltpu.make_async_remote_copy(
            src_ref=held(u)[1].at[pl.ds((1 - first) * 8, 8)], dst_ref=held(u)[2], send_sem=r.sent.at[1, size_of(u)],
            recv_sem=r.a_recv.at[u], device_id=device, device_id_type=MESH)

    def stage_b(u, order):
        first, second, _, _, device = route[order]
        return pltpu.make_async_remote_copy(
            src_ref=held(u)[1].at[pl.ds(first * 8 + (1 - second) * 4, 4)], dst_ref=held(u)[3], send_sem=r.sent.at[2, size_of(u)],
            recv_sem=r.b_recv.at[u], device_id=device, device_id_type=MESH)

    def wait_spread(u):
        came = held(u)[4]
        pltpu.make_async_remote_copy(
            src_ref=came, dst_ref=came, send_sem=r.sent.at[3, size_of(u)], recv_sem=r.c_recv.at[u],
            device_id=core, device_id_type=MESH).wait_recv()

    def wait_sent():
        for size, bufs in enumerate(((r.g_out, r.g_a, r.g_b, r.g_c), (r.h_out, r.h_a, r.h_b, r.h_c))):
            for stage, ref in enumerate(bufs):
                pltpu.make_async_remote_copy(
                    src_ref=ref, dst_ref=ref, send_sem=r.sent.at[stage, size], recv_sem=r.core_recv.at[0],
                    device_id=core, device_id_type=MESH).wait_send()

    def stage_c(u, order, step):
        first, second, _, _, _ = route[order]
        if order in (X_FIRST, Y_FIRST):
            place, device = (z + step) % nz, z_side[step - 1]
        else:
            place, device = ((y + step // 2) % 2) * 2 + (x + step) % 2, plane_side[step - 1]
        return pltpu.make_async_remote_copy(
            src_ref=held(u)[1].at[first * 8 + second * 4 + place], dst_ref=held(u)[4].at[step - 1],
            send_sem=r.sent.at[3, size_of(u)], recv_sem=r.c_recv.at[u],
            device_id=device, device_id_type=MESH)

    def lay_out(u, value):
        ref = held(u)[0]
        for place, block in enumerate(shard_order(ORDER[u])):
            ref[place] = value[block * shard:(block + 1) * shard].astype(BF)

    def start_core(u):
        to_core(u).start()

    def hold(u, value):
        r.own[u % r.own.shape[0], :, :value.shape[1]] = value

    def start_a(u):
        to_core(u).wait_recv()
        ref = held(u)[1]
        for place, block in enumerate(shard_order(ORDER[u])):
            mine = r.own[u % r.own.shape[0], pl.ds(block * shard, shard), :ref.shape[-1]]
            ref[place] = (mine + ref[place].astype(F32)).astype(BF)
        stage_a(u, ORDER[u]).start()

    def start_b(u):
        order = ORDER[u]
        stage_a(u, order).wait_recv()
        kept = pl.ds(route[order][0] * 8, 8)
        _, ref, came, _, _ = held(u)
        ref[kept] = ref[kept] + came[...]
        stage_b(u, order).start()

    def start_c(u):
        order = ORDER[u]
        stage_b(u, order).wait_recv()
        kept = pl.ds(route[order][0] * 8 + route[order][1] * 4, 4)
        _, ref, _, came, _ = held(u)
        ref[kept] = ref[kept] + came[...]
        for step in range(1, 4):
            stage_c(u, order, step).start()

    def finish(u):
        order = ORDER[u]
        first, second, third, _, _ = route[order]
        _, ref, _, _, came = held(u)
        acc = ref[first * 8 + second * 4 + third].astype(F32)
        wait_spread(u)
        for step in range(1, 4):
            acc += came[step - 1].astype(F32)
        return acc

    def vec_copy(k, stage, src, device):
        group = min(stage, 3)
        return pltpu.make_async_remote_copy(
            src_ref=src, dst_ref=r.v_in.at[k, stage], send_sem=r.v_send.at[k, group],
            recv_sem=r.v_recv.at[k, group], device_id=device, device_id_type=MESH)

    def vec_spread(k):
        came = r.v_in.at[k, pl.ds(3, nz - 1)]
        return pltpu.make_async_remote_copy(
            src_ref=came, dst_ref=came, send_sem=r.v_send.at[k, 3], recv_sem=r.v_recv.at[k, 3],
            device_id=core, device_id_type=MESH)

    def vec_core(k):
        return vec_copy(k, 0, r.v_out.at[k], core)

    def vec_side(k, stage):
        return vec_copy(k, stage, r.v_sum.at[k, stage - 1], (x_side, y_side)[stage - 1])

    def vec_z(k, step):
        return vec_copy(k, 2 + step, r.v_sum.at[k, 2], z_side[step - 1])

    def vec_next(k, stage):
        if stage == 0:
            vec_core(k).wait_recv()
            r.v_sum[k, 0] = r.v_own[k] + r.v_in[k, 0]
            vec_side(k, 1).start()
        elif stage == 1:
            vec_side(k, 1).wait_recv()
            r.v_sum[k, 1] = r.v_sum[k, 0] + r.v_in[k, 1]
            vec_side(k, 2).start()
        elif stage == 2:
            vec_side(k, 2).wait_recv()
            r.v_sum[k, 2] = r.v_sum[k, 1] + r.v_in[k, 2]
            for step in range(1, nz):
                vec_z(k, step).start()
        else:
            vec_spread(k).wait_recv()
            terms = [r.v_sum[k, 2]] + [r.v_in[k, 2 + step] for step in range(1, nz)]
            acc = jnp.zeros(terms[0].shape, F32)
            for zz in range(nz):
                came = lax.rem(z - zz + nz, nz)
                term = terms[0]
                for step in range(1, nz):
                    term = jnp.where(came == step, terms[step], term)
                acc = acc + term
            if k == 0:
                for j, ref in enumerate((r.bout_o, r.gain1_o, r.shift1_o, r.bdown_o, r.gain2_o, r.shift2_o)):
                    for part in range(2):
                        ref[:, part * BLOCK:(part + 1) * BLOCK] = acc[2 * j + part:2 * j + part + 1]
                for c in range(chunks):
                    r.bup_o[:, c * BLOCK:(c + 1) * BLOCK] = acc[12 + c:13 + c]
            else:
                r.bq_o[...] = acc[0:1]
                r.bv_o[...] = acc[1:2]

    def store_sum(u):
        total_ = finish(u)
        if u < 2 * chunks:
            column = u % chunks * BLOCK
            (r.gd_o, r.gu_o)[u // chunks][:, column:column + BLOCK] = total_
        elif u < WHOLE_UNITS:
            r.go_o[...] = total_
        else:
            column = (u - WHOLE_UNITS) // 3 * HALF
            (r.gq_o, r.gk_o, r.gv_o)[(u - WHOLE_UNITS) % 3][:, column:column + HALF] = total_

    def sums(k):
        def step(stage):
            if stage == 4:
                vec_core(k).wait_send()
                vec_side(k, 1).wait_send()
                vec_side(k, 2).wait_send()
                vec_spread(k).wait_send()
            elif stage < 0:
                vec_core(k).start()
            else:
                vec_next(k, stage)

        return step

    steps = dict(M=start_core, A=start_a, B=start_b, C=start_c, F=store_sum, D=sums(0), E=sums(1))

    def after(piece):
        for step, *units in PLAN.get(piece, ()):
            for u in units:
                steps[step](u)

    def down_grad(j):
        return dot_nn(r.dT[...], r.active[j].reshape(items * lanes, BLOCK))

    def active_grad(j):
        r.work[j % 2] = dot_nt(r.dlow[...], r.wd[j])

    def upper_grad(j):
        for i in range(items):
            rows = pl.ds(i * rows_pad, rows_pad)
            r.upg[j % 3, i, pl.ds(0, rows_pad), :] = (r.work[j % 2, rows, :] * r.slope[j, rows, :].astype(F32)).astype(BF)

    def up_grad(j):
        return dot_nn(r.hT[...], r.upg[j % 3].reshape(items * lanes, BLOCK))

    def hidden_grad(j):
        r.gp[...] += dot_nt(r.upg[j % 3][:, :rows_pad].reshape(total, BLOCK), r.wu[j])

    def turn(i):
        rows = pl.ds(i * rows_pad, rows_pad)
        r.hT[pl.ds(0, width), pl.ds(i * lanes, lanes)] = transposed(r.hlow[rows, :].astype(F32))

    def turn_input(i):
        rows = pl.ds(i * rows_pad, rows_pad)
        r.xT[pl.ds(0, width), pl.ds(i * lanes, lanes)] = transposed(r.x_v[rows, :].astype(F32))

    def turn_keys(n):
        r.tra[n, 1] = transposed(r.keys[n].astype(F32) * 0.125)

    for c in range(chunks):
        lay_out(c, down_grad(chunks + c))
        after(10 + c)
    for c in range(chunks):
        hold(c, down_grad(c))
        if c < items:
            turn(c)
    r.out_o[...] = r.acc[pl.ds(0, items * length), :].astype(BF)
    order = list(range(chunks, 2 * chunks)) + list(range(chunks))
    active_grad(order[0])
    after(14)
    for k, j in enumerate(order):
        if k + 1 < 2 * chunks:
            active_grad(order[k + 1])
        upper_grad(j)
        up = up_grad(j)
        c = j % chunks
        if j >= chunks:
            lay_out(chunks + c, up)
            r.v_out[0, pl.ds(12 + c, 1), :] = up[width:width + 1]
        else:
            hold(chunks + c, up[:width])
            r.v_own[0, pl.ds(12 + c, 1), :] = up[width:width + 1]
        hidden_grad(j)
        if k < 2 * items:
            turn_keys(k)
        else:
            turn_input(k - 2 * items)
        after(20 + k)
    turn_input(2)

    bout, gain1, shift1 = [], [], []

    def first_back(i):
        rows = pl.ds(i * rows_pad, rows_pad)
        hidden = r.gp[rows, :]
        normed = r.n1[rows, :]
        inverse = r.inv1[rows, :][:, :1]
        g = hidden * r.gain_one[...]
        grad = inverse * (g - mean(g) - normed * mean(g * normed))
        r.gp[rows, :] = grad
        r.olow[i, pl.ds(0, rows_pad), :] = grad.astype(BF)
        r.oT[:, pl.ds(i * lanes, lanes)] = transposed(grad)
        bout.append(column_sum(grad))
        gain1.append(column_sum(hidden * normed))
        shift1.append(column_sum(hidden))

    for i in range(items):
        first_back(i)
    for k, v in enumerate((bout, gain1, shift1, bdown, gain2, shift2)):
        v = sum(v[1:], v[0])
        for part in range(2):
            piece = v[:, part * BLOCK:(part + 1) * BLOCK]
            r.v_out[0, pl.ds(2 * k + part, 1), :] = piece
            r.v_own[0, pl.ds(2 * k + part, 1), :] = piece
    after(30)

    lay_out(8, dot_nt(r.oT[...], r.ctxT[1]))
    for n in [*range(items, 2 * items), *range(items)]:
        r.cgT[n] = dot_nt(r.wo[n // items], r.olow[n % items]).astype(BF)
    hold(8, dot_nt(r.oT[...], r.ctxT[0]))
    after(31)

    def probs_grad(n, heads):
        for h in heads:
            r.score[(n % 2) * 4 + h] = dot_nn(r.values[n, :, pair_of(h)] * half[h % 2], r.cgT[n, pair_of(h), :])

    def store_grad(n, k, h, value):
        r.gT[n // items, pl.ds(k * 256 + h * 64, 64), pl.ds((n % items) * lanes, lanes)] = value.astype(BF)

    def value_grad(n, heads):
        for h in heads:
            store_grad(n, 2, h, dot_nt(r.cgT[n, head_of(h), :], r.probs[n * 4 + h]))

    def score_grad(n, heads):
        for h in heads:
            pg = r.score[(n % 2) * 4 + h]
            p = r.probs[n * 4 + h, pl.ds(0, rows_pad), :].astype(F32)
            inner = jnp.sum(p * pg, axis=0, keepdims=True)
            r.dscore[(n % 2) * 4 + h, pl.ds(0, rows_pad), :] = (p * (pg - inner)).astype(BF)

    def query_key_grad(n, heads):
        for h in heads:
            ds = r.dscore[(n % 2) * 4 + h]
            store_grad(n, 0, h, dot_nn(r.tra[n, 1, head_of(h), :], ds))
            store_grad(n, 1, h, dot_nt(r.tra[n, 0, head_of(h), :], ds))

    def projection_grad(slot, k):
        return dot_nt(r.xT[...], r.gT[slot, pl.ds(k * 256, 256), :])

    for s in remote:
        s.wait_send()

    def attend_back(n, heads):
        probs_grad(n, heads)
        value_grad(n, heads)
        score_grad(n, heads)
        query_key_grad(n, heads)

    for n in range(items, 2 * items):
        attend_back(n, range(4))
        after(40 + n - items)
    for part in range(3):
        grad = projection_grad(1, part)
        for pair in range(2):
            lay_out(WHOLE_UNITS + 3 * pair + part, grad[:, pair * HALF:(pair + 1) * HALF])
        if part != 1:
            r.v_out[1, pl.ds(part // 2, 1), :] = grad[width:width + 1]
    after(43)
    for pair in range(2):
        for n in range(items):
            attend_back(n, (2 * pair, 2 * pair + 1))
            after(50 + 10 * pair + n)
        rows = [r.gT[0, pl.ds(part * BLOCK + pair * HALF, HALF), :] for part in range(3)]
        grad = dot_nt(r.xT[...], jnp.concatenate(rows, axis=0))
        for part in range(3):
            columns = slice(part * HALF, (part + 1) * HALF)
            hold(WHOLE_UNITS + 3 * pair + part, grad[:width, columns])
            if part != 1:
                r.v_own[1, pl.ds(part // 2, 1), pair * HALF:(pair + 1) * HALF] = grad[width:width + 1, columns]
        after(53 + 10 * pair)

    for i in range(items):
        if i > 0:
            after(70 + i)
        acc = None
        for slot in range(2):
            for k in range(3):
                term = dot_nn(r.wqkv[slot, k], r.gT[slot, pl.ds(k * 256, 256), pl.ds(i * lanes, lanes)])
                acc = term if acc is None else acc + term
        r.ig_o[pl.ds(i * length, length), :] = acc.T[:length] + r.gp[pl.ds(i * rows_pad, length), :]
    after(73)
    wait_sent()


def hand_over(count, *refs):
    sems = refs[-1]
    copies = [pltpu.make_async_copy(refs[k], refs[count + k], sems.at[k]) for k in range(count)]
    for c in copies:
        c.start()
    for c in copies:
        c.wait()


def layer_by_items(
    inputs, region_counts, w_query, b_query, w_key, w_value, b_value, w_out, b_out, gain_one, shift_one,
    w_up, b_up, w_down, b_down, gain_two, shift_two, cotangent,
):
    total_rows, width = inputs.shape
    item_count = region_counts.shape[0]
    length = total_rows // item_count
    items = item_count // 2
    rows_pad = -(-length // ITEM_PAD) * ITEM_PAD
    lanes = -(-length // 128) * 128
    dp_size = lax.axis_size("dp")
    nz = dp_size // 4
    shard = width // dp_size
    total = items * rows_pad
    chunks = w_up.shape[1] // BLOCK
    own_rows = items * length

    two_chunks = 2 * chunks
    hd = w_query.shape[1]
    inner = [
        ("x_raw", (total_rows, width), BF), ("x_v", (total, width), BF),
        ("cot_raw", (total_rows - own_rows // 8 * 8 + 16, width), F32), ("cot", (total, width), F32),
        ("bias_q", (2, 1, BLOCK), F32), ("bias_v", (2, 1, BLOCK), F32), ("bias_u", (2, 1, chunks * BLOCK), F32),
        ("b_out", (1, width), F32), ("gain_one", (1, width), F32), ("shift_one", (1, width), F32),
        ("b_down", (1, width), F32), ("gain_two", (1, width), F32), ("shift_two", (1, width), F32),
        ("wqkv", (2, 3, width, hd), BF), ("wo", (2, hd, width), BF),
        ("wu", (two_chunks, width, BLOCK), BF), ("wd", (two_chunks, BLOCK, width), BF),
        ("xT", (width + 16, items * lanes), BF), ("hT", (width + 16, items * lanes), BF),
        ("dT", (width, items * lanes), BF), ("oT", (width, items * lanes), BF),
        ("keys", (2 * items, rows_pad, hd), BF), ("values", (2 * items, rows_pad, hd), BF),
        ("tra", (2 * items, 3, hd, lanes), BF), ("score", (8, rows_pad, lanes), F32),
        ("probs", (8 * items, lanes, lanes), BF), ("ctxT", (2, hd, items * lanes), BF),
        ("ctx", (2, total, hd), BF), ("n1", (total, width), F32), ("inv1", (total, 128), F32),
        ("hlow", (total, width), BF), ("slope", (two_chunks, total, BLOCK), BF),
        ("active", (two_chunks, items, lanes, BLOCK), BF), ("acc", (total, width), F32),
        ("work", (3, total, BLOCK), F32), ("own", (4, width, BLOCK), F32),
        ("gp", (total, width), F32),
        ("dlow", (total, width), BF), ("upg", (3, items, lanes, BLOCK), BF), ("olow", (items, lanes, width), BF),
        ("cgT", (2 * items, hd, lanes), BF), ("dscore", (8, lanes, lanes), BF), ("gT", (2, 3 * hd, items * lanes), BF),
        ("g_out", (WHOLE_UNITS, 16, shard, BLOCK), BF), ("g", (WHOLE_UNITS, 16, shard, BLOCK), BF),
        ("g_a", (WHOLE_UNITS, 8, shard, BLOCK), BF), ("g_b", (WHOLE_UNITS, 4, shard, BLOCK), BF),
        ("g_c", (WHOLE_UNITS, 3, shard, BLOCK), BF),
        ("h_out", (HALF_UNITS, 16, shard, HALF), BF), ("h", (HALF_UNITS, 16, shard, HALF), BF),
        ("h_a", (HALF_UNITS, 8, shard, HALF), BF), ("h_b", (HALF_UNITS, 4, shard, HALF), BF),
        ("h_c", (HALF_UNITS, 3, shard, HALF), BF),
        ("v_out", (2, 16, BLOCK), F32), ("v_own", (2, 16, BLOCK), F32),
        ("v_in", (2, 2 + nz, 16, BLOCK), F32), ("v_sum", (2, 3, 16, BLOCK), F32),
    ]
    n_weights = 8 + chunks
    sems = [
        ("in_sem", (16 + chunks,)), ("w_send", (n_weights,)), ("w_recv", (n_weights,)), ("sent", (4, 2)),
        ("core_recv", (UNITS,)), ("a_recv", (UNITS,)), ("b_recv", (UNITS,)), ("c_recv", (UNITS,)),
        ("v_send", (2, 4)), ("v_recv", (2, 4)),
    ]
    operands = [
        ("counts", region_counts), ("x_h", inputs), ("cot_h", cotangent), ("wq_h", w_query), ("wk_h", w_key),
        ("wv_h", w_value), ("wo_h", w_out), ("wu_h", w_up), ("wd_h", w_down.reshape(chunks, BLOCK, width)),
        ("b_query_h", b_query[None]), ("b_value_h", b_value[None]), ("b_up_h", b_up[None]), ("b_out_h", b_out[None]),
        ("gain_one_h", gain_one[None]), ("shift_one_h", shift_one[None]), ("b_down_h", b_down[None]),
        ("gain_two_h", gain_two[None]), ("shift_two_h", shift_two[None]),
    ]
    hidden = chunks * BLOCK
    results = [
        ("out_o", (own_rows, width), BF), ("ig_o", (own_rows, width), F32),
        ("gq_o", (shard, hd), F32), ("bq_o", (1, hd), F32),
        ("gk_o", (shard, hd), F32), ("gv_o", (shard, hd), F32),
        ("bv_o", (1, hd), F32), ("go_o", (shard, hd), F32),
        ("bout_o", (1, width), F32), ("gain1_o", (1, width), F32),
        ("shift1_o", (1, width), F32), ("gu_o", (shard, hidden), F32),
        ("bup_o", (1, hidden), F32), ("gd_o", (shard, hidden), F32),
        ("bdown_o", (1, width), F32), ("gain2_o", (1, width), F32),
        ("shift2_o", (1, width), F32),
    ]
    names = [n for n, _ in operands] + [n for n, *_ in results] + [n for n, *_ in inner] + [n for n, _ in sems]
    smem = pl.BlockSpec(memory_space=pltpu.SMEM)
    shapes = [jax.ShapeDtypeStruct(s, d) for _, s, d in results]
    made = pl.pallas_call(
        functools.partial(layer_kernel, (items, length, rows_pad, lanes, nz, shard), names),
        out_shape=[pltpu.VMEM(s, d) for _, s, d in results],
        in_specs=[smem] + [pl.BlockSpec(memory_space=pl.ANY)] * (len(operands) - 1),
        out_specs=[pl.BlockSpec(memory_space=pltpu.VMEM)] * len(results),
        scratch_shapes=[pltpu.VMEM(s, d) for _, s, d in inner] + [pltpu.SemaphoreType.DMA(s) for _, s in sems],
        compiler_params=pltpu.CompilerParams(
            collective_id=0, has_side_effects=True, vmem_limit_bytes=59 * 2**20),
        name="layer",
    )(*[v for _, v in operands])
    count = len(shapes)
    made = pl.pallas_call(
        functools.partial(hand_over, count),
        out_shape=shapes,
        in_specs=[pl.BlockSpec(memory_space=pltpu.VMEM)] * count,
        out_specs=[pl.BlockSpec(memory_space=pl.ANY)] * count,
        scratch_shapes=[pltpu.SemaphoreType.DMA((count,))],
        compiler_params=pltpu.CompilerParams(vmem_limit_bytes=2**20),
        name="hand_over",
    )(*[pltpu.with_memory_space_constraint(v, pltpu.VMEM) for v in made])
    made = [v.reshape(-1) if v.shape[0] == 1 else v for v in made]
    made[7], made[13] = made[7].T, made[13].T
    return tuple(made)


def solution(mesh):
    placed = (
        P("dp", None),
        P("dp"),
        P(None, "mp"),
        P("mp"),
        P(None, "mp"),
        P(None, "mp"),
        P("mp"),
        P("mp", None),
        P(),
        P(),
        P(),
        P(None, "mp"),
        P("mp"),
        P("mp", None),
        P(),
        P(),
        P(),
        P("dp", None),
    )
    dp_size, mp_size = mesh.shape["dp"], mesh.shape["mp"]

    def body(*args):
        width, hidden = args[0].shape[1], args[11].shape[1]
        whole_items = mp_size == 2 and args[1].shape[0] % 2 == 0
        even_shards = dp_size == 16 and width % (16 * dp_size) == 0
        blocks = args[2].shape[1] == BLOCK and width == 2 * BLOCK and hidden == 4 * BLOCK
        fits = args[0].shape[0] // args[1].shape[0] <= 256
        if whole_items and even_shards and blocks and fits:
            return layer_by_items(*args)
        return per_device(*args)

    return jax.shard_map(
        body,
        mesh=mesh,
        in_specs=placed,
        out_specs=(
            P(("dp", "mp"), None),
            P(("dp", "mp"), None),
            P("dp", "mp"),
            P("mp"),
            P("dp", "mp"),
            P("dp", "mp"),
            P("mp"),
            P("mp", "dp"),
            P(),
            P(),
            P(),
            P("dp", "mp"),
            P("mp"),
            P("mp", "dp"),
            P(),
            P(),
            P(),
        ),
        check_vma=False,
    )
```

```python
import functools
import types

import jax
import jax.numpy as jnp
from jax import lax
from jax.experimental import pallas as pl
from jax.experimental.pallas import tpu as pltpu
from jax.sharding import PartitionSpec as P

HEAD_DIM = 64
TEXT = 128


def layer_stats(pre_rows):
    row_mean = jnp.mean(pre_rows, axis=-1, keepdims=True)
    centred = pre_rows - row_mean
    inverse = lax.rsqrt(jnp.mean(centred * centred, axis=-1, keepdims=True) + 1e-12)
    return (centred * inverse, inverse)


def norm_back(grad_rows, normed, inverse, gain_vec):
    scaled = grad_rows * gain_vec
    return inverse * (
        scaled
        - jnp.mean(scaled, axis=-1, keepdims=True)
        - normed * jnp.mean(scaled * normed, axis=-1, keepdims=True)
    )


def gelu_slope(upper_part):
    return (
        0.5 * (1.0 + lax.erf(upper_part * 0.7071067811865476))
        + upper_part * jnp.exp(-0.5 * upper_part * upper_part) * 0.3989422804014327
    )


def contract_rows(first_op, second_op):
    return lax.dot_general(
        first_op, second_op, (((0,), (0,)), ((), ())), preferred_element_type=jnp.float32
    )


def times_transposed(first_op, second_op):
    return lax.dot_general(
        first_op, second_op, (((1,), (1,)), ((), ())), preferred_element_type=jnp.float32
    )


def per_device(
    inputs,
    region_counts,
    w_query,
    b_query,
    w_key,
    w_value,
    b_value,
    w_out,
    b_out,
    gain_one,
    shift_one,
    w_up,
    b_up,
    w_down,
    b_down,
    gain_two,
    shift_two,
    cotangent,
):
    total_rows = inputs.shape[0]
    item_count = region_counts.shape[0]
    length = total_rows // item_count
    heads_here = w_query.shape[1] // HEAD_DIM
    score_scale = HEAD_DIM ** (-0.5)
    share_rows = total_rows // lax.axis_size("mp")
    row_start = lax.axis_index("mp") * share_rows

    def own_rows(full_rows):
        return lax.dynamic_slice_in_dim(full_rows, row_start, share_rows, 0)

    def split_heads(flat_rows):
        return flat_rows.reshape(item_count, length, heads_here, HEAD_DIM)

    position = jnp.arange(length)
    visible = (position[None, :] < TEXT) | (position[None, :] - TEXT < region_counts[:, None])
    key_mask = visible[:, None, None, :]
    queries = (jnp.dot(inputs, w_query, preferred_element_type=jnp.float32) + b_query).astype(
        jnp.bfloat16
    )
    key_rows = jnp.dot(inputs, w_key, preferred_element_type=jnp.float32).astype(jnp.bfloat16)
    value_rows = (jnp.dot(inputs, w_value, preferred_element_type=jnp.float32) + b_value).astype(
        jnp.bfloat16
    )
    query_heads = split_heads(queries)
    key_heads = split_heads(key_rows)
    value_heads = split_heads(value_rows)

    def masked_scores():
        raw_scores = (
            jnp.einsum(
                "ishd,ithd->ihst", query_heads, key_heads, preferred_element_type=jnp.float32
            )
            * score_scale
        )
        return jnp.where(key_mask, raw_scores, -1000000000.0)

    scores = masked_scores()
    row_top = jnp.max(scores, axis=-1, keepdims=True)
    exponent = jnp.exp(scores - row_top)
    row_total = jnp.sum(exponent, axis=-1, keepdims=True)
    probs = exponent / row_total
    log_total = row_top + jnp.log(row_total)
    context = jnp.einsum(
        "ihst,ithd->ishd",
        probs.astype(jnp.bfloat16),
        value_heads,
        preferred_element_type=jnp.float32,
    )
    context = context.reshape(total_rows, heads_here * HEAD_DIM).astype(jnp.bfloat16)
    partial_attn = jnp.dot(context, w_out, preferred_element_type=jnp.float32)
    attended = lax.psum(partial_attn, "mp")
    normed_one, inverse_one = layer_stats(attended + b_out + inputs.astype(jnp.float32))
    hidden_one = normed_one * gain_one + shift_one
    hidden_low = hidden_one.astype(jnp.bfloat16)
    upper_part = jnp.dot(hidden_low, w_up, preferred_element_type=jnp.float32) + b_up
    active = jax.nn.gelu(upper_part, approximate=False).astype(jnp.bfloat16)
    partial_ffn = jnp.dot(active, w_down, preferred_element_type=jnp.float32)
    lowered = lax.psum(partial_ffn, "mp")
    normed_two, inverse_two = layer_stats(lowered + b_down + hidden_one)
    output = own_rows(normed_two * gain_two + shift_two).astype(jnp.bfloat16)
    grad_pre_two = norm_back(cotangent, normed_two, inverse_two, gain_two)
    down_low = grad_pre_two.astype(jnp.bfloat16)
    grad_output = own_rows(cotangent)
    normed_two_own = own_rows(normed_two)
    grad_two_own = own_rows(grad_pre_two)
    grad_gain_two = jnp.sum(grad_output * normed_two_own, axis=0)
    grad_shift_two = jnp.sum(grad_output, axis=0)
    grad_b_down = jnp.sum(grad_two_own, axis=0)
    grad_w_down = contract_rows(active, down_low)
    active_grad = times_transposed(down_low, w_down)
    upper_grad = (active_grad * gelu_slope(upper_part)).astype(jnp.bfloat16)
    grad_b_up = jnp.sum(upper_grad.astype(jnp.float32), axis=0)
    grad_w_up = contract_rows(hidden_low, upper_grad)
    partial_hidden = times_transposed(upper_grad, w_up)
    hidden_grad = lax.psum(partial_hidden, "mp") + grad_pre_two
    grad_pre_one = norm_back(hidden_grad, normed_one, inverse_one, gain_one)
    out_low = grad_pre_one.astype(jnp.bfloat16)
    hidden_grad_own = own_rows(hidden_grad)
    normed_one_own = own_rows(normed_one)
    grad_one_own = own_rows(grad_pre_one)
    grad_gain_one = jnp.sum(hidden_grad_own * normed_one_own, axis=0)
    grad_shift_one = jnp.sum(hidden_grad_own, axis=0)
    grad_b_out = jnp.sum(grad_one_own, axis=0)
    grad_w_out = contract_rows(context, out_low)
    context_grad = split_heads(times_transposed(out_low, w_out).astype(jnp.bfloat16))
    probs_again = jnp.exp(masked_scores() - log_total)
    prob_grad = jnp.einsum(
        "ishd,ithd->ihst", context_grad, value_heads, preferred_element_type=jnp.float32
    )
    row_inner = jnp.sum(probs_again * prob_grad, axis=-1, keepdims=True)
    score_grad = (probs_again * (prob_grad - row_inner)).astype(jnp.bfloat16)
    query_grad = (
        (
            jnp.einsum("ihst,ithd->ishd", score_grad, key_heads, preferred_element_type=jnp.float32)
            * score_scale
        )
        .astype(jnp.bfloat16)
        .reshape(total_rows, heads_here * HEAD_DIM)
    )
    key_grad = (
        (
            jnp.einsum(
                "ihst,ishd->ithd", score_grad, query_heads, preferred_element_type=jnp.float32
            )
            * score_scale
        )
        .astype(jnp.bfloat16)
        .reshape(total_rows, heads_here * HEAD_DIM)
    )
    value_grad = jnp.einsum(
        "ihst,ishd->ithd",
        probs_again.astype(jnp.bfloat16),
        context_grad,
        preferred_element_type=jnp.float32,
    ).astype(jnp.bfloat16)
    value_grad = value_grad.reshape(total_rows, heads_here * HEAD_DIM)
    grad_b_query = jnp.sum(query_grad.astype(jnp.float32), axis=0)
    grad_b_value = jnp.sum(value_grad.astype(jnp.float32), axis=0)
    grad_w_query = contract_rows(inputs, query_grad)
    grad_w_key = contract_rows(inputs, key_grad)
    grad_w_value = contract_rows(inputs, value_grad)
    partial_input = (
        times_transposed(query_grad, w_query)
        + times_transposed(key_grad, w_key)
        + times_transposed(value_grad, w_value)
    )
    input_grad = own_rows(
        lax.psum(partial_input.astype(jnp.bfloat16), "mp").astype(jnp.float32) + grad_pre_one
    )
    bias_sums = lax.psum((grad_b_query, grad_b_value, grad_b_up), "dp")
    norm_sums = lax.psum(
        (grad_b_out, grad_gain_one, grad_shift_one, grad_b_down, grad_gain_two, grad_shift_two),
        ("dp", "mp"),
    )
    weight_sums = (
        lax.psum_scatter(
            grad_w_query.astype(jnp.bfloat16), "dp", scatter_dimension=0, tiled=True
        ).astype(jnp.float32),
        lax.psum_scatter(
            grad_w_key.astype(jnp.bfloat16), "dp", scatter_dimension=0, tiled=True
        ).astype(jnp.float32),
        lax.psum_scatter(
            grad_w_value.astype(jnp.bfloat16), "dp", scatter_dimension=0, tiled=True
        ).astype(jnp.float32),
        lax.psum_scatter(
            grad_w_out.astype(jnp.bfloat16), "dp", scatter_dimension=1, tiled=True
        ).astype(jnp.float32),
        lax.psum_scatter(
            grad_w_up.astype(jnp.bfloat16), "dp", scatter_dimension=0, tiled=True
        ).astype(jnp.float32),
        lax.psum_scatter(
            grad_w_down.astype(jnp.bfloat16), "dp", scatter_dimension=1, tiled=True
        ).astype(jnp.float32),
    )
    return (
        output,
        input_grad,
        weight_sums[0],
        bias_sums[0],
        weight_sums[1],
        weight_sums[2],
        bias_sums[1],
        weight_sums[3],
        norm_sums[0],
        norm_sums[1],
        norm_sums[2],
        weight_sums[4],
        bias_sums[2],
        weight_sums[5],
        norm_sums[3],
        norm_sums[4],
        norm_sums[5],
    )


ITEM_PAD = 16
MESH = pl.DeviceIdType.MESH
BF = jnp.bfloat16
F32 = jnp.float32
BLOCK = 256
HALF = 128
WHOLE_UNITS, HALF_UNITS = 9, 6
UNITS = WHOLE_UNITS + HALF_UNITS
X_FIRST, Y_FIRST, Z_FIRST = 0, 1, 2
ORDER = (0, 1, 2, 0, 1, 2, 0, 1, 0, 1, 0, 1, 0, 1, 0)
PLAN = {
    13: (('M', 0, 1, 2, 3),),
    14: (('A', 0, 1),),
    21: (('M', 4, 5),),
    23: (('M', 6, 7),),
    24: (('A', 4),),
    25: (('A', 5),),
    26: (('B', 0, 1), ('A', 6),),
    27: (('B', 2), ('A', 7),),
    31: (('M', 8), ('D', -1), ('B', 3, 4),),
    41: (('D', 0), ('A', 8), ('C', 0, 1), ('B', 5),),
    43: (('M', 9, 10, 11, 12, 13, 14), ('E', -1), ('C', 2),),
    51: (('C', 4), ('B', 6),),
    53: (('D', 1), ('A', 9, 10, 11),),
    63: (('E', 0), ('B', 8, 7), ('A', 12, 13, 14), ('C', 3, 6, 5),),
    71: (('D', 2), ('B', 9, 10),),
    72: (('B', 11), ('C', 7, 8),),
    73: (('E', 1), ('B', 12, 13, 14), ('F', 0, 1, 2), ('C', 9, 10, 11), ('E', 2), ('D', 3), ('F', 3, 4), ('C', 12, 13, 14), ('F', 5, 6, 7, 8), ('F', 9, 10, 11, 12, 13, 14), ('E', 3), ('D', 4), ('E', 4),),
    20: (('A', 2, 3),),
}


def dot_nn(a, b):
    return lax.dot_general(a, b, (((1,), (0,)), ((), ())), preferred_element_type=F32)


def dot_nt(a, b):
    return lax.dot_general(a, b, (((1,), (1,)), ((), ())), preferred_element_type=F32)


def layer_kernel(dims, names, *refs):
    r = types.SimpleNamespace(**dict(zip(names, refs, strict=True)))
    items, length, rows_pad, lanes, nz, shard = dims
    total = items * rows_pad
    chunks = r.wu_h.shape[1] // BLOCK
    width = r.x_h.shape[1]
    dp, mp = lax.axis_index("dp"), lax.axis_index("mp")
    z, y, x = dp // 4, (dp // 2) % 2, dp % 2

    def at(z_, y_, x_):
        return z_ * 4 + y_ * 2 + x_

    core = (dp, 1 - mp)
    x_side = (at(z, y, 1 - x), mp)
    y_side = (at(z, 1 - y, x), mp)
    z_side = [(at((z + step) % nz, y, x), mp) for step in range(1, nz)]
    low_side = (at(z + 1 - 2 * (z % 2), y, x), mp)
    high_side = z_side[1]
    plane_side = [(at(z, (y + step // 2) % 2, (x + step) % 2), mp) for step in range(1, 4)]

    local = []

    def bring(src, dst):
        copy = pltpu.make_async_copy(src, dst, r.in_sem.at[len(local)])
        copy.start()
        local.append(copy)
        return copy

    c_x = bring(r.x_h, r.x_raw)
    c_w = [bring(src, r.wqkv.at[0, k]) for k, src in enumerate((r.wq_h, r.wk_h, r.wv_h))]
    c_p = [bring(r.b_query_h, r.bias_q.at[0]), bring(r.b_value_h, r.bias_v.at[0]), bring(r.b_up_h, r.bias_u.at[0])]

    barrier = pltpu.get_barrier_semaphore()
    near = [core] + plane_side + z_side
    for device in near:
        pl.semaphore_signal(barrier, inc=1, device_id=device, device_id_type=MESH)
    vectors = (
        (r.b_out_h, r.b_out), (r.gain_one_h, r.gain_one), (r.shift_one_h, r.shift_one),
        (r.b_down_h, r.b_down), (r.gain_two_h, r.gain_two), (r.shift_two_h, r.shift_two))
    c_vec = [bring(src, dst) for src, dst in vectors]
    c_wo = bring(r.wo_h, r.wo.at[0])
    c_wu = [bring(r.wu_h.at[:, pl.ds(c * BLOCK, BLOCK)], r.wu.at[c]) for c in range(chunks)]
    c_wd = bring(r.wd_h, r.wd.at[pl.ds(0, chunks)])
    full_rows = r.x_h.shape[0]
    base = items * length // 8 * 8
    cot_count = full_rows - base
    c_cot = bring(r.cot_h.at[pl.ds(pl.multiple_of(mp * base, 8), cot_count)], r.cot_raw.at[pl.ds(0, cot_count)])

    pad_rows = lanes - rows_pad

    def transposed(block):
        full = jnp.concatenate([block, jnp.zeros((pad_rows, block.shape[1]), F32)], axis=0)
        return full.T.astype(BF)

    def rows_of(i):
        return pl.ds(pl.multiple_of(i * rows_pad, 16), rows_pad)

    def lanes_of(i):
        return pl.ds(pl.multiple_of(i * lanes, lanes), lanes)

    def greet():
        pl.semaphore_wait(barrier, len(near))

    def clear(n, carry):
        r.probs[n, pl.ds(rows_pad, pad_rows), :] = jnp.zeros((pad_rows, lanes), BF)
        return carry

    lax.fori_loop(0, r.probs.shape[0], clear, 0)
    zero_block = jnp.zeros((pad_rows, BLOCK), BF)
    for i in range(items):
        r.olow[i, pl.ds(rows_pad, pad_rows), :] = jnp.zeros((pad_rows, width), BF)
        for j in range(r.upg.shape[0]):
            r.upg[j, i, pl.ds(rows_pad, pad_rows), :] = zero_block
        for j in range(2 * chunks):
            r.active[j, i, pl.ds(rows_pad, pad_rows), :] = zero_block
    for k in range(r.dscore.shape[0]):
        r.dscore[k, pl.ds(rows_pad, pad_rows), :] = jnp.zeros((pad_rows, lanes), BF)
    one_row = jnp.where(lax.broadcasted_iota(jnp.int32, (16, items * lanes), 0) == 0, 1.0, 0.0).astype(BF)
    r.xT[pl.ds(width, 16), :] = one_row
    r.hT[pl.ds(width, 16), :] = one_row
    cot_rows = r.cot_raw.shape[0]
    r.cot_raw[pl.ds(cot_count, cot_rows - cot_count), :] = jnp.zeros((cot_rows - cot_count, width), F32)

    c_x.wait()
    down_ = lax.broadcasted_iota(jnp.int32, (rows_pad, 256), 0)
    across = lax.broadcasted_iota(jnp.int32, (rows_pad, 256), 1)
    for i in range(items):
        block = None
        for m in range(2):
            start = (m * items + i) * length
            window = start // 16 * 16
            count = min(256, full_rows - window)
            shift = jnp.where(mp == m, start - window, 2 * 256)
            pick = jnp.where((across == down_ + shift) & (down_ < length), 1.0, 0.0).astype(BF)
            term = dot_nn(pick[:, :count], r.x_raw[pl.ds(window, count), :])
            block = term if block is None else block + term
        r.x_v[rows_of(i), :] = block.astype(BF)

    greet()

    remote = []

    def send_weight(src, dst):
        k = len(remote)
        copy = pltpu.make_async_remote_copy(
            src_ref=src, dst_ref=dst, send_sem=r.w_send.at[k], recv_sem=r.w_recv.at[k],
            device_id=core, device_id_type=MESH)
        copy.start()
        remote.append(copy)
        return copy

    s_w = [send_weight(src, r.wqkv.at[1, k]) for k, src in enumerate((r.wq_h, r.wk_h, r.wv_h))]
    s_w += [send_weight(src, dst.at[1]) for src, dst in (
        (r.b_query_h, r.bias_q), (r.b_value_h, r.bias_v), (r.b_up_h, r.bias_u))]
    s_wo = send_weight(r.wo_h, r.wo.at[1])
    s_wu = [send_weight(r.wu_h.at[:, pl.ds(c * BLOCK, BLOCK)], r.wu.at[chunks + c]) for c in range(chunks)]
    s_wd = send_weight(r.wd_h, r.wd.at[pl.ds(chunks, chunks)])

    def project(slot, k):
        r.work[k] = dot_nn(r.x_v[...], r.wqkv[slot, k])

    def keep(slot, k):
        for i in range(items):
            block = r.work[k, pl.ds(i * rows_pad, rows_pad), :]
            n = slot * items + i
            if k == 0:
                r.tra[n, 0] = transposed((block + r.bias_q[slot]) * 0.125)
            elif k == 1:
                r.keys[n] = block.astype(BF)
            else:
                block = block + r.bias_v[slot]
                r.values[n] = block.astype(BF)
                r.tra[n, 2] = transposed(block)

    for c in c_w + c_p:
        c.wait()
    for k in range(3):
        project(0, k)
    for k in range(3):
        keep(0, k)
    lane = lax.broadcasted_iota(jnp.int32, (1, 128), 1)
    half = [jnp.where(lane < 64, 1.0, 0.0).astype(BF), jnp.where(lane >= 64, 1.0, 0.0).astype(BF)]
    position = lax.broadcasted_iota(jnp.int32, (rows_pad, lanes), 0)

    def pair_of(h):
        return slice((h // 2) * 128, (h // 2) * 128 + 128)

    def head_of(h):
        return slice(h * 64, (h + 1) * 64)

    def scores_of(n):
        for h in range(4):
            r.score[(n % 2) * 4 + h] = dot_nn(r.keys[n, :, pair_of(h)] * half[h % 2], r.tra[n, 0, pair_of(h), :])

    def soften(n):
        mask = jnp.where(position < TEXT + r.counts[mp * items + n % items], 0.0, -1e9)
        for h in range(4):
            score = r.score[(n % 2) * 4 + h] + mask
            top = jnp.max(score, axis=0, keepdims=True)
            e = jnp.exp(score - top)
            p = e * (1.0 / jnp.sum(e, axis=0, keepdims=True))
            r.probs[n * 4 + h, pl.ds(0, rows_pad), :] = p.astype(BF)

    def contexts_of(n):
        parts = [dot_nn(r.tra[n, 2, head_of(h), :], r.probs[n * 4 + h]) for h in range(4)]
        context = jnp.concatenate(parts, axis=0)
        slot, i = n // items, n % items
        r.ctxT[slot, :, pl.ds(i * lanes, lanes)] = context.astype(BF)
        r.ctx[slot, pl.ds(i * rows_pad, rows_pad), :] = context.T[:rows_pad].astype(BF)

    scores_of(0)
    for n in range(2 * items):
        if n + 1 == items:
            soften(n)
            for c in s_w:
                c.wait_recv()
            for k in range(3):
                project(1, k)
            contexts_of(n)
            for k in range(3):
                keep(1, k)
            scores_of(n + 1)
            continue
        if n + 1 < 2 * items:
            scores_of(n + 1)
        soften(n)
        contexts_of(n)

    c_wo.wait()
    s_wo.wait_recv()
    for c in c_vec:
        c.wait()

    def attended(i):
        rows = pl.ds(i * rows_pad, rows_pad)
        r.acc[rows, :] = dot_nn(r.ctx[0, rows, :], r.wo[0]) + dot_nn(r.ctx[1, rows, :], r.wo[1])

    def first_norm(i):
        rows = pl.ds(i * rows_pad, rows_pad)
        pre = r.acc[rows, :] + r.b_out[...] + r.x_v[rows, :].astype(F32)
        centred = pre - jnp.mean(pre, axis=1, keepdims=True)
        inverse = lax.rsqrt(jnp.mean(centred * centred, axis=1, keepdims=True) + 1e-12)
        normed = centred * inverse
        r.n1[rows, :] = normed
        r.inv1[rows, :] = jnp.broadcast_to(inverse, (rows_pad, 128))
        r.hlow[rows, :] = (normed * r.gain_one[...] + r.shift_one[...]).astype(BF)

    for i in range(items):
        attended(i)
    for i in range(items):
        first_norm(i)

    for c in c_wu + [c_wd]:
        c.wait()
    for c in s_wu + [s_wd]:
        c.wait_recv()
    c_cot.wait()
    valid = lax.broadcasted_iota(jnp.int32, (rows_pad, 1), 0) < length

    def own_cotangent(i):
        at_ = [r.cot_raw[pl.ds(m * (items * length - base) + i * length, rows_pad), :] for m in range(2)]
        r.cot[pl.ds(i * rows_pad, rows_pad), :] = jnp.where(valid, jnp.where(mp == 0, at_[0], at_[1]), 0.0)

    def lift(j):
        slot, c = j // chunks, j % chunks
        r.work[j % 2] = dot_nn(r.hlow[...], r.wu[j]) + r.bias_u[slot, :, c * BLOCK:(c + 1) * BLOCK]

    def activate(j):
        for i in range(items):
            rows = pl.ds(i * rows_pad, rows_pad)
            u = r.work[j % 2, rows, :]
            phi = 0.5 + 0.5 * lax.erf(u * 0.7071067811865476)
            r.slope[j, rows, :] = (phi + u * (jnp.exp(-0.5 * u * u) * 0.3989422804014327)).astype(BF)
            r.active[j, i, pl.ds(0, rows_pad), :] = (u * phi).astype(BF)

    def lower(j):
        part = dot_nn(r.active[j][:, :rows_pad].reshape(total, BLOCK), r.wd[j])
        if j == 0:
            r.acc[...] = part
        else:
            r.acc[...] += part

    lift(0)
    for j in range(2 * chunks):
        if j > 0:
            lower(j - 1)
        if j + 1 < 2 * chunks:
            lift(j + 1)
        activate(j)
        if 2 <= j < 2 + items:
            own_cotangent(j - 2)
    lower(2 * chunks - 1)

    def mean(v):
        return jnp.mean(v, axis=1, keepdims=True)

    def column_sum(v):
        return jnp.sum(v, axis=0, keepdims=True)

    gain2, shift2, bdown = [], [], []

    def second_norm(i):
        rows = pl.ds(i * rows_pad, rows_pad)
        hidden = r.n1[rows, :] * r.gain_one[...] + r.shift_one[...]
        pre = r.acc[rows, :] + r.b_down[...] + hidden
        centred = pre - mean(pre)
        inverse = lax.rsqrt(mean(centred * centred) + 1e-12)
        normed = centred * inverse
        cot = r.cot[rows, :]
        g = cot * r.gain_two[...]
        grad = inverse * (g - mean(g) - normed * mean(g * normed))
        r.gp[rows, :] = grad
        r.dlow[rows, :] = grad.astype(BF)
        r.dT[:, pl.ds(i * lanes, lanes)] = transposed(grad)
        r.acc[pl.ds(i * length, rows_pad), :] = normed * r.gain_two[...] + r.shift_two[...]
        gain2.append(column_sum(cot * normed))
        shift2.append(column_sum(cot))
        bdown.append(column_sum(grad))

    for i in range(items):
        second_norm(i)

    def held(u):
        if u < WHOLE_UNITS:
            return [ref.at[u] for ref in (r.g_out, r.g, r.g_a, r.g_b, r.g_c)]
        return [ref.at[u - WHOLE_UNITS] for ref in (r.h_out, r.h, r.h_a, r.h_b, r.h_c)]

    def size_of(u):
        return 0 if u < WHOLE_UNITS else 1

    def to_core(u):
        return pltpu.make_async_remote_copy(
            src_ref=held(u)[0], dst_ref=held(u)[1], send_sem=r.sent.at[0, size_of(u)],
            recv_sem=r.core_recv.at[u], device_id=core, device_id_type=MESH)

    route = (
        (x, y, z, x_side, y_side), (y, x, z, y_side, x_side), (z % 2, z // 2, y * 2 + x, low_side, high_side))

    def shard_order(order):
        if order == X_FIRST:
            return [at(c, b, a) for a in range(2) for b in range(2) for c in range(nz)]
        if order == Y_FIRST:
            return [at(c, a, b) for a in range(2) for b in range(2) for c in range(nz)]
        return [at(2 * b + a, c, d) for a in range(2) for b in range(2) for c in range(2) for d in range(2)]

    def stage_a(u, order):
        first, _, _, device, _ = route[order]
        return pltpu.make_async_remote_copy(
            src_ref=held(u)[1].at[pl.ds((1 - first) * 8, 8)], dst_ref=held(u)[2], send_sem=r.sent.at[1, size_of(u)],
            recv_sem=r.a_recv.at[u], device_id=device, device_id_type=MESH)

    def stage_b(u, order):
        first, second, _, _, device = route[order]
        return pltpu.make_async_remote_copy(
            src_ref=held(u)[1].at[pl.ds(first * 8 + (1 - second) * 4, 4)], dst_ref=held(u)[3], send_sem=r.sent.at[2, size_of(u)],
            recv_sem=r.b_recv.at[u], device_id=device, device_id_type=MESH)

    def wait_spread(u):
        came = held(u)[4]
        pltpu.make_async_remote_copy(
            src_ref=came, dst_ref=came, send_sem=r.sent.at[3, size_of(u)], recv_sem=r.c_recv.at[u],
            device_id=core, device_id_type=MESH).wait_recv()

    def wait_sent():
        for size, bufs in enumerate(((r.g_out, r.g_a, r.g_b, r.g_c), (r.h_out, r.h_a, r.h_b, r.h_c))):
            for stage, ref in enumerate(bufs):
                pltpu.make_async_remote_copy(
                    src_ref=ref, dst_ref=ref, send_sem=r.sent.at[stage, size], recv_sem=r.core_recv.at[0],
                    device_id=core, device_id_type=MESH).wait_send()

    def stage_c(u, order, step):
        first, second, _, _, _ = route[order]
        if order in (X_FIRST, Y_FIRST):
            place, device = (z + step) % nz, z_side[step - 1]
        else:
            place, device = ((y + step // 2) % 2) * 2 + (x + step) % 2, plane_side[step - 1]
        return pltpu.make_async_remote_copy(
            src_ref=held(u)[1].at[first * 8 + second * 4 + place], dst_ref=held(u)[4].at[step - 1],
            send_sem=r.sent.at[3, size_of(u)], recv_sem=r.c_recv.at[u],
            device_id=device, device_id_type=MESH)

    def lay_out(u, value):
        ref = held(u)[0]
        for place, block in enumerate(shard_order(ORDER[u])):
            ref[place] = value[block * shard:(block + 1) * shard].astype(BF)

    def start_core(u):
        to_core(u).start()

    def hold(u, value):
        r.own[u % r.own.shape[0], :, :value.shape[1]] = value

    def start_a(u):
        to_core(u).wait_recv()
        ref = held(u)[1]
        for place, block in enumerate(shard_order(ORDER[u])):
            mine = r.own[u % r.own.shape[0], pl.ds(block * shard, shard), :ref.shape[-1]]
            ref[place] = (mine + ref[place].astype(F32)).astype(BF)
        stage_a(u, ORDER[u]).start()

    def start_b(u):
        order = ORDER[u]
        stage_a(u, order).wait_recv()
        kept = pl.ds(route[order][0] * 8, 8)
        _, ref, came, _, _ = held(u)
        ref[kept] = ref[kept] + came[...]
        stage_b(u, order).start()

    def start_c(u):
        order = ORDER[u]
        stage_b(u, order).wait_recv()
        kept = pl.ds(route[order][0] * 8 + route[order][1] * 4, 4)
        _, ref, _, came, _ = held(u)
        ref[kept] = ref[kept] + came[...]
        for step in range(1, 4):
            stage_c(u, order, step).start()

    def finish(u):
        order = ORDER[u]
        first, second, third, _, _ = route[order]
        _, ref, _, _, came = held(u)
        acc = ref[first * 8 + second * 4 + third].astype(F32)
        wait_spread(u)
        for step in range(1, 4):
            acc += came[step - 1].astype(F32)
        return acc

    def vec_copy(k, stage, src, device):
        group = min(stage, 3)
        return pltpu.make_async_remote_copy(
            src_ref=src, dst_ref=r.v_in.at[k, stage], send_sem=r.v_send.at[k, group],
            recv_sem=r.v_recv.at[k, group], device_id=device, device_id_type=MESH)

    def vec_spread(k):
        came = r.v_in.at[k, pl.ds(3, nz - 1)]
        return pltpu.make_async_remote_copy(
            src_ref=came, dst_ref=came, send_sem=r.v_send.at[k, 3], recv_sem=r.v_recv.at[k, 3],
            device_id=core, device_id_type=MESH)

    def vec_core(k):
        return vec_copy(k, 0, r.v_out.at[k], core)

    def vec_side(k, stage):
        return vec_copy(k, stage, r.v_sum.at[k, stage - 1], (x_side, y_side)[stage - 1])

    def vec_z(k, step):
        return vec_copy(k, 2 + step, r.v_sum.at[k, 2], z_side[step - 1])

    def vec_next(k, stage):
        if stage == 0:
            vec_core(k).wait_recv()
            r.v_sum[k, 0] = r.v_own[k] + r.v_in[k, 0]
            vec_side(k, 1).start()
        elif stage == 1:
            vec_side(k, 1).wait_recv()
            r.v_sum[k, 1] = r.v_sum[k, 0] + r.v_in[k, 1]
            vec_side(k, 2).start()
        elif stage == 2:
            vec_side(k, 2).wait_recv()
            r.v_sum[k, 2] = r.v_sum[k, 1] + r.v_in[k, 2]
            for step in range(1, nz):
                vec_z(k, step).start()
        else:
            vec_spread(k).wait_recv()
            terms = [r.v_sum[k, 2]] + [r.v_in[k, 2 + step] for step in range(1, nz)]
            acc = jnp.zeros(terms[0].shape, F32)
            for zz in range(nz):
                came = lax.rem(z - zz + nz, nz)
                term = terms[0]
                for step in range(1, nz):
                    term = jnp.where(came == step, terms[step], term)
                acc = acc + term
            if k == 0:
                for j, ref in enumerate((r.bout_o, r.gain1_o, r.shift1_o, r.bdown_o, r.gain2_o, r.shift2_o)):
                    for part in range(2):
                        ref[:, part * BLOCK:(part + 1) * BLOCK] = acc[2 * j + part:2 * j + part + 1]
                for c in range(chunks):
                    r.bup_o[:, c * BLOCK:(c + 1) * BLOCK] = acc[12 + c:13 + c]
            else:
                r.bq_o[...] = acc[0:1]
                r.bv_o[...] = acc[1:2]

    def store_sum(u):
        total_ = finish(u)
        if u < 2 * chunks:
            column = u % chunks * BLOCK
            (r.gd_o, r.gu_o)[u // chunks][:, column:column + BLOCK] = total_
        elif u < WHOLE_UNITS:
            r.go_o[...] = total_
        else:
            column = (u - WHOLE_UNITS) // 3 * HALF
            (r.gq_o, r.gk_o, r.gv_o)[(u - WHOLE_UNITS) % 3][:, column:column + HALF] = total_

    def sums(k):
        def step(stage):
            if stage == 4:
                vec_core(k).wait_send()
                vec_side(k, 1).wait_send()
                vec_side(k, 2).wait_send()
                vec_spread(k).wait_send()
            elif stage < 0:
                vec_core(k).start()
            else:
                vec_next(k, stage)

        return step

    steps = dict(M=start_core, A=start_a, B=start_b, C=start_c, F=store_sum, D=sums(0), E=sums(1))

    def after(piece):
        for step, *units in PLAN.get(piece, ()):
            for u in units:
                steps[step](u)

    def down_grad(j):
        return dot_nn(r.dT[...], r.active[j].reshape(items * lanes, BLOCK))

    def active_grad(j):
        r.work[j % 2] = dot_nt(r.dlow[...], r.wd[j])

    def upper_grad(j):
        for i in range(items):
            rows = pl.ds(i * rows_pad, rows_pad)
            r.upg[j % 3, i, pl.ds(0, rows_pad), :] = (r.work[j % 2, rows, :] * r.slope[j, rows, :].astype(F32)).astype(BF)

    def up_grad(j):
        return dot_nn(r.hT[...], r.upg[j % 3].reshape(items * lanes, BLOCK))

    def hidden_grad(j):
        r.gp[...] += dot_nt(r.upg[j % 3][:, :rows_pad].reshape(total, BLOCK), r.wu[j])

    def turn(i):
        rows = pl.ds(i * rows_pad, rows_pad)
        r.hT[pl.ds(0, width), pl.ds(i * lanes, lanes)] = transposed(r.hlow[rows, :].astype(F32))

    def turn_input(i):
        rows = pl.ds(i * rows_pad, rows_pad)
        r.xT[pl.ds(0, width), pl.ds(i * lanes, lanes)] = transposed(r.x_v[rows, :].astype(F32))

    def turn_keys(n):
        r.tra[n, 1] = transposed(r.keys[n].astype(F32) * 0.125)

    for c in range(chunks):
        lay_out(c, down_grad(chunks + c))
        after(10 + c)
    for c in range(chunks):
        hold(c, down_grad(c))
        if c < items:
            turn(c)
    r.out_o[...] = r.acc[pl.ds(0, items * length), :].astype(BF)
    order = list(range(chunks, 2 * chunks)) + list(range(chunks))
    active_grad(order[0])
    after(14)
    for k, j in enumerate(order):
        if k + 1 < 2 * chunks:
            active_grad(order[k + 1])
        upper_grad(j)
        up = up_grad(j)
        c = j % chunks
        if j >= chunks:
            lay_out(chunks + c, up)
            r.v_out[0, pl.ds(12 + c, 1), :] = up[width:width + 1]
        else:
            hold(chunks + c, up[:width])
            r.v_own[0, pl.ds(12 + c, 1), :] = up[width:width + 1]
        hidden_grad(j)
        if k < 2 * items:
            turn_keys(k)
        else:
            turn_input(k - 2 * items)
        after(20 + k)
    turn_input(2)

    bout, gain1, shift1 = [], [], []

    def first_back(i):
        rows = pl.ds(i * rows_pad, rows_pad)
        hidden = r.gp[rows, :]
        normed = r.n1[rows, :]
        inverse = r.inv1[rows, :][:, :1]
        g = hidden * r.gain_one[...]
        grad = inverse * (g - mean(g) - normed * mean(g * normed))
        r.gp[rows, :] = grad
        r.olow[i, pl.ds(0, rows_pad), :] = grad.astype(BF)
        r.oT[:, pl.ds(i * lanes, lanes)] = transposed(grad)
        bout.append(column_sum(grad))
        gain1.append(column_sum(hidden * normed))
        shift1.append(column_sum(hidden))

    for i in range(items):
        first_back(i)
    for k, v in enumerate((bout, gain1, shift1, bdown, gain2, shift2)):
        v = sum(v[1:], v[0])
        for part in range(2):
            piece = v[:, part * BLOCK:(part + 1) * BLOCK]
            r.v_out[0, pl.ds(2 * k + part, 1), :] = piece
            r.v_own[0, pl.ds(2 * k + part, 1), :] = piece
    after(30)

    lay_out(8, dot_nt(r.oT[...], r.ctxT[1]))
    for n in [*range(items, 2 * items), *range(items)]:
        r.cgT[n] = dot_nt(r.wo[n // items], r.olow[n % items]).astype(BF)
    hold(8, dot_nt(r.oT[...], r.ctxT[0]))
    after(31)

    def probs_grad(n, heads):
        for h in heads:
            r.score[(n % 2) * 4 + h] = dot_nn(r.values[n, :, pair_of(h)] * half[h % 2], r.cgT[n, pair_of(h), :])

    def store_grad(n, k, h, value):
        r.gT[n // items, pl.ds(k * 256 + h * 64, 64), pl.ds((n % items) * lanes, lanes)] = value.astype(BF)

    def value_grad(n, heads):
        for h in heads:
            store_grad(n, 2, h, dot_nt(r.cgT[n, head_of(h), :], r.probs[n * 4 + h]))

    def score_grad(n, heads):
        for h in heads:
            pg = r.score[(n % 2) * 4 + h]
            p = r.probs[n * 4 + h, pl.ds(0, rows_pad), :].astype(F32)
            inner = jnp.sum(p * pg, axis=0, keepdims=True)
            r.dscore[(n % 2) * 4 + h, pl.ds(0, rows_pad), :] = (p * (pg - inner)).astype(BF)

    def query_key_grad(n, heads):
        for h in heads:
            ds = r.dscore[(n % 2) * 4 + h]
            store_grad(n, 0, h, dot_nn(r.tra[n, 1, head_of(h), :], ds))
            store_grad(n, 1, h, dot_nt(r.tra[n, 0, head_of(h), :], ds))

    def projection_grad(slot, k):
        return dot_nt(r.xT[...], r.gT[slot, pl.ds(k * 256, 256), :])

    for s in remote:
        s.wait_send()

    def attend_back(n, heads):
        probs_grad(n, heads)
        value_grad(n, heads)
        score_grad(n, heads)
        query_key_grad(n, heads)

    for n in range(items, 2 * items):
        attend_back(n, range(4))
        after(40 + n - items)
    for part in range(3):
        grad = projection_grad(1, part)
        for pair in range(2):
            lay_out(WHOLE_UNITS + 3 * pair + part, grad[:, pair * HALF:(pair + 1) * HALF])
        if part != 1:
            r.v_out[1, pl.ds(part // 2, 1), :] = grad[width:width + 1]
    after(43)
    for pair in range(2):
        for n in range(items):
            attend_back(n, (2 * pair, 2 * pair + 1))
            after(50 + 10 * pair + n)
        rows = [r.gT[0, pl.ds(part * BLOCK + pair * HALF, HALF), :] for part in range(3)]
        grad = dot_nt(r.xT[...], jnp.concatenate(rows, axis=0))
        for part in range(3):
            columns = slice(part * HALF, (part + 1) * HALF)
            hold(WHOLE_UNITS + 3 * pair + part, grad[:width, columns])
            if part != 1:
                r.v_own[1, pl.ds(part // 2, 1), pair * HALF:(pair + 1) * HALF] = grad[width:width + 1, columns]
        after(53 + 10 * pair)

    for i in range(items):
        if i > 0:
            after(70 + i)
        acc = None
        for slot in range(2):
            for k in range(3):
                term = dot_nn(r.wqkv[slot, k], r.gT[slot, pl.ds(k * 256, 256), pl.ds(i * lanes, lanes)])
                acc = term if acc is None else acc + term
        r.ig_o[pl.ds(i * length, length), :] = acc.T[:length] + r.gp[pl.ds(i * rows_pad, length), :]
    after(73)
    wait_sent()


def hand_over(count, *refs):
    sems = refs[-1]
    copies = [pltpu.make_async_copy(refs[k], refs[count + k], sems.at[k]) for k in range(count)]
    for c in copies:
        c.start()
    for c in copies:
        c.wait()


def layer_by_items(
    inputs, region_counts, w_query, b_query, w_key, w_value, b_value, w_out, b_out, gain_one, shift_one,
    w_up, b_up, w_down, b_down, gain_two, shift_two, cotangent,
):
    total_rows, width = inputs.shape
    item_count = region_counts.shape[0]
    length = total_rows // item_count
    items = item_count // 2
    rows_pad = -(-length // ITEM_PAD) * ITEM_PAD
    lanes = -(-length // 128) * 128
    dp_size = lax.axis_size("dp")
    nz = dp_size // 4
    shard = width // dp_size
    total = items * rows_pad
    chunks = w_up.shape[1] // BLOCK
    own_rows = items * length

    two_chunks = 2 * chunks
    hd = w_query.shape[1]
    inner = [
        ("x_raw", (total_rows, width), BF), ("x_v", (total, width), BF),
        ("cot_raw", (total_rows - own_rows // 8 * 8 + 16, width), F32), ("cot", (total, width), F32),
        ("bias_q", (2, 1, BLOCK), F32), ("bias_v", (2, 1, BLOCK), F32), ("bias_u", (2, 1, chunks * BLOCK), F32),
        ("b_out", (1, width), F32), ("gain_one", (1, width), F32), ("shift_one", (1, width), F32),
        ("b_down", (1, width), F32), ("gain_two", (1, width), F32), ("shift_two", (1, width), F32),
        ("wqkv", (2, 3, width, hd), BF), ("wo", (2, hd, width), BF),
        ("wu", (two_chunks, width, BLOCK), BF), ("wd", (two_chunks, BLOCK, width), BF),
        ("xT", (width + 16, items * lanes), BF), ("hT", (width + 16, items * lanes), BF),
        ("dT", (width, items * lanes), BF), ("oT", (width, items * lanes), BF),
        ("keys", (2 * items, rows_pad, hd), BF), ("values", (2 * items, rows_pad, hd), BF),
        ("tra", (2 * items, 3, hd, lanes), BF), ("score", (8, rows_pad, lanes), F32),
        ("probs", (8 * items, lanes, lanes), BF), ("ctxT", (2, hd, items * lanes), BF),
        ("ctx", (2, total, hd), BF), ("n1", (total, width), F32), ("inv1", (total, 128), F32),
        ("hlow", (total, width), BF), ("slope", (two_chunks, total, BLOCK), BF),
        ("active", (two_chunks, items, lanes, BLOCK), BF), ("acc", (total, width), F32),
        ("work", (3, total, BLOCK), F32), ("own", (4, width, BLOCK), F32),
        ("gp", (total, width), F32),
        ("dlow", (total, width), BF), ("upg", (3, items, lanes, BLOCK), BF), ("olow", (items, lanes, width), BF),
        ("cgT", (2 * items, hd, lanes), BF), ("dscore", (8, lanes, lanes), BF), ("gT", (2, 3 * hd, items * lanes), BF),
        ("g_out", (WHOLE_UNITS, 16, shard, BLOCK), BF), ("g", (WHOLE_UNITS, 16, shard, BLOCK), BF),
        ("g_a", (WHOLE_UNITS, 8, shard, BLOCK), BF), ("g_b", (WHOLE_UNITS, 4, shard, BLOCK), BF),
        ("g_c", (WHOLE_UNITS, 3, shard, BLOCK), BF),
        ("h_out", (HALF_UNITS, 16, shard, HALF), BF), ("h", (HALF_UNITS, 16, shard, HALF), BF),
        ("h_a", (HALF_UNITS, 8, shard, HALF), BF), ("h_b", (HALF_UNITS, 4, shard, HALF), BF),
        ("h_c", (HALF_UNITS, 3, shard, HALF), BF),
        ("v_out", (2, 16, BLOCK), F32), ("v_own", (2, 16, BLOCK), F32),
        ("v_in", (2, 2 + nz, 16, BLOCK), F32), ("v_sum", (2, 3, 16, BLOCK), F32),
    ]
    n_weights = 8 + chunks
    sems = [
        ("in_sem", (16 + chunks,)), ("w_send", (n_weights,)), ("w_recv", (n_weights,)), ("sent", (4, 2)),
        ("core_recv", (UNITS,)), ("a_recv", (UNITS,)), ("b_recv", (UNITS,)), ("c_recv", (UNITS,)),
        ("v_send", (2, 4)), ("v_recv", (2, 4)),
    ]
    operands = [
        ("counts", region_counts), ("x_h", inputs), ("cot_h", cotangent), ("wq_h", w_query), ("wk_h", w_key),
        ("wv_h", w_value), ("wo_h", w_out), ("wu_h", w_up), ("wd_h", w_down.reshape(chunks, BLOCK, width)),
        ("b_query_h", b_query[None]), ("b_value_h", b_value[None]), ("b_up_h", b_up[None]), ("b_out_h", b_out[None]),
        ("gain_one_h", gain_one[None]), ("shift_one_h", shift_one[None]), ("b_down_h", b_down[None]),
        ("gain_two_h", gain_two[None]), ("shift_two_h", shift_two[None]),
    ]
    hidden = chunks * BLOCK
    results = [
        ("out_o", (own_rows, width), BF), ("ig_o", (own_rows, width), F32),
        ("gq_o", (shard, hd), F32), ("bq_o", (1, hd), F32),
        ("gk_o", (shard, hd), F32), ("gv_o", (shard, hd), F32),
        ("bv_o", (1, hd), F32), ("go_o", (shard, hd), F32),
        ("bout_o", (1, width), F32), ("gain1_o", (1, width), F32),
        ("shift1_o", (1, width), F32), ("gu_o", (shard, hidden), F32),
        ("bup_o", (1, hidden), F32), ("gd_o", (shard, hidden), F32),
        ("bdown_o", (1, width), F32), ("gain2_o", (1, width), F32),
        ("shift2_o", (1, width), F32),
    ]
    names = [n for n, _ in operands] + [n for n, *_ in results] + [n for n, *_ in inner] + [n for n, _ in sems]
    smem = pl.BlockSpec(memory_space=pltpu.SMEM)
    shapes = [jax.ShapeDtypeStruct(s, d) for _, s, d in results]
    made = pl.pallas_call(
        functools.partial(layer_kernel, (items, length, rows_pad, lanes, nz, shard), names),
        out_shape=[pltpu.VMEM(s, d) for _, s, d in results],
        in_specs=[smem] + [pl.BlockSpec(memory_space=pl.ANY)] * (len(operands) - 1),
        out_specs=[pl.BlockSpec(memory_space=pltpu.VMEM)] * len(results),
        scratch_shapes=[pltpu.VMEM(s, d) for _, s, d in inner] + [pltpu.SemaphoreType.DMA(s) for _, s in sems],
        compiler_params=pltpu.CompilerParams(
            collective_id=0, has_side_effects=True, vmem_limit_bytes=59 * 2**20),
        name="layer",
    )(*[v for _, v in operands])
    count = len(shapes)
    made = pl.pallas_call(
        functools.partial(hand_over, count),
        out_shape=shapes,
        in_specs=[pl.BlockSpec(memory_space=pltpu.VMEM)] * count,
        out_specs=[pl.BlockSpec(memory_space=pl.ANY)] * count,
        scratch_shapes=[pltpu.SemaphoreType.DMA((count,))],
        compiler_params=pltpu.CompilerParams(vmem_limit_bytes=2**20),
        name="hand_over",
    )(*[pltpu.with_memory_space_constraint(v, pltpu.VMEM) for v in made])
    made = [v.reshape(-1) if v.shape[0] == 1 else v for v in made]
    made[7], made[13] = made[7].T, made[13].T
    return tuple(made)


def solution(mesh):
    placed = (
        P("dp", None),
        P("dp"),
        P(None, "mp"),
        P("mp"),
        P(None, "mp"),
        P(None, "mp"),
        P("mp"),
        P("mp", None),
        P(),
        P(),
        P(),
        P(None, "mp"),
        P("mp"),
        P("mp", None),
        P(),
        P(),
        P(),
        P("dp", None),
    )
    dp_size, mp_size = mesh.shape["dp"], mesh.shape["mp"]

    def body(*args):
        width, hidden = args[0].shape[1], args[11].shape[1]
        whole_items = mp_size == 2 and args[1].shape[0] % 2 == 0
        even_shards = dp_size == 16 and width % (16 * dp_size) == 0
        blocks = args[2].shape[1] == BLOCK and width == 2 * BLOCK and hidden == 4 * BLOCK
        fits = args[0].shape[0] // args[1].shape[0] <= 256
        if whole_items and even_shards and blocks and fits:
            return layer_by_items(*args)
        return per_device(*args)

    return jax.shard_map(
        body,
        mesh=mesh,
        in_specs=placed,
        out_specs=(
            P(("dp", "mp"), None),
            P(("dp", "mp"), None),
            P("dp", "mp"),
            P("mp"),
            P("dp", "mp"),
            P("dp", "mp"),
            P("mp"),
            P("mp", "dp"),
            P(),
            P(),
            P(),
            P("dp", "mp"),
            P("mp"),
            P("mp", "dp"),
            P(),
            P(),
            P(),
        ),
        check_vma=False,
    )
```

```python
import functools
import types

import jax
import jax.numpy as jnp
from jax import lax
from jax.experimental import pallas as pl
from jax.experimental.pallas import tpu as pltpu
from jax.sharding import PartitionSpec as P

HEAD_DIM = 64
TEXT = 128


def layer_stats(pre_rows):
    row_mean = jnp.mean(pre_rows, axis=-1, keepdims=True)
    centred = pre_rows - row_mean
    inverse = lax.rsqrt(jnp.mean(centred * centred, axis=-1, keepdims=True) + 1e-12)
    return (centred * inverse, inverse)


def norm_back(grad_rows, normed, inverse, gain_vec):
    scaled = grad_rows * gain_vec
    return inverse * (
        scaled
        - jnp.mean(scaled, axis=-1, keepdims=True)
        - normed * jnp.mean(scaled * normed, axis=-1, keepdims=True)
    )


def gelu_slope(upper_part):
    return (
        0.5 * (1.0 + lax.erf(upper_part * 0.7071067811865476))
        + upper_part * jnp.exp(-0.5 * upper_part * upper_part) * 0.3989422804014327
    )


def contract_rows(first_op, second_op):
    return lax.dot_general(
        first_op, second_op, (((0,), (0,)), ((), ())), preferred_element_type=jnp.float32
    )


def times_transposed(first_op, second_op):
    return lax.dot_general(
        first_op, second_op, (((1,), (1,)), ((), ())), preferred_element_type=jnp.float32
    )


def per_device(
    inputs,
    region_counts,
    w_query,
    b_query,
    w_key,
    w_value,
    b_value,
    w_out,
    b_out,
    gain_one,
    shift_one,
    w_up,
    b_up,
    w_down,
    b_down,
    gain_two,
    shift_two,
    cotangent,
):
    total_rows = inputs.shape[0]
    item_count = region_counts.shape[0]
    length = total_rows // item_count
    heads_here = w_query.shape[1] // HEAD_DIM
    score_scale = HEAD_DIM ** (-0.5)
    share_rows = total_rows // lax.axis_size("mp")
    row_start = lax.axis_index("mp") * share_rows

    def own_rows(full_rows):
        return lax.dynamic_slice_in_dim(full_rows, row_start, share_rows, 0)

    def split_heads(flat_rows):
        return flat_rows.reshape(item_count, length, heads_here, HEAD_DIM)

    position = jnp.arange(length)
    visible = (position[None, :] < TEXT) | (position[None, :] - TEXT < region_counts[:, None])
    key_mask = visible[:, None, None, :]
    queries = (jnp.dot(inputs, w_query, preferred_element_type=jnp.float32) + b_query).astype(
        jnp.bfloat16
    )
    key_rows = jnp.dot(inputs, w_key, preferred_element_type=jnp.float32).astype(jnp.bfloat16)
    value_rows = (jnp.dot(inputs, w_value, preferred_element_type=jnp.float32) + b_value).astype(
        jnp.bfloat16
    )
    query_heads = split_heads(queries)
    key_heads = split_heads(key_rows)
    value_heads = split_heads(value_rows)

    def masked_scores():
        raw_scores = (
            jnp.einsum(
                "ishd,ithd->ihst", query_heads, key_heads, preferred_element_type=jnp.float32
            )
            * score_scale
        )
        return jnp.where(key_mask, raw_scores, -1000000000.0)

    scores = masked_scores()
    row_top = jnp.max(scores, axis=-1, keepdims=True)
    exponent = jnp.exp(scores - row_top)
    row_total = jnp.sum(exponent, axis=-1, keepdims=True)
    probs = exponent / row_total
    log_total = row_top + jnp.log(row_total)
    context = jnp.einsum(
        "ihst,ithd->ishd",
        probs.astype(jnp.bfloat16),
        value_heads,
        preferred_element_type=jnp.float32,
    )
    context = context.reshape(total_rows, heads_here * HEAD_DIM).astype(jnp.bfloat16)
    partial_attn = jnp.dot(context, w_out, preferred_element_type=jnp.float32)
    attended = lax.psum(partial_attn, "mp")
    normed_one, inverse_one = layer_stats(attended + b_out + inputs.astype(jnp.float32))
    hidden_one = normed_one * gain_one + shift_one
    hidden_low = hidden_one.astype(jnp.bfloat16)
    upper_part = jnp.dot(hidden_low, w_up, preferred_element_type=jnp.float32) + b_up
    active = jax.nn.gelu(upper_part, approximate=False).astype(jnp.bfloat16)
    partial_ffn = jnp.dot(active, w_down, preferred_element_type=jnp.float32)
    lowered = lax.psum(partial_ffn, "mp")
    normed_two, inverse_two = layer_stats(lowered + b_down + hidden_one)
    output = own_rows(normed_two * gain_two + shift_two).astype(jnp.bfloat16)
    grad_pre_two = norm_back(cotangent, normed_two, inverse_two, gain_two)
    down_low = grad_pre_two.astype(jnp.bfloat16)
    grad_output = own_rows(cotangent)
    normed_two_own = own_rows(normed_two)
    grad_two_own = own_rows(grad_pre_two)
    grad_gain_two = jnp.sum(grad_output * normed_two_own, axis=0)
    grad_shift_two = jnp.sum(grad_output, axis=0)
    grad_b_down = jnp.sum(grad_two_own, axis=0)
    grad_w_down = contract_rows(active, down_low)
    active_grad = times_transposed(down_low, w_down)
    upper_grad = (active_grad * gelu_slope(upper_part)).astype(jnp.bfloat16)
    grad_b_up = jnp.sum(upper_grad.astype(jnp.float32), axis=0)
    grad_w_up = contract_rows(hidden_low, upper_grad)
    partial_hidden = times_transposed(upper_grad, w_up)
    hidden_grad = lax.psum(partial_hidden, "mp") + grad_pre_two
    grad_pre_one = norm_back(hidden_grad, normed_one, inverse_one, gain_one)
    out_low = grad_pre_one.astype(jnp.bfloat16)
    hidden_grad_own = own_rows(hidden_grad)
    normed_one_own = own_rows(normed_one)
    grad_one_own = own_rows(grad_pre_one)
    grad_gain_one = jnp.sum(hidden_grad_own * normed_one_own, axis=0)
    grad_shift_one = jnp.sum(hidden_grad_own, axis=0)
    grad_b_out = jnp.sum(grad_one_own, axis=0)
    grad_w_out = contract_rows(context, out_low)
    context_grad = split_heads(times_transposed(out_low, w_out).astype(jnp.bfloat16))
    probs_again = jnp.exp(masked_scores() - log_total)
    prob_grad = jnp.einsum(
        "ishd,ithd->ihst", context_grad, value_heads, preferred_element_type=jnp.float32
    )
    row_inner = jnp.sum(probs_again * prob_grad, axis=-1, keepdims=True)
    score_grad = (probs_again * (prob_grad - row_inner)).astype(jnp.bfloat16)
    query_grad = (
        (
            jnp.einsum("ihst,ithd->ishd", score_grad, key_heads, preferred_element_type=jnp.float32)
            * score_scale
        )
        .astype(jnp.bfloat16)
        .reshape(total_rows, heads_here * HEAD_DIM)
    )
    key_grad = (
        (
            jnp.einsum(
                "ihst,ishd->ithd", score_grad, query_heads, preferred_element_type=jnp.float32
            )
            * score_scale
        )
        .astype(jnp.bfloat16)
        .reshape(total_rows, heads_here * HEAD_DIM)
    )
    value_grad = jnp.einsum(
        "ihst,ishd->ithd",
        probs_again.astype(jnp.bfloat16),
        context_grad,
        preferred_element_type=jnp.float32,
    ).astype(jnp.bfloat16)
    value_grad = value_grad.reshape(total_rows, heads_here * HEAD_DIM)
    grad_b_query = jnp.sum(query_grad.astype(jnp.float32), axis=0)
    grad_b_value = jnp.sum(value_grad.astype(jnp.float32), axis=0)
    grad_w_query = contract_rows(inputs, query_grad)
    grad_w_key = contract_rows(inputs, key_grad)
    grad_w_value = contract_rows(inputs, value_grad)
    partial_input = (
        times_transposed(query_grad, w_query)
        + times_transposed(key_grad, w_key)
        + times_transposed(value_grad, w_value)
    )
    input_grad = own_rows(
        lax.psum(partial_input.astype(jnp.bfloat16), "mp").astype(jnp.float32) + grad_pre_one
    )
    bias_sums = lax.psum((grad_b_query, grad_b_value, grad_b_up), "dp")
    norm_sums = lax.psum(
        (grad_b_out, grad_gain_one, grad_shift_one, grad_b_down, grad_gain_two, grad_shift_two),
        ("dp", "mp"),
    )
    weight_sums = (
        lax.psum_scatter(
            grad_w_query.astype(jnp.bfloat16), "dp", scatter_dimension=0, tiled=True
        ).astype(jnp.float32),
        lax.psum_scatter(
            grad_w_key.astype(jnp.bfloat16), "dp", scatter_dimension=0, tiled=True
        ).astype(jnp.float32),
        lax.psum_scatter(
            grad_w_value.astype(jnp.bfloat16), "dp", scatter_dimension=0, tiled=True
        ).astype(jnp.float32),
        lax.psum_scatter(
            grad_w_out.astype(jnp.bfloat16), "dp", scatter_dimension=1, tiled=True
        ).astype(jnp.float32),
        lax.psum_scatter(
            grad_w_up.astype(jnp.bfloat16), "dp", scatter_dimension=0, tiled=True
        ).astype(jnp.float32),
        lax.psum_scatter(
            grad_w_down.astype(jnp.bfloat16), "dp", scatter_dimension=1, tiled=True
        ).astype(jnp.float32),
    )
    return (
        output,
        input_grad,
        weight_sums[0],
        bias_sums[0],
        weight_sums[1],
        weight_sums[2],
        bias_sums[1],
        weight_sums[3],
        norm_sums[0],
        norm_sums[1],
        norm_sums[2],
        weight_sums[4],
        bias_sums[2],
        weight_sums[5],
        norm_sums[3],
        norm_sums[4],
        norm_sums[5],
    )


ITEM_PAD = 16
MESH = pl.DeviceIdType.MESH
BF = jnp.bfloat16
F32 = jnp.float32
BLOCK = 256
HALF = 128
WHOLE_UNITS, HALF_UNITS = 9, 6
UNITS = WHOLE_UNITS + HALF_UNITS
X_FIRST, Y_FIRST, Z_FIRST = 0, 1, 2
ORDER = (0, 1, 2, 0, 1, 2, 0, 1, 0, 1, 0, 1, 0, 1, 0)
PLAN = {
    13: (('M', 0, 1, 2, 3),),
    14: (('A', 0, 1),),
    21: (('M', 4, 5),),
    23: (('M', 6, 7),),
    24: (('A', 4),),
    25: (('A', 5),),
    26: (('B', 0, 1), ('A', 6),),
    27: (('B', 2), ('A', 7),),
    31: (('M', 8), ('D', -1), ('B', 3, 4),),
    41: (('D', 0), ('A', 8), ('C', 0, 1), ('B', 5),),
    43: (('M', 9, 10, 11, 12, 13, 14), ('E', -1), ('C', 2),),
    51: (('B', 6),),
    53: (('D', 1), ('C', 4), ('A', 9, 10, 11),),
    63: (('E', 0), ('B', 8, 7), ('A', 12, 13, 14), ('C', 3, 6, 5),),
    71: (('D', 2), ('B', 9, 10),),
    72: (('B', 11), ('C', 7, 8),),
    73: (('E', 1), ('B', 12, 13, 14), ('F', 0, 1, 2), ('C', 9, 10, 11), ('E', 2), ('D', 3), ('F', 3, 4), ('C', 12, 13, 14), ('F', 5, 6, 7, 8), ('F', 9, 10, 11, 12, 13, 14), ('E', 3), ('D', 4), ('E', 4),),
    20: (('A', 2, 3),),
}


def dot_nn(a, b):
    return lax.dot_general(a, b, (((1,), (0,)), ((), ())), preferred_element_type=F32)


def dot_nt(a, b):
    return lax.dot_general(a, b, (((1,), (1,)), ((), ())), preferred_element_type=F32)


def layer_kernel(dims, names, *refs):
    r = types.SimpleNamespace(**dict(zip(names, refs, strict=True)))
    items, length, rows_pad, lanes, nz, shard = dims
    total = items * rows_pad
    chunks = r.wu_h.shape[1] // BLOCK
    width = r.x_h.shape[1]
    dp, mp = lax.axis_index("dp"), lax.axis_index("mp")
    z, y, x = dp // 4, (dp // 2) % 2, dp % 2

    def at(z_, y_, x_):
        return z_ * 4 + y_ * 2 + x_

    core = (dp, 1 - mp)
    x_side = (at(z, y, 1 - x), mp)
    y_side = (at(z, 1 - y, x), mp)
    z_side = [(at((z + step) % nz, y, x), mp) for step in range(1, nz)]
    low_side = (at(z + 1 - 2 * (z % 2), y, x), mp)
    high_side = z_side[1]
    plane_side = [(at(z, (y + step // 2) % 2, (x + step) % 2), mp) for step in range(1, 4)]

    local = []

    def bring(src, dst):
        copy = pltpu.make_async_copy(src, dst, r.in_sem.at[len(local)])
        copy.start()
        local.append(copy)
        return copy

    def bring_parts(parts, whole):
        sem = r.in_sem.at[len(local)]
        for src, dst in parts:
            pltpu.make_async_copy(src, dst, sem).start()
        copy = pltpu.make_async_copy(whole, whole, sem)
        local.append(copy)
        return copy

    c_x = bring(r.x_h, r.x_raw)
    c_w = [bring_parts([(src, r.wqkv.at[0, k]) for k, src in enumerate((r.wq_h, r.wk_h, r.wv_h))], r.wqkv.at[0])]
    c_p = [bring(r.b_query_h, r.bias_q.at[0]), bring(r.b_value_h, r.bias_v.at[0]), bring(r.b_up_h, r.bias_u.at[0])]

    barrier = pltpu.get_barrier_semaphore()
    near = [core] + plane_side + z_side
    for device in near:
        pl.semaphore_signal(barrier, inc=1, device_id=device, device_id_type=MESH)
    vectors = (
        (r.b_out_h, r.b_out), (r.gain_one_h, r.gain_one), (r.shift_one_h, r.shift_one),
        (r.b_down_h, r.b_down), (r.gain_two_h, r.gain_two), (r.shift_two_h, r.shift_two))
    c_vec = [bring(src, dst) for src, dst in vectors]
    c_wo = bring(r.wo_h, r.wo.at[0])
    up_blocks = [r.wu_h.at[:, pl.ds(c * BLOCK, BLOCK)] for c in range(chunks)]
    c_wu = [bring_parts([(src, r.wu.at[c]) for c, src in enumerate(up_blocks)], r.wu.at[pl.ds(0, chunks)])]
    c_wd = bring(r.wd_h, r.wd.at[pl.ds(0, chunks)])
    full_rows = r.x_h.shape[0]
    base = items * length // 8 * 8
    cot_count = full_rows - base
    c_cot = bring(r.cot_h.at[pl.ds(pl.multiple_of(mp * base, 8), cot_count)], r.cot_raw.at[pl.ds(0, cot_count)])

    pad_rows = lanes - rows_pad

    def transposed(block):
        full = jnp.concatenate([block, jnp.zeros((pad_rows, block.shape[1]), F32)], axis=0)
        return full.T.astype(BF)

    def rows_of(i):
        return pl.ds(pl.multiple_of(i * rows_pad, 16), rows_pad)

    def lanes_of(i):
        return pl.ds(pl.multiple_of(i * lanes, lanes), lanes)

    def greet():
        pl.semaphore_wait(barrier, len(near))

    def clear(n, carry):
        r.probs[n, pl.ds(rows_pad, pad_rows), :] = jnp.zeros((pad_rows, lanes), BF)
        return carry

    lax.fori_loop(0, r.probs.shape[0], clear, 0)
    zero_block = jnp.zeros((pad_rows, BLOCK), BF)
    for i in range(items):
        r.olow[i, pl.ds(rows_pad, pad_rows), :] = jnp.zeros((pad_rows, width), BF)
        for j in range(r.upg.shape[0]):
            r.upg[j, i, pl.ds(rows_pad, pad_rows), :] = zero_block
        for j in range(2 * chunks):
            r.active[j, i, pl.ds(rows_pad, pad_rows), :] = zero_block
    for k in range(r.dscore.shape[0]):
        r.dscore[k, pl.ds(rows_pad, pad_rows), :] = jnp.zeros((pad_rows, lanes), BF)
    one_row = jnp.where(lax.broadcasted_iota(jnp.int32, (16, items * lanes), 0) == 0, 1.0, 0.0).astype(BF)
    r.xT[pl.ds(width, 16), :] = one_row
    r.hT[pl.ds(width, 16), :] = one_row
    cot_rows = r.cot_raw.shape[0]
    r.cot_raw[pl.ds(cot_count, cot_rows - cot_count), :] = jnp.zeros((cot_rows - cot_count, width), F32)

    c_x.wait()
    down_ = lax.broadcasted_iota(jnp.int32, (rows_pad, 256), 0)
    across = lax.broadcasted_iota(jnp.int32, (rows_pad, 256), 1)
    for i in range(items):
        block = None
        for m in range(2):
            start = (m * items + i) * length
            window = start // 16 * 16
            count = min(256, full_rows - window)
            shift = jnp.where(mp == m, start - window, 2 * 256)
            pick = jnp.where((across == down_ + shift) & (down_ < length), 1.0, 0.0).astype(BF)
            term = dot_nn(pick[:, :count], r.x_raw[pl.ds(window, count), :])
            block = term if block is None else block + term
        r.x_v[rows_of(i), :] = block.astype(BF)

    greet()

    remote = []

    def send_weight(src, dst):
        k = len(remote)
        copy = pltpu.make_async_remote_copy(
            src_ref=src, dst_ref=dst, send_sem=r.w_send.at[k], recv_sem=r.w_recv.at[k],
            device_id=core, device_id_type=MESH)
        copy.start()
        remote.append(copy)
        return copy

    def send_parts(parts, whole):
        k = len(remote)

        def copy_of(src, dst):
            return pltpu.make_async_remote_copy(
                src_ref=src, dst_ref=dst, send_sem=r.w_send.at[k], recv_sem=r.w_recv.at[k],
                device_id=core, device_id_type=MESH)

        for src, dst in parts:
            copy_of(src, dst).start()
        copy = copy_of(whole, whole)
        remote.append(copy)
        return copy

    s_w = [send_parts([(src, r.wqkv.at[1, k]) for k, src in enumerate((r.wq_h, r.wk_h, r.wv_h))], r.wqkv.at[1])]
    s_w += [send_weight(src, dst.at[1]) for src, dst in (
        (r.b_query_h, r.bias_q), (r.b_value_h, r.bias_v), (r.b_up_h, r.bias_u))]
    s_wo = send_weight(r.wo_h, r.wo.at[1])
    s_wu = [send_parts([(src, r.wu.at[chunks + c]) for c, src in enumerate(up_blocks)], r.wu.at[pl.ds(chunks, chunks)])]
    s_wd = send_weight(r.wd_h, r.wd.at[pl.ds(chunks, chunks)])

    def project(slot, k):
        r.work[k] = dot_nn(r.x_v[...], r.wqkv[slot, k])

    def keep(slot, k):
        for i in range(items):
            block = r.work[k, pl.ds(i * rows_pad, rows_pad), :]
            n = slot * items + i
            if k == 0:
                r.tra[n, 0] = transposed((block + r.bias_q[slot]) * 0.125)
            elif k == 1:
                r.keys[n] = block.astype(BF)
            else:
                block = block + r.bias_v[slot]
                r.values[n] = block.astype(BF)
                r.tra[n, 2] = transposed(block)

    for c in c_w + c_p:
        c.wait()
    for k in range(3):
        project(0, k)
    for k in range(3):
        keep(0, k)
    lane = lax.broadcasted_iota(jnp.int32, (1, 128), 1)
    half = [jnp.where(lane < 64, 1.0, 0.0).astype(BF), jnp.where(lane >= 64, 1.0, 0.0).astype(BF)]
    position = lax.broadcasted_iota(jnp.int32, (rows_pad, lanes), 0)

    def pair_of(h):
        return slice((h // 2) * 128, (h // 2) * 128 + 128)

    def head_of(h):
        return slice(h * 64, (h + 1) * 64)

    def scores_of(n):
        for h in range(4):
            r.score[(n % 2) * 4 + h] = dot_nn(r.keys[n, :, pair_of(h)] * half[h % 2], r.tra[n, 0, pair_of(h), :])

    def soften(n):
        mask = jnp.where(position < TEXT + r.counts[mp * items + n % items], 0.0, -1e9)
        for h in range(4):
            score = r.score[(n % 2) * 4 + h] + mask
            top = jnp.max(score, axis=0, keepdims=True)
            e = jnp.exp(score - top)
            p = e * (1.0 / jnp.sum(e, axis=0, keepdims=True))
            r.probs[n * 4 + h, pl.ds(0, rows_pad), :] = p.astype(BF)

    def contexts_of(n):
        parts = [dot_nn(r.tra[n, 2, head_of(h), :], r.probs[n * 4 + h]) for h in range(4)]
        context = jnp.concatenate(parts, axis=0)
        slot, i = n // items, n % items
        r.ctxT[slot, :, pl.ds(i * lanes, lanes)] = context.astype(BF)
        r.ctx[slot, pl.ds(i * rows_pad, rows_pad), :] = context.T[:rows_pad].astype(BF)

    scores_of(0)
    for n in range(2 * items):
        if n + 1 == items:
            soften(n)
            for c in s_w:
                c.wait_recv()
            for k in range(3):
                project(1, k)
            contexts_of(n)
            for k in range(3):
                keep(1, k)
            scores_of(n + 1)
            continue
        if n + 1 < 2 * items:
            scores_of(n + 1)
        soften(n)
        contexts_of(n)

    c_wo.wait()
    s_wo.wait_recv()
    for c in c_vec:
        c.wait()

    def attended(i):
        rows = pl.ds(i * rows_pad, rows_pad)
        r.acc[rows, :] = dot_nn(r.ctx[0, rows, :], r.wo[0]) + dot_nn(r.ctx[1, rows, :], r.wo[1])

    def first_norm(i):
        rows = pl.ds(i * rows_pad, rows_pad)
        pre = r.acc[rows, :] + r.b_out[...] + r.x_v[rows, :].astype(F32)
        centred = pre - jnp.mean(pre, axis=1, keepdims=True)
        inverse = lax.rsqrt(jnp.mean(centred * centred, axis=1, keepdims=True) + 1e-12)
        normed = centred * inverse
        r.n1[rows, :] = normed
        r.inv1[rows, :] = jnp.broadcast_to(inverse, (rows_pad, 128))
        r.hlow[rows, :] = (normed * r.gain_one[...] + r.shift_one[...]).astype(BF)

    attended(0)
    for i in range(items):
        if i + 1 < items:
            attended(i + 1)
        first_norm(i)

    for c in c_wu + [c_wd]:
        c.wait()
    for c in s_wu + [s_wd]:
        c.wait_recv()
    c_cot.wait()
    valid = lax.broadcasted_iota(jnp.int32, (rows_pad, 1), 0) < length

    def own_cotangent(i):
        at_ = [r.cot_raw[pl.ds(m * (items * length - base) + i * length, rows_pad), :] for m in range(2)]
        r.cot[pl.ds(i * rows_pad, rows_pad), :] = jnp.where(valid, jnp.where(mp == 0, at_[0], at_[1]), 0.0)

    def lift(j):
        slot, c = j // chunks, j % chunks
        r.work[j % 2] = dot_nn(r.hlow[...], r.wu[j]) + r.bias_u[slot, :, c * BLOCK:(c + 1) * BLOCK]

    def activate(j):
        for i in range(items):
            rows = pl.ds(i * rows_pad, rows_pad)
            u = r.work[j % 2, rows, :]
            phi = 0.5 + 0.5 * lax.erf(u * 0.7071067811865476)
            r.slope[j, rows, :] = (phi + u * (jnp.exp(-0.5 * u * u) * 0.3989422804014327)).astype(BF)
            r.active[j, i, pl.ds(0, rows_pad), :] = (u * phi).astype(BF)

    def lower(j):
        part = dot_nn(r.active[j][:, :rows_pad].reshape(total, BLOCK), r.wd[j])
        if j == 0:
            r.acc[...] = part
        else:
            r.acc[...] += part

    lift(0)
    for j in range(2 * chunks):
        if j > 0:
            lower(j - 1)
        if j + 1 < 2 * chunks:
            lift(j + 1)
        activate(j)
        if 2 <= j < 2 + items:
            own_cotangent(j - 2)
    lower(2 * chunks - 1)

    def mean(v):
        return jnp.mean(v, axis=1, keepdims=True)

    def column_sum(v):
        return jnp.sum(v, axis=0, keepdims=True)

    gain2, shift2, bdown = [], [], []

    def second_norm(i):
        rows = pl.ds(i * rows_pad, rows_pad)
        hidden = r.n1[rows, :] * r.gain_one[...] + r.shift_one[...]
        pre = r.acc[rows, :] + r.b_down[...] + hidden
        centred = pre - mean(pre)
        inverse = lax.rsqrt(mean(centred * centred) + 1e-12)
        normed = centred * inverse
        cot = r.cot[rows, :]
        g = cot * r.gain_two[...]
        grad = inverse * (g - mean(g) - normed * mean(g * normed))
        r.gp[rows, :] = grad
        r.dlow[rows, :] = grad.astype(BF)
        r.dT[:, pl.ds(i * lanes, lanes)] = transposed(grad)
        r.acc[pl.ds(i * length, rows_pad), :] = normed * r.gain_two[...] + r.shift_two[...]
        gain2.append(column_sum(cot * normed))
        shift2.append(column_sum(cot))
        bdown.append(column_sum(grad))

    for i in range(items):
        second_norm(i)

    def held(u):
        if u < WHOLE_UNITS:
            return [ref.at[u] for ref in (r.g_out, r.g, r.g_a, r.g_b, r.g_c)]
        return [ref.at[u - WHOLE_UNITS] for ref in (r.h_out, r.h, r.h_a, r.h_b, r.h_c)]

    def size_of(u):
        return 0 if u < WHOLE_UNITS else 1

    def to_core(u):
        return pltpu.make_async_remote_copy(
            src_ref=held(u)[0], dst_ref=held(u)[1], send_sem=r.sent.at[0, size_of(u)],
            recv_sem=r.core_recv.at[u], device_id=core, device_id_type=MESH)

    route = (
        (x, y, z, x_side, y_side), (y, x, z, y_side, x_side), (z % 2, z // 2, y * 2 + x, low_side, high_side))

    def shard_order(order):
        if order == X_FIRST:
            return [at(c, b, a) for a in range(2) for b in range(2) for c in range(nz)]
        if order == Y_FIRST:
            return [at(c, a, b) for a in range(2) for b in range(2) for c in range(nz)]
        return [at(2 * b + a, c, d) for a in range(2) for b in range(2) for c in range(2) for d in range(2)]

    def stage_a(u, order):
        first, _, _, device, _ = route[order]
        return pltpu.make_async_remote_copy(
            src_ref=held(u)[1].at[pl.ds((1 - first) * 8, 8)], dst_ref=held(u)[2], send_sem=r.sent.at[1, size_of(u)],
            recv_sem=r.a_recv.at[u], device_id=device, device_id_type=MESH)

    def stage_b(u, order):
        first, second, _, _, device = route[order]
        return pltpu.make_async_remote_copy(
            src_ref=held(u)[1].at[pl.ds(first * 8 + (1 - second) * 4, 4)], dst_ref=held(u)[3], send_sem=r.sent.at[2, size_of(u)],
            recv_sem=r.b_recv.at[u], device_id=device, device_id_type=MESH)

    def wait_spread(u):
        came = held(u)[4]
        pltpu.make_async_remote_copy(
            src_ref=came, dst_ref=came, send_sem=r.sent.at[3, size_of(u)], recv_sem=r.c_recv.at[u],
            device_id=core, device_id_type=MESH).wait_recv()

    def wait_sent():
        for size, bufs in enumerate(((r.g_out, r.g_a, r.g_b, r.g_c), (r.h_out, r.h_a, r.h_b, r.h_c))):
            for stage, ref in enumerate(bufs):
                pltpu.make_async_remote_copy(
                    src_ref=ref, dst_ref=ref, send_sem=r.sent.at[stage, size], recv_sem=r.core_recv.at[0],
                    device_id=core, device_id_type=MESH).wait_send()

    def stage_c(u, order, step):
        first, second, _, _, _ = route[order]
        if order in (X_FIRST, Y_FIRST):
            place, device = (z + step) % nz, z_side[step - 1]
        else:
            place, device = ((y + step // 2) % 2) * 2 + (x + step) % 2, plane_side[step - 1]
        return pltpu.make_async_remote_copy(
            src_ref=held(u)[1].at[first * 8 + second * 4 + place], dst_ref=held(u)[4].at[step - 1],
            send_sem=r.sent.at[3, size_of(u)], recv_sem=r.c_recv.at[u],
            device_id=device, device_id_type=MESH)

    def lay_out(u, value):
        ref = held(u)[0]
        for place, block in enumerate(shard_order(ORDER[u])):
            ref[place] = value[block * shard:(block + 1) * shard].astype(BF)

    def start_core(u):
        to_core(u).start()

    def hold(u, value):
        r.own[u % r.own.shape[0], :, :value.shape[1]] = value

    def start_a(u):
        to_core(u).wait_recv()
        ref = held(u)[1]
        for place, block in enumerate(shard_order(ORDER[u])):
            mine = r.own[u % r.own.shape[0], pl.ds(block * shard, shard), :ref.shape[-1]]
            ref[place] = (mine + ref[place].astype(F32)).astype(BF)
        stage_a(u, ORDER[u]).start()

    def start_b(u):
        order = ORDER[u]
        stage_a(u, order).wait_recv()
        kept = pl.ds(route[order][0] * 8, 8)
        _, ref, came, _, _ = held(u)
        ref[kept] = ref[kept] + came[...]
        stage_b(u, order).start()

    def start_c(u):
        order = ORDER[u]
        stage_b(u, order).wait_recv()
        kept = pl.ds(route[order][0] * 8 + route[order][1] * 4, 4)
        _, ref, _, came, _ = held(u)
        ref[kept] = ref[kept] + came[...]
        for step in range(1, 4):
            stage_c(u, order, step).start()

    def finish(u):
        order = ORDER[u]
        first, second, third, _, _ = route[order]
        _, ref, _, _, came = held(u)
        acc = ref[first * 8 + second * 4 + third].astype(F32)
        wait_spread(u)
        for step in range(1, 4):
            acc += came[step - 1].astype(F32)
        return acc

    def vec_copy(k, stage, src, device):
        group = min(stage, 3)
        return pltpu.make_async_remote_copy(
            src_ref=src, dst_ref=r.v_in.at[k, stage], send_sem=r.v_send.at[k, group],
            recv_sem=r.v_recv.at[k, group], device_id=device, device_id_type=MESH)

    def vec_spread(k):
        came = r.v_in.at[k, pl.ds(3, nz - 1)]
        return pltpu.make_async_remote_copy(
            src_ref=came, dst_ref=came, send_sem=r.v_send.at[k, 3], recv_sem=r.v_recv.at[k, 3],
            device_id=core, device_id_type=MESH)

    def vec_core(k):
        return vec_copy(k, 0, r.v_out.at[k], core)

    def vec_side(k, stage):
        return vec_copy(k, stage, r.v_sum.at[k, stage - 1], (x_side, y_side)[stage - 1])

    def vec_z(k, step):
        return vec_copy(k, 2 + step, r.v_sum.at[k, 2], z_side[step - 1])

    def vec_next(k, stage):
        if stage == 0:
            vec_core(k).wait_recv()
            r.v_sum[k, 0] = r.v_own[k] + r.v_in[k, 0]
            vec_side(k, 1).start()
        elif stage == 1:
            vec_side(k, 1).wait_recv()
            r.v_sum[k, 1] = r.v_sum[k, 0] + r.v_in[k, 1]
            vec_side(k, 2).start()
        elif stage == 2:
            vec_side(k, 2).wait_recv()
            r.v_sum[k, 2] = r.v_sum[k, 1] + r.v_in[k, 2]
            for step in range(1, nz):
                vec_z(k, step).start()
        else:
            vec_spread(k).wait_recv()
            terms = [r.v_sum[k, 2]] + [r.v_in[k, 2 + step] for step in range(1, nz)]
            acc = jnp.zeros(terms[0].shape, F32)
            for zz in range(nz):
                came = lax.rem(z - zz + nz, nz)
                term = terms[0]
                for step in range(1, nz):
                    term = jnp.where(came == step, terms[step], term)
                acc = acc + term
            if k == 0:
                for j, ref in enumerate((r.bout_o, r.gain1_o, r.shift1_o, r.bdown_o, r.gain2_o, r.shift2_o)):
                    for part in range(2):
                        ref[:, part * BLOCK:(part + 1) * BLOCK] = acc[2 * j + part:2 * j + part + 1]
                for c in range(chunks):
                    r.bup_o[:, c * BLOCK:(c + 1) * BLOCK] = acc[12 + c:13 + c]
            else:
                r.bq_o[...] = acc[0:1]
                r.bv_o[...] = acc[1:2]

    def store_sum(u):
        total_ = finish(u)
        if u < 2 * chunks:
            column = u % chunks * BLOCK
            (r.gd_o, r.gu_o)[u // chunks][:, column:column + BLOCK] = total_
        elif u < WHOLE_UNITS:
            r.go_o[...] = total_
        else:
            column = (u - WHOLE_UNITS) // 3 * HALF
            (r.gq_o, r.gk_o, r.gv_o)[(u - WHOLE_UNITS) % 3][:, column:column + HALF] = total_

    def sums(k):
        def step(stage):
            if stage == 4:
                vec_core(k).wait_send()
                vec_side(k, 1).wait_send()
                vec_side(k, 2).wait_send()
                vec_spread(k).wait_send()
            elif stage < 0:
                vec_core(k).start()
            else:
                vec_next(k, stage)

        return step

    steps = dict(M=start_core, A=start_a, B=start_b, C=start_c, F=store_sum, D=sums(0), E=sums(1))

    def after(piece):
        for step, *units in PLAN.get(piece, ()):
            for u in units:
                steps[step](u)

    def down_grad(j):
        return dot_nn(r.dT[...], r.active[j].reshape(items * lanes, BLOCK))

    def active_grad(j):
        r.work[j % 2] = dot_nt(r.dlow[...], r.wd[j])

    def upper_grad(j):
        for i in range(items):
            rows = pl.ds(i * rows_pad, rows_pad)
            r.upg[j % 3, i, pl.ds(0, rows_pad), :] = (r.work[j % 2, rows, :] * r.slope[j, rows, :].astype(F32)).astype(BF)

    def up_grad(j):
        return dot_nn(r.hT[...], r.upg[j % 3].reshape(items * lanes, BLOCK))

    def hidden_grad(j):
        r.gp[...] += dot_nt(r.upg[j % 3][:, :rows_pad].reshape(total, BLOCK), r.wu[j])

    def turn(i):
        rows = pl.ds(i * rows_pad, rows_pad)
        r.hT[pl.ds(0, width), pl.ds(i * lanes, lanes)] = transposed(r.hlow[rows, :].astype(F32))

    def turn_input(i):
        rows = pl.ds(i * rows_pad, rows_pad)
        r.xT[pl.ds(0, width), pl.ds(i * lanes, lanes)] = transposed(r.x_v[rows, :].astype(F32))

    def turn_keys(n):
        r.tra[n, 1] = transposed(r.keys[n].astype(F32) * 0.125)

    for c in range(chunks):
        lay_out(c, down_grad(chunks + c))
        after(10 + c)
    for c in range(chunks):
        hold(c, down_grad(c))
        if c < items:
            turn(c)
    r.out_o[...] = r.acc[pl.ds(0, items * length), :].astype(BF)
    order = list(range(chunks, 2 * chunks)) + list(range(chunks))
    active_grad(order[0])
    after(14)
    for k, j in enumerate(order):
        if k + 1 < 2 * chunks:
            active_grad(order[k + 1])
        upper_grad(j)
        up = up_grad(j)
        c = j % chunks
        if j >= chunks:
            lay_out(chunks + c, up)
            r.v_out[0, pl.ds(12 + c, 1), :] = up[width:width + 1]
        else:
            hold(chunks + c, up[:width])
            r.v_own[0, pl.ds(12 + c, 1), :] = up[width:width + 1]
        hidden_grad(j)
        if k < 2 * items:
            turn_keys(k)
        else:
            turn_input(k - 2 * items)
        after(20 + k)
    turn_input(2)

    bout, gain1, shift1 = [], [], []

    def first_back(i):
        rows = pl.ds(i * rows_pad, rows_pad)
        hidden = r.gp[rows, :]
        normed = r.n1[rows, :]
        inverse = r.inv1[rows, :][:, :1]
        g = hidden * r.gain_one[...]
        grad = inverse * (g - mean(g) - normed * mean(g * normed))
        r.gp[rows, :] = grad
        r.olow[i, pl.ds(0, rows_pad), :] = grad.astype(BF)
        r.oT[:, pl.ds(i * lanes, lanes)] = transposed(grad)
        bout.append(column_sum(grad))
        gain1.append(column_sum(hidden * normed))
        shift1.append(column_sum(hidden))

    for i in range(items):
        first_back(i)
    for k, v in enumerate((bout, gain1, shift1, bdown, gain2, shift2)):
        v = sum(v[1:], v[0])
        for part in range(2):
            piece = v[:, part * BLOCK:(part + 1) * BLOCK]
            r.v_out[0, pl.ds(2 * k + part, 1), :] = piece
            r.v_own[0, pl.ds(2 * k + part, 1), :] = piece
    after(30)

    lay_out(8, dot_nt(r.oT[...], r.ctxT[1]))
    for n in [*range(items, 2 * items), *range(items)]:
        r.cgT[n] = dot_nt(r.wo[n // items], r.olow[n % items]).astype(BF)
    hold(8, dot_nt(r.oT[...], r.ctxT[0]))
    after(31)

    def probs_grad(n, heads):
        for h in heads:
            r.score[(n % 2) * 4 + h] = dot_nn(r.values[n, :, pair_of(h)] * half[h % 2], r.cgT[n, pair_of(h), :])

    def store_grad(n, k, h, value):
        r.gT[n // items, pl.ds(k * 256 + h * 64, 64), pl.ds((n % items) * lanes, lanes)] = value.astype(BF)

    def value_grad(n, heads):
        for h in heads:
            store_grad(n, 2, h, dot_nt(r.cgT[n, head_of(h), :], r.probs[n * 4 + h]))

    def score_grad(n, heads):
        for h in heads:
            pg = r.score[(n % 2) * 4 + h]
            p = r.probs[n * 4 + h, pl.ds(0, rows_pad), :].astype(F32)
            inner = jnp.sum(p * pg, axis=0, keepdims=True)
            r.dscore[(n % 2) * 4 + h, pl.ds(0, rows_pad), :] = (p * (pg - inner)).astype(BF)

    def query_key_grad(n, heads):
        for h in heads:
            ds = r.dscore[(n % 2) * 4 + h]
            store_grad(n, 0, h, dot_nn(r.tra[n, 1, head_of(h), :], ds))
            store_grad(n, 1, h, dot_nt(r.tra[n, 0, head_of(h), :], ds))

    def projection_grad(slot, k):
        return dot_nt(r.xT[...], r.gT[slot, pl.ds(k * 256, 256), :])

    for s in remote:
        s.wait_send()

    def attend_back(n, heads):
        probs_grad(n, heads)
        value_grad(n, heads)
        score_grad(n, heads)
        query_key_grad(n, heads)

    for n in range(items, 2 * items):
        attend_back(n, range(4))
        after(40 + n - items)
    for part in range(3):
        grad = projection_grad(1, part)
        for pair in range(2):
            lay_out(WHOLE_UNITS + 3 * pair + part, grad[:, pair * HALF:(pair + 1) * HALF])
        if part != 1:
            r.v_out[1, pl.ds(part // 2, 1), :] = grad[width:width + 1]
    after(43)
    for pair in range(2):
        for n in range(items):
            attend_back(n, (2 * pair, 2 * pair + 1))
            after(50 + 10 * pair + n)
        rows = [r.gT[0, pl.ds(part * BLOCK + pair * HALF, HALF), :] for part in range(3)]
        grad = dot_nt(r.xT[...], jnp.concatenate(rows, axis=0))
        for part in range(3):
            columns = slice(part * HALF, (part + 1) * HALF)
            hold(WHOLE_UNITS + 3 * pair + part, grad[:width, columns])
            if part != 1:
                r.v_own[1, pl.ds(part // 2, 1), pair * HALF:(pair + 1) * HALF] = grad[width:width + 1, columns]
        after(53 + 10 * pair)

    for i in range(items):
        if i > 0:
            after(70 + i)
        acc = None
        for slot in range(2):
            for k in range(3):
                term = dot_nn(r.wqkv[slot, k], r.gT[slot, pl.ds(k * 256, 256), pl.ds(i * lanes, lanes)])
                acc = term if acc is None else acc + term
        r.ig_o[pl.ds(i * length, length), :] = acc.T[:length] + r.gp[pl.ds(i * rows_pad, length), :]
    after(73)
    wait_sent()


def hand_over(count, *refs):
    sems = refs[-1]
    copies = [pltpu.make_async_copy(refs[k], refs[count + k], sems.at[k]) for k in range(count)]
    for c in copies:
        c.start()
    for c in copies:
        c.wait()


def layer_by_items(
    inputs, region_counts, w_query, b_query, w_key, w_value, b_value, w_out, b_out, gain_one, shift_one,
    w_up, b_up, w_down, b_down, gain_two, shift_two, cotangent,
):
    total_rows, width = inputs.shape
    item_count = region_counts.shape[0]
    length = total_rows // item_count
    items = item_count // 2
    rows_pad = -(-length // ITEM_PAD) * ITEM_PAD
    lanes = -(-length // 128) * 128
    dp_size = lax.axis_size("dp")
    nz = dp_size // 4
    shard = width // dp_size
    total = items * rows_pad
    chunks = w_up.shape[1] // BLOCK
    own_rows = items * length

    two_chunks = 2 * chunks
    hd = w_query.shape[1]
    inner = [
        ("x_raw", (total_rows, width), BF), ("x_v", (total, width), BF),
        ("cot_raw", (total_rows - own_rows // 8 * 8 + 16, width), F32), ("cot", (total, width), F32),
        ("bias_q", (2, 1, BLOCK), F32), ("bias_v", (2, 1, BLOCK), F32), ("bias_u", (2, 1, chunks * BLOCK), F32),
        ("b_out", (1, width), F32), ("gain_one", (1, width), F32), ("shift_one", (1, width), F32),
        ("b_down", (1, width), F32), ("gain_two", (1, width), F32), ("shift_two", (1, width), F32),
        ("wqkv", (2, 3, width, hd), BF), ("wo", (2, hd, width), BF),
        ("wu", (two_chunks, width, BLOCK), BF), ("wd", (two_chunks, BLOCK, width), BF),
        ("xT", (width + 16, items * lanes), BF), ("hT", (width + 16, items * lanes), BF),
        ("dT", (width, items * lanes), BF), ("oT", (width, items * lanes), BF),
        ("keys", (2 * items, rows_pad, hd), BF), ("values", (2 * items, rows_pad, hd), BF),
        ("tra", (2 * items, 3, hd, lanes), BF), ("score", (8, rows_pad, lanes), F32),
        ("probs", (8 * items, lanes, lanes), BF), ("ctxT", (2, hd, items * lanes), BF),
        ("ctx", (2, total, hd), BF), ("n1", (total, width), F32), ("inv1", (total, 128), F32),
        ("hlow", (total, width), BF), ("slope", (two_chunks, total, BLOCK), BF),
        ("active", (two_chunks, items, lanes, BLOCK), BF), ("acc", (total, width), F32),
        ("work", (3, total, BLOCK), F32), ("own", (4, width, BLOCK), F32),
        ("gp", (total, width), F32),
        ("dlow", (total, width), BF), ("upg", (3, items, lanes, BLOCK), BF), ("olow", (items, lanes, width), BF),
        ("cgT", (2 * items, hd, lanes), BF), ("dscore", (8, lanes, lanes), BF), ("gT", (2, 3 * hd, items * lanes), BF),
        ("g_out", (WHOLE_UNITS, 16, shard, BLOCK), BF), ("g", (WHOLE_UNITS, 16, shard, BLOCK), BF),
        ("g_a", (WHOLE_UNITS, 8, shard, BLOCK), BF), ("g_b", (WHOLE_UNITS, 4, shard, BLOCK), BF),
        ("g_c", (WHOLE_UNITS, 3, shard, BLOCK), BF),
        ("h_out", (HALF_UNITS, 16, shard, HALF), BF), ("h", (HALF_UNITS, 16, shard, HALF), BF),
        ("h_a", (HALF_UNITS, 8, shard, HALF), BF), ("h_b", (HALF_UNITS, 4, shard, HALF), BF),
        ("h_c", (HALF_UNITS, 3, shard, HALF), BF),
        ("v_out", (2, 16, BLOCK), F32), ("v_own", (2, 16, BLOCK), F32),
        ("v_in", (2, 2 + nz, 16, BLOCK), F32), ("v_sum", (2, 3, 16, BLOCK), F32),
    ]
    n_weights = 7
    sems = [
        ("in_sem", (15,)), ("w_send", (n_weights,)), ("w_recv", (n_weights,)), ("sent", (4, 2)),
        ("core_recv", (UNITS,)), ("a_recv", (UNITS,)), ("b_recv", (UNITS,)), ("c_recv", (UNITS,)),
        ("v_send", (2, 4)), ("v_recv", (2, 4)),
    ]
    operands = [
        ("counts", region_counts), ("x_h", inputs), ("cot_h", cotangent), ("wq_h", w_query), ("wk_h", w_key),
        ("wv_h", w_value), ("wo_h", w_out), ("wu_h", w_up), ("wd_h", w_down.reshape(chunks, BLOCK, width)),
        ("b_query_h", b_query[None]), ("b_value_h", b_value[None]), ("b_up_h", b_up[None]), ("b_out_h", b_out[None]),
        ("gain_one_h", gain_one[None]), ("shift_one_h", shift_one[None]), ("b_down_h", b_down[None]),
        ("gain_two_h", gain_two[None]), ("shift_two_h", shift_two[None]),
    ]
    hidden = chunks * BLOCK
    results = [
        ("out_o", (own_rows, width), BF), ("ig_o", (own_rows, width), F32),
        ("gq_o", (shard, hd), F32), ("bq_o", (1, hd), F32),
        ("gk_o", (shard, hd), F32), ("gv_o", (shard, hd), F32),
        ("bv_o", (1, hd), F32), ("go_o", (shard, hd), F32),
        ("bout_o", (1, width), F32), ("gain1_o", (1, width), F32),
        ("shift1_o", (1, width), F32), ("gu_o", (shard, hidden), F32),
        ("bup_o", (1, hidden), F32), ("gd_o", (shard, hidden), F32),
        ("bdown_o", (1, width), F32), ("gain2_o", (1, width), F32),
        ("shift2_o", (1, width), F32),
    ]
    names = [n for n, _ in operands] + [n for n, *_ in results] + [n for n, *_ in inner] + [n for n, _ in sems]
    smem = pl.BlockSpec(memory_space=pltpu.SMEM)
    shapes = [jax.ShapeDtypeStruct(s, d) for _, s, d in results]
    made = pl.pallas_call(
        functools.partial(layer_kernel, (items, length, rows_pad, lanes, nz, shard), names),
        out_shape=[pltpu.VMEM(s, d) for _, s, d in results],
        in_specs=[smem] + [pl.BlockSpec(memory_space=pl.ANY)] * (len(operands) - 1),
        out_specs=[pl.BlockSpec(memory_space=pltpu.VMEM)] * len(results),
        scratch_shapes=[pltpu.VMEM(s, d) for _, s, d in inner] + [pltpu.SemaphoreType.DMA(s) for _, s in sems],
        compiler_params=pltpu.CompilerParams(
            collective_id=0, has_side_effects=True, vmem_limit_bytes=59 * 2**20),
        name="layer",
    )(*[v for _, v in operands])
    count = len(shapes)
    made = pl.pallas_call(
        functools.partial(hand_over, count),
        out_shape=shapes,
        in_specs=[pl.BlockSpec(memory_space=pltpu.VMEM)] * count,
        out_specs=[pl.BlockSpec(memory_space=pl.ANY)] * count,
        scratch_shapes=[pltpu.SemaphoreType.DMA((count,))],
        compiler_params=pltpu.CompilerParams(vmem_limit_bytes=2**20),
        name="hand_over",
    )(*[pltpu.with_memory_space_constraint(v, pltpu.VMEM) for v in made])
    made = [v.reshape(-1) if v.shape[0] == 1 else v for v in made]
    made[7], made[13] = made[7].T, made[13].T
    return tuple(made)


def solution(mesh):
    placed = (
        P("dp", None),
        P("dp"),
        P(None, "mp"),
        P("mp"),
        P(None, "mp"),
        P(None, "mp"),
        P("mp"),
        P("mp", None),
        P(),
        P(),
        P(),
        P(None, "mp"),
        P("mp"),
        P("mp", None),
        P(),
        P(),
        P(),
        P("dp", None),
    )
    dp_size, mp_size = mesh.shape["dp"], mesh.shape["mp"]

    def body(*args):
        width, hidden = args[0].shape[1], args[11].shape[1]
        whole_items = mp_size == 2 and args[1].shape[0] % 2 == 0
        even_shards = dp_size == 16 and width % (16 * dp_size) == 0
        blocks = args[2].shape[1] == BLOCK and width == 2 * BLOCK and hidden == 4 * BLOCK
        fits = args[0].shape[0] // args[1].shape[0] <= 256
        if whole_items and even_shards and blocks and fits:
            return layer_by_items(*args)
        return per_device(*args)

    return jax.shard_map(
        body,
        mesh=mesh,
        in_specs=placed,
        out_specs=(
            P(("dp", "mp"), None),
            P(("dp", "mp"), None),
            P("dp", "mp"),
            P("mp"),
            P("dp", "mp"),
            P("dp", "mp"),
            P("mp"),
            P("mp", "dp"),
            P(),
            P(),
            P(),
            P("dp", "mp"),
            P("mp"),
            P("mp", "dp"),
            P(),
            P(),
            P(),
        ),
        check_vma=False,
    )
```
